32 devices in a mesh: dp: 8 (over z, core), tensor: 4 (over y, x).
Axes of the slice: x: 2, y: 2, z: 4, core: 2. Of those that a mesh axis runs over, the one named last changes fastest.
Arguments:
- inputs: bfloat16 [32, 512, 512], P(('dp', 'tensor')), may hold values from -6 to 6
- encoder: bfloat16 [32, 512, 512], P(('dp', 'tensor')), may hold values from -6 to 6
- dec_segments: int32 [32, 512], P(('dp', 'tensor')), may hold values from 0 to 3, never falling along the last dimension, each value on 1 to 256 neighbouring positions
- enc_segments: int32 [32, 512], P(('dp', 'tensor')), may hold values from 0 to 3, never falling along the last dimension, each value on 1 to 256 neighbouring positions
- cotangent: bfloat16 [32, 512, 512], P(('dp', 'tensor')), may hold values from -6 to 6
- attn_master: float32 [8, 512, 512], P(None, 'dp')
- attn_momentum: float32 [8, 512, 512], P(None, 'dp')
- expand_master: float32 [512, 2048], P(None, 'tensor'), may hold values from -0.25 to 0.25
- expand_momentum: float32 [512, 2048], P(None, 'tensor'), may hold values from -224 to 224
- contract_master: float32 [2048, 512], P('tensor'), may hold values from -0.125 to 0.125
- contract_momentum: float32 [2048, 512], P('tensor'), may hold values from -448 to 448
- norm_params: float32 [6, 512], P(None, 'dp')
- first_moments: float32 [6, 512], P(None, 'dp')
- second_moments: float32 [6, 512], P(None, 'dp'), as said below
Outputs:
- output: bfloat16 [32, 512, 512], P(('dp', 'tensor'))
- input_grad: bfloat16 [32, 512, 512], P(('dp', 'tensor'))
- encoder_grad: bfloat16 [32, 512, 512], P(('dp', 'tensor'))
- attn_updated: float32 [8, 512, 512], P(None, 'dp')
- attn_velocity: float32 [8, 512, 512], P(None, 'dp')
- attn_copy: bfloat16 [8, 512, 512], P(None, 'dp')
- expand_updated: float32 [512, 2048], P(None, 'tensor')
- expand_velocity: float32 [512, 2048], P(None, 'tensor')
- expand_copy: bfloat16 [512, 2048], P(None, 'tensor')
- contract_updated: float32 [2048, 512], P('tensor')
- contract_velocity: float32 [2048, 512], P('tensor')
- contract_copy: bfloat16 [2048, 512], P('tensor')
- norm_updated: float32 [6, 512], P(None, 'dp')
- first_updated: float32 [6, 512], P(None, 'dp')
- second_updated: float32 [6, 512], P(None, 'dp')
The draws below stay inside these ranges and needn't reach their ends.
Inputs may be any that keep to these rules, and one draw needn't show every extreme that they name: `dec_segments`: in every row the numbers never fall and each of 0 to 3 is present; a run is at most 256 tokens, and some run of each row has exactly that length. `enc_segments`: in every row the numbers never fall and each of 0 to 3 is present; a run is at most 256 states, and some run of each row has exactly that length. `second_moments`: Positive.
All inputs are finite; a program needn't handle non-finite values.
Results may differ from the reference program's by a relative error of at most 0.025.
Values may be sent and summed in bfloat16 or wider, within the bound.
No kernel may reach another device: no remote copies, remote signals or barrier semaphores. Data moves between devices by JAX's collectives and lax.ppermute only.
A program may use at most 192 MiB of HBM per device.

```python
import math
import jax
import jax.numpy as jnp
import numpy as np
from jax import lax

D = 512
HEADS = 8
FF = 2048
LEN = 512
ENC_LEN = 512
SEGS = 4
NS_STEPS = 5
STEP = 10
ROWS = 32
TOKENS = 16384


def row_gradients():
    return jnp.array([0.2, 0.2, 0.2, 0.2, 1.0, 1.0], jnp.float32) * TOKENS ** 0.5


def draw_attn_master(key, part):
    key = jax.random.fold_in(key, 11)
    factors = jnp.array([1.0, 1.0, 1.0, 2.0, 1.0, 1.0, 1.0, 2.0], jnp.float32) * D ** (-0.5)
    noise = jax.random.normal(key, (8, D, D), jnp.float32)
    return noise * factors[:, None, None]


def draw_attn_momentum(key, part):
    key = jax.random.fold_in(key, 12)
    factors = jnp.array([0.05, 0.05, 0.2, 0.1, 0.05, 0.05, 0.2, 0.1], jnp.float32) * TOKENS ** 0.5
    noise = jax.random.normal(key, (8, D, D), jnp.float32)
    return noise * factors[:, None, None]


def draw_norm_params(key, part):
    key = jax.random.fold_in(key, 13)
    noise = jax.random.normal(key, (6, D), jnp.float32)
    gains = jnp.array([1.0, 0.0, 1.0, 0.0, 1.0, 0.0], jnp.float32)[:, None]
    widths = jnp.array([0.1, 0.2, 0.1, 0.2, 0.1, 0.2], jnp.float32)[:, None]
    return gains + widths * noise


def draw_first_moments(key, part):
    key = jax.random.fold_in(key, 14)
    noise = jax.random.normal(key, (6, D), jnp.float32)
    return noise * (0.11 * row_gradients())[:, None]


def draw_second_moments(key, part):
    key = jax.random.fold_in(key, 15)
    level = jax.random.uniform(key, (6, D), jnp.float32, jnp.log(0.0005), jnp.log(0.008))
    return jnp.exp(level) * (row_gradients() * row_gradients())[:, None]


def shard_levels(own_key, dims, cuts, low, top_value):
    loudness, own = 1.0, jax.random.fold_in(own_key, 6)
    for dim, shards_of in cuts:
        draws = jnp.exp(jax.random.uniform(jax.random.fold_in(own, dim), (shards_of,), jnp.float32, low / len(cuts), top_value / len(cuts)))
        loudness = loudness * jnp.repeat(draws, dims[dim] // shards_of).reshape([-1 if axis == dim else 1 for axis in range(len(dims))])
    return loudness


def profile(count, total, most, skew):
    loads = [(1 << 20) // math.isqrt(grade ** skew) + 1 for grade in range(2, count + 1)]
    rest, holding = total - most - (count - 1), [1] * (count - 1)
    while rest > 0:
        candidates = [i for i in range(count - 1) if holding[i] < most]
        pool, budget = sum([loads[i] for i in candidates]), rest
        for i in candidates:
            more = min(most - holding[i], max(1, budget * loads[i] // pool), rest)
            holding[i] = holding[i] + more
            rest = rest - more
    return np.array([most] + holding)


def ragged_sizes(key, amount, total, reach, lean):
    if amount == 2:
        one = jax.random.randint(key, (), max(1, total - reach), min(reach, total - 1) + 1)
        return jnp.stack([one, total - one])
    lengths = jnp.asarray(profile(amount, total, reach, lean), jnp.int32)
    couples = (amount - 1) // 2
    source_of, receiver = lengths[1:1 + 2 * couples:2], lengths[2:2 + 2 * couples:2]
    room = jnp.minimum(source_of - 1, reach - receiver)
    passed = jax.random.randint(jax.random.fold_in(key, 1), (couples,), 0, 1 << 20) % (room + 1)
    lengths = lengths.at[1:1 + 2 * couples:2].set(source_of - passed).at[2:2 + 2 * couples:2].set(receiver + passed)
    return lengths[jax.random.permutation(jax.random.fold_in(key, 2), amount)]


def normal_values(own_key, shape, deviation, most, shards=(), dtype=jnp.bfloat16):
    gain = shard_levels(own_key, shape, shards, -0.22, 0.18) if shards else 1.0
    entries = jax.random.normal(own_key, shape, jnp.float32) * deviation * gain
    return jnp.minimum(jnp.maximum(entries, -most), most).astype(dtype)


def setup_inputs(seed: int = 0) -> dict:
    seeds = jax.random.split(jax.random.key(seed), 15)
    inputs = normal_values(seeds[0], (ROWS, LEN, D), 1.0, 6.0, ((0, 32),))
    encoder = normal_values(seeds[1], (ROWS, ENC_LEN, D), 1.0, 6.0, ((0, 32),))
    dec_segments = jax.vmap(lambda own: jnp.searchsorted(jnp.cumsum(ragged_sizes(own, SEGS, LEN, LEN // 2, 1)), jnp.arange(LEN), side="right"))(jax.random.split(seeds[2], ROWS)).reshape((ROWS, LEN)).astype(jnp.int32)
    enc_segments = jax.vmap(lambda own: jnp.searchsorted(jnp.cumsum(ragged_sizes(own, SEGS, ENC_LEN, ENC_LEN // 2, 1)), jnp.arange(ENC_LEN), side="right"))(jax.random.split(seeds[3], ROWS)).reshape((ROWS, ENC_LEN)).astype(jnp.int32)
    cotangent = normal_values(seeds[4], (ROWS, LEN, D), 1.0, 6.0, ((0, 32),))
    attn_master = draw_attn_master(jax.random.fold_in(seeds[14], 71), 0)
    attn_momentum = draw_attn_momentum(jax.random.fold_in(seeds[14], 71), 0)
    expand_master = normal_values(seeds[7], (D, FF), D ** -0.5, 0.25, ((1, 4),), jnp.float32)
    expand_momentum = normal_values(seeds[8], (D, FF), (0.3 * TOKENS ** 0.5), 224.0, ((1, 4),), jnp.float32)
    contract_master = normal_values(seeds[9], (FF, D), FF ** -0.5, 0.125, ((0, 4),), jnp.float32)
    contract_momentum = normal_values(seeds[10], (FF, D), (0.6 * TOKENS ** 0.5), 448.0, ((0, 4),), jnp.float32)
    norm_params = draw_norm_params(jax.random.fold_in(seeds[14], 71), 0)
    first_moments = draw_first_moments(jax.random.fold_in(seeds[14], 71), 0)
    second_moments = draw_second_moments(jax.random.fold_in(seeds[14], 71), 0)
    return {"inputs": inputs, "encoder": encoder, "dec_segments": dec_segments, "enc_segments": enc_segments, "cotangent": cotangent, "attn_master": attn_master, "attn_momentum": attn_momentum, "expand_master": expand_master, "expand_momentum": expand_momentum, "contract_master": contract_master, "contract_momentum": contract_momentum, "norm_params": norm_params, "first_moments": first_moments, "second_moments": second_moments}


@jax.custom_vjp
def low(v):
    return lax.optimization_barrier(v.astype(jnp.bfloat16)).astype(jnp.float32)

@jax.custom_vjp
def low_back(v):
    return v

def low_keep(v):
    return (low(v), None)

def low_pass(kept, grad):
    return (grad,)

def back_keep(v):
    return (v, None)

def back_low(kept, grad):
    return (low(grad),)
low.defvjp(low_keep, low_pass)
low_back.defvjp(back_keep, back_low)
HIGHEST = lax.Precision.HIGHEST
MASKED_SCORE = -1e+30
NORM_EPSILON = 1e-05
MOMENTUM_DECAY = 0.95
MUON_RATE = 0.15
MUON_DECAY = 0.01
POLY_FIRST = 3.4445
POLY_SECOND = -4.775
POLY_THIRD = 2.0315
ADAM_RATE = 0.4
BETA_FIRST = 0.9
BETA_SECOND = 0.999
ADAM_EPSILON = 1e-08

def product(left, right):
    return jnp.dot(left, right, precision=HIGHEST)

def layer_norm(values, gain_row, shift_row):
    average = lax.optimization_barrier(jnp.mean(values, -1, keepdims=True))
    centred = values - average
    spread = lax.optimization_barrier(jnp.mean(centred * centred, -1, keepdims=True))
    return centred * lax.rsqrt(spread + NORM_EPSILON) * gain_row + shift_row

def attend(queries, key_rows, value_rows, query_segs, key_segs):
    head_size = queries.shape[1] // HEADS
    scaling = head_size ** (-0.5)
    split_q = queries.reshape(queries.shape[0], HEADS, head_size)
    split_k = key_rows.reshape(key_rows.shape[0], HEADS, head_size)
    split_v = value_rows.reshape(value_rows.shape[0], HEADS, head_size)
    raw_scores = jnp.einsum('qhd,khd->hqk', split_q, split_k, precision=HIGHEST) * scaling
    allowed = (query_segs[:, None] == key_segs[None, :])[None]
    scores = jnp.where(allowed, low_back(raw_scores), MASKED_SCORE)
    weights_soft = jax.nn.softmax(scores, axis=-1)
    mixed_rows = jnp.einsum('hqk,khd->qhd', low(weights_soft), split_v, precision=HIGHEST)
    return mixed_rows.reshape(queries.shape[0], -1)

def row_forward(params, row_tokens, row_encoder, dec_seg, enc_seg):
    attn_w, norm_w, w_in, w_out = params
    normed_a = low(layer_norm(row_tokens, norm_w[0], norm_w[1]))
    self_proj = jnp.concatenate([attn_w[0], attn_w[1], attn_w[2]], 1)
    qkv_rows = low(low_back(product(normed_a, self_proj)))
    queries, key_rows, value_rows = jnp.split(qkv_rows, 3, axis=1)
    self_out = low(low_back(attend(queries, key_rows, value_rows, dec_seg, dec_seg)))
    middle = row_tokens + low_back(product(self_out, attn_w[3]))
    normed_c = low(layer_norm(middle, norm_w[2], norm_w[3]))
    cross_query = low(low_back(product(normed_c, attn_w[4])))
    cross_proj = jnp.concatenate([attn_w[5], attn_w[6]], 1)
    cross_kv = low(low_back(product(row_encoder, cross_proj)))
    cross_keys, cross_values = jnp.split(cross_kv, 2, axis=1)
    cross_out = low(low_back(attend(cross_query, cross_keys, cross_values, dec_seg, enc_seg)))
    late = middle + low_back(product(cross_out, attn_w[7]))
    normed_f = low(layer_norm(late, norm_w[4], norm_w[5]))
    pre_act = low_back(product(normed_f, w_in))
    post_act = low(jax.nn.gelu(pre_act))
    return late + product(post_act, w_out)

def orthogonalize(matrix):
    current = matrix / (jnp.sqrt(jnp.sum(matrix * matrix)) + 1e-07)
    for sweep_index in range(NS_STEPS):
        gram_matrix = product(current, current.T)
        polynomial = POLY_SECOND * gram_matrix + POLY_THIRD * product(gram_matrix, gram_matrix)
        current = POLY_FIRST * current + product(polynomial, current)
    return current

def reference(inputs, encoder, dec_segments, enc_segments, cotangent, attn_master, attn_momentum, expand_master, expand_momentum, contract_master, contract_momentum, norm_params, first_moments, second_moments):
    params = (low(attn_master), low(norm_params), low(expand_master), low(contract_master))
    rows_total = inputs.shape[0]
    group_size = 4 if rows_total % 4 == 0 else 1

    def regroup(source):
        return source.reshape((rows_total // group_size, group_size) + source.shape[1:])
    batches = tuple((regroup(source) for source in (inputs, encoder, dec_segments, enc_segments, cotangent)))

    def scan_step(totals, batch_rows):
        group_tokens, group_encoder, group_dec, group_enc, group_cot = batch_rows

        def forward(pieces, tokens_full, encoder_full):
            return jax.vmap(row_forward, in_axes=(None, 0, 0, 0, 0))(pieces, tokens_full, encoder_full, group_dec, group_enc)
        result, pullback = jax.vjp(forward, params, group_tokens.astype(jnp.float32), group_encoder.astype(jnp.float32))
        grad_params, grad_tokens, grad_encoder = pullback(group_cot.astype(jnp.float32))
        totals = jax.tree.map(jnp.add, totals, grad_params)
        return (totals, (result.astype(jnp.bfloat16), grad_tokens.astype(jnp.bfloat16), grad_encoder.astype(jnp.bfloat16)))
    zero_grads = jax.tree.map(jnp.zeros_like, params)
    totals, (output, input_grad, encoder_grad) = lax.scan(scan_step, zero_grads, batches)
    output = output.reshape(inputs.shape)
    input_grad = input_grad.reshape(inputs.shape)
    encoder_grad = encoder_grad.reshape(encoder.shape)
    grad_attn, grad_norm, grad_expand, grad_contract = totals
    attn_velocity = MOMENTUM_DECAY * attn_momentum + grad_attn
    attn_nest = grad_attn + MOMENTUM_DECAY * attn_velocity
    attn_ortho = lax.map(orthogonalize, attn_nest)
    attn_updated = attn_master - MUON_RATE * (MUON_DECAY * attn_master + 0.2 * math.sqrt(D) * attn_ortho)
    wide_scale = 0.2 * math.sqrt(max(D, FF))
    expand_velocity = MOMENTUM_DECAY * expand_momentum + grad_expand
    expand_nest = grad_expand + MOMENTUM_DECAY * expand_velocity
    expand_ortho = orthogonalize(expand_nest)
    expand_updated = expand_master - MUON_RATE * (MUON_DECAY * expand_master + wide_scale * expand_ortho)
    contract_velocity = MOMENTUM_DECAY * contract_momentum + grad_contract
    contract_nest = grad_contract + MOMENTUM_DECAY * contract_velocity
    contract_ortho = orthogonalize(contract_nest.T).T
    contract_updated = contract_master - MUON_RATE * (MUON_DECAY * contract_master + wide_scale * contract_ortho)
    first_updated = BETA_FIRST * first_moments + (1.0 - BETA_FIRST) * grad_norm
    second_updated = BETA_SECOND * second_moments + (1.0 - BETA_SECOND) * grad_norm * grad_norm
    corrected = first_updated / (1.0 - BETA_FIRST ** STEP)
    denominator = jnp.sqrt(second_updated / (1.0 - BETA_SECOND ** STEP)) + ADAM_EPSILON
    norm_updated = norm_params - ADAM_RATE * corrected / denominator
    return (output, input_grad, encoder_grad, attn_updated, attn_velocity, attn_updated.astype(jnp.bfloat16), expand_updated, expand_velocity, expand_updated.astype(jnp.bfloat16), contract_updated, contract_velocity, contract_updated.astype(jnp.bfloat16), norm_updated, first_updated, second_updated)
```

```python
import functools
import math

import jax
import jax.numpy as jnp
from jax import lax
from jax.experimental import pallas as pl
from jax.experimental.pallas import tpu as pltpu
from jax.sharding import PartitionSpec as P

D = 512
HEADS = 8
HEAD = D // HEADS
PAIR = 2 * HEAD
NS_STEPS = 5
STEP = 10

MASKED_SCORE = -1e30
NORM_EPSILON = 1e-05
MOMENTUM_DECAY = 0.95
MUON_RATE = 0.15
MUON_DECAY = 0.01
POLY_FIRST = 3.4445
POLY_SECOND = -4.775
POLY_THIRD = 2.0315
ADAM_RATE = 0.4
BETA_FIRST = 0.9
BETA_SECOND = 0.999
ADAM_EPSILON = 1e-08
GROUP = 4
QUERY_BLOCK = 256

F32 = jnp.float32
BF16 = jnp.bfloat16
AXES = ("dp", "tensor")
VMEM_BYTES = 60 * 1024 * 1024


def mm(left, right):
    return lax.dot_general(left, right, (((1,), (0,)), ((), ())), preferred_element_type=F32)


def mm_nt(left, right):
    return lax.dot_general(left, right, (((1,), (1,)), ((), ())), preferred_element_type=F32)


def mm_tn(left, right):
    return lax.dot_general(left, right, (((0,), (0,)), ((), ())), preferred_element_type=F32)


def normalized(values):
    average = jnp.mean(values, -1, keepdims=True)
    centred = values - average
    inv_std = lax.rsqrt(jnp.mean(centred * centred, -1, keepdims=True) + NORM_EPSILON)
    return centred * inv_std, inv_std


def norm_backward(incoming, values, gain_row):
    normed, inv_std = normalized(values)
    scaled = incoming * gain_row
    inner = (
        scaled
        - jnp.mean(scaled, -1, keepdims=True)
        - normed * jnp.mean(scaled * normed, -1, keepdims=True)
    )
    gain_grad = jnp.sum(incoming * normed, 0, keepdims=True)
    shift_grad = jnp.sum(incoming, 0, keepdims=True)
    return inner * inv_std, gain_grad, shift_grad


def head_mask(half, value):
    lane = lax.broadcasted_iota(jnp.int32, (1, PAIR), 1)
    inside = jnp.logical_and(lane >= half * HEAD, lane < (half + 1) * HEAD)
    return jnp.where(inside, value, 0.0).astype(BF16)


def pair_columns(pair):
    return pl.ds(pl.multiple_of(pair * PAIR, PAIR), PAIR)


def attend(q_ref, k_ref, v_ref, key_seg_ref, query_seg_ref, prob_ref, out_ref):
    queries = q_ref.shape[0]
    block = min(QUERY_BLOCK, queries)

    def one_pair(pair, carry):
        cols = pair_columns(pair)
        keys, values = k_ref[:, cols], v_ref[:, cols]
        for start in range(0, queries, block):
            rows = pl.ds(start, block)
            query = q_ref[rows, cols]
            allowed = key_seg_ref[...] == query_seg_ref[:, rows]
            total = None
            for half in range(2):
                scores = mm_nt(keys * head_mask(half, HEAD**-0.5), query)
                scores = jnp.where(allowed, scores, MASKED_SCORE)
                peak = jnp.max(scores, 0, keepdims=True)
                weights = jnp.exp(scores - peak)
                soft = (weights * (1.0 / jnp.sum(weights, 0, keepdims=True))).astype(BF16)
                prob_ref[pair * 2 + half, :, rows] = soft
                part = mm_tn(soft, values * head_mask(half, 1.0))
                total = part if total is None else total + part
            out_ref[rows, cols] = total.astype(BF16)
        return carry

    lax.fori_loop(0, HEADS // 2, one_pair, 0)


def attend_back(q_ref, k_ref, v_ref, prob_ref, grad_ref, dq_ref, dk_ref, dv_ref):
    queries = q_ref.shape[0]
    block = min(QUERY_BLOCK, queries)
    scaling = HEAD**-0.5

    def one_pair(pair, carry):
        cols = pair_columns(pair)
        keys, values = k_ref[:, cols], v_ref[:, cols]
        key_sum = value_sum = None
        for start in range(0, queries, block):
            rows = pl.ds(start, block)
            query, grad = q_ref[rows, cols], grad_ref[rows, cols]
            query_sum = None
            for half in range(2):
                mask = head_mask(half, 1.0)
                soft = prob_ref[pair * 2 + half, :, rows]
                weights = soft.astype(F32)
                grad_soft = mm_nt(values * mask, grad)
                product = weights * grad_soft
                inner = jnp.sum(product, 0, keepdims=True)
                grad_scores = (product - weights * inner).astype(BF16)
                value_part = mm(soft, grad * mask)
                key_part = mm(grad_scores, query * mask)
                query_part = mm_tn(grad_scores, keys * mask)
                value_sum = value_part if value_sum is None else value_sum + value_part
                key_sum = key_part if key_sum is None else key_sum + key_part
                query_sum = query_part if query_sum is None else query_sum + query_part
            dq_ref[rows, cols] = (query_sum * scaling).astype(BF16)
        dk_ref[:, cols] = (key_sum * scaling).astype(BF16)
        dv_ref[:, cols] = value_sum.astype(BF16)
        return carry

    lax.fori_loop(0, HEADS // 2, one_pair, 0)


def reorder(core, position, bits):
    if core == 0:
        return position
    return sum(((position >> bit) & 1) << (bits - 1 - bit) for bit in range(bits))


class Layout:
    def __init__(self, dp_size, tensor_size):
        self.dp, self.tensor = dp_size, tensor_size
        self.bits = tensor_size.bit_length() - 1
        self.planes = dp_size // 2
        self.parts = tensor_size // GROUP
        self.rows = D // dp_size
        self.width = D // self.parts

    def pairs(self, move):
        return [
            (d * self.tensor + t, move(d, t)) for d in range(self.dp) for t in range(self.tensor)
        ]

    def inplane(self, bit):
        return self.pairs(
            lambda d, t: d * self.tensor + (t ^ reorder(d & 1, 1 << bit, self.bits))
        )

    def plane(self, slot):
        return self.pairs(lambda d, t: (d ^ (2 * slot)) * self.tensor + t)

    def other_core(self):
        return self.pairs(lambda d, t: (d ^ 1) * self.tensor + t)


def send(values, pairs):
    return lax.ppermute(values, AXES, pairs)


def gather_inplane(layout, piece, bits=None):
    pieces = [piece]
    for bit in range(layout.bits if bits is None else bits):
        pieces = pieces + [send(one, layout.inplane(bit)) for one in pieces]
    return pieces


def gather_planes(layout, piece):
    return [piece] + [send(piece, layout.plane(slot)) for slot in range(1, layout.planes)]


def swap_cores(layout, values):
    return send(values, layout.other_core())


def add_low(*values):
    return sum(one.astype(F32) for one in values).astype(BF16)


def reduce_inplane(layout, stacked):
    for bit in reversed(range(layout.bits)):
        half = 1 << bit
        got = send(stacked[half:], layout.inplane(bit))
        stacked = add_low(stacked[:half], got)
    return stacked[0]


def reduce_planes(layout, slots):
    got = [send(slots[slot], layout.plane(slot)) for slot in range(1, layout.planes)]
    return add_low(slots[0], *got)


def whole_kernel(body, out_shape, scratch=(), flops=0, moved=0, name=None):
    def call(info, *operands):
        return pl.pallas_call(
            body,
            out_shape=out_shape,
            in_specs=[pl.BlockSpec(memory_space=pltpu.SMEM)]
            + [pl.BlockSpec(memory_space=pltpu.VMEM)] * len(operands),
            out_specs=jax.tree.map(lambda _: pl.BlockSpec(memory_space=pltpu.VMEM), out_shape),
            scratch_shapes=list(scratch),
            compiler_params=pltpu.CompilerParams(vmem_limit_bytes=VMEM_BYTES),
            cost_estimate=pl.CostEstimate(flops=flops, bytes_accessed=moved, transcendentals=0),
            name=name,
        )(info, *operands)

    return call


def low_shape(*shape):
    return jax.ShapeDtypeStruct(shape, BF16)


def wide_shape(*shape):
    return jax.ShapeDtypeStruct(shape, F32)


UNIT = 2 * D * D * D


def owner_at(info_ref, layout, position, other=False):
    core = info_ref[0]
    first = 1 if other else 0
    offset = jnp.where(
        core == first, reorder(0, position, layout.bits), reorder(1, position, layout.bits)
    )
    return jnp.bitwise_xor(info_ref[2], offset)


def row_start(info_ref, layout, slot, other=False):
    core, plane = info_ref[0], info_ref[1]
    if other:
        core = 1 - core
    block = jnp.bitwise_xor(plane, slot) * 2 + core
    return pl.multiple_of(block * layout.rows, layout.rows)


def place_weights(info_ref, layout, own_refs, other_refs, weights_ref):
    for other, refs in ((False, own_refs), (True, other_refs)):
        for position, ref in enumerate(refs):
            owner = owner_at(info_ref, layout, position, other)
            for slot in range(layout.planes):
                rows = pl.ds(row_start(info_ref, layout, slot, other), layout.rows)
                block = ref[slot]
                if layout.parts == 1:
                    weights_ref[owner, rows, :] = block
                else:
                    part = lax.rem(owner, layout.parts) * layout.width
                    cols = pl.ds(pl.multiple_of(part, layout.width), layout.width)
                    weights_ref[lax.div(owner, layout.parts), rows, cols] = block


def place_grads(info_ref, layout, grads_ref, keep_ref, send_ref):
    for other, ref in ((False, keep_ref), (True, send_ref)):
        for position in range(layout.tensor):
            owner = owner_at(info_ref, layout, position, other)
            for slot in range(layout.planes):
                rows = pl.ds(row_start(info_ref, layout, slot, other), layout.rows)
                if layout.parts == 1:
                    block = grads_ref[owner, rows, :]
                else:
                    part = lax.rem(owner, layout.parts) * layout.width
                    cols = pl.ds(pl.multiple_of(part, layout.width), layout.width)
                    block = grads_ref[lax.div(owner, layout.parts), rows, cols]
                ref[position, slot] = block


def self_forward(layout, tokens):
    count = layout.tensor

    def body(info_ref, x_ref, gains_ref, query_seg_ref, key_seg_ref, *refs):
        own, other = refs[:count], refs[count : 2 * count]
        w_ref, a_ref, q_ref, k_ref, v_ref, prob_ref, mix_ref, mid_ref, c_ref = refs[2 * count :]
        place_weights(info_ref, layout, own, other, w_ref)
        values = x_ref[...].astype(F32)
        normed, _ = normalized(values)
        a_ref[...] = (normed * gains_ref[0:1, :] + gains_ref[1:2, :]).astype(BF16)
        for index, ref in enumerate((q_ref, k_ref, v_ref)):
            ref[...] = mm(a_ref[...], w_ref[index]).astype(BF16)
        attend(q_ref, k_ref, v_ref, key_seg_ref, query_seg_ref, prob_ref, mix_ref)
        mid = x_ref[...].astype(F32) + mm(mix_ref[...], w_ref[3])
        mid_ref[...] = mid
        normed, _ = normalized(mid)
        c_ref[...] = (normed * gains_ref[2:3, :] + gains_ref[3:4, :]).astype(BF16)

    low = low_shape(tokens, D)
    return whole_kernel(
        body,
        (
            low_shape(GROUP, D, D),
            low,
            low,
            low,
            low,
            low_shape(HEADS, tokens, tokens),
            low,
            wide_shape(tokens, D),
            low,
        ),
        flops=14 * UNIT,
        moved=12 << 20,
        name="self_forward",
    )


def cross_forward(layout, tokens, states):
    count = layout.tensor

    def body(
        info_ref, c_ref, enc_ref, mid_ref, gains_ref, query_seg_ref, key_seg_ref, *refs
    ):
        own, other = refs[:count], refs[count : 2 * count]
        w_ref, q_ref, k_ref, v_ref, prob_ref, mix_ref, late_ref, f_ref = refs[2 * count :]
        place_weights(info_ref, layout, own, other, w_ref)
        q_ref[...] = mm(c_ref[...], w_ref[0]).astype(BF16)
        k_ref[...] = mm(enc_ref[...], w_ref[1]).astype(BF16)
        v_ref[...] = mm(enc_ref[...], w_ref[2]).astype(BF16)
        attend(q_ref, k_ref, v_ref, key_seg_ref, query_seg_ref, prob_ref, mix_ref)
        late = mid_ref[...] + mm(mix_ref[...], w_ref[3])
        late_ref[...] = late
        normed, _ = normalized(late)
        f_ref[...] = (normed * gains_ref[4:5, :] + gains_ref[5:6, :]).astype(BF16)

    low = low_shape(tokens, D)
    return whole_kernel(
        body,
        (
            low_shape(GROUP, D, D),
            low,
            low_shape(states, D),
            low_shape(states, D),
            low_shape(HEADS, states, tokens),
            low,
            wide_shape(tokens, D),
            low,
        ),
        flops=14 * UNIT,
        moved=12 << 20,
        name="cross_forward",
    )


def gelu_parts(pre):
    slope = math.sqrt(2.0 / math.pi)
    square = pre * pre
    bent = jnp.tanh(slope * pre * (1.0 + 0.044715 * square))
    half = 0.5 * (1.0 + bent)
    inner = slope * (1.0 + 3 * 0.044715 * square)
    return pre * half, half + 0.5 * pre * (1.0 - bent * bent) * inner


def feed_forward(layout, tokens, hidden):
    count = layout.tensor
    planes = layout.planes
    piece_rows = D // planes

    def body(info_ref, f_ref, cot_ref, late_ref, gains_ref, *refs):
        mine, others = refs[:count], refs[count : 2 * count]
        out_ref, glate_ref, dlate_ref, norm_ref, keep_ref, send_ref = refs[2 * count : -6]
        w_in, w_out, f_t, cot_t, value_sum, back_sum = refs[-6:]
        core, plane = info_ref[0], info_ref[1]
        for position in range(count):
            turned = reorder(1, position, layout.bits)

            @pl.when(core == 0)
            def _():
                w_in[position] = mine[position][...]
                w_out[position] = others[turned][...]

            @pl.when(core != 0)
            def _():
                w_in[position] = others[position][...]
                w_out[position] = mine[turned][...]

        f_t[...] = f_ref[...].T
        cot_t[...] = cot_ref[...].T
        value_sum[...] = jnp.zeros_like(value_sum)
        back_sum[...] = jnp.zeros_like(back_sum)

        def one_block(position, carry):
            turned = sum(
                ((position >> bit) & 1) << (layout.bits - 1 - bit) for bit in range(layout.bits)
            )
            first, second = w_in[position], w_out[position]
            cot = cot_ref[...]
            pre = mm(f_ref[...], first)
            post, slope = gelu_parts(pre)
            post = post.astype(BF16)
            value_sum[...] += mm_nt(post, second)
            d_pre = (slope * mm(cot, second)).astype(BF16)
            back_sum[...] += mm_nt(d_pre, first)
            grad_in = mm(f_t[...], d_pre).astype(BF16)
            grad_out = mm(cot_t[...], post).astype(BF16)
            for block in range(planes):
                slot = jnp.bitwise_xor(plane, block)
                part = slice(block * piece_rows, (block + 1) * piece_rows)

                @pl.when(core == 0)
                def _():
                    keep_ref[position, slot] = grad_in[part]
                    send_ref[turned, slot] = grad_out[part]

                @pl.when(core != 0)
                def _():
                    keep_ref[turned, slot] = grad_out[part]
                    send_ref[position, slot] = grad_in[part]

            return carry

        lax.fori_loop(0, count, one_block, 0)
        late = late_ref[...]
        out_ref[...] = (late + value_sum[...]).astype(BF16)
        back, gain_grad, shift_grad = norm_backward(back_sum[...], late, gains_ref[4:5, :])
        grad_late = cot_ref[...].astype(F32) + back
        glate_ref[...] = grad_late
        dlate_ref[...] = grad_late.astype(BF16)
        norm_ref[0:1, :] = gain_grad
        norm_ref[1:2, :] = shift_grad

    low = low_shape(tokens, D)
    pieces = low_shape(count, planes, piece_rows, hidden)
    return whole_kernel(
        body,
        (low, wide_shape(tokens, D), low, wide_shape(2, D), pieces, pieces),
        scratch=[
            pltpu.VMEM((count, D, hidden), BF16),
            pltpu.VMEM((count, D, hidden), BF16),
            pltpu.VMEM((D, tokens), BF16),
            pltpu.VMEM((D, tokens), BF16),
            pltpu.VMEM((tokens, D), F32),
            pltpu.VMEM((tokens, D), F32),
        ],
        flops=6 * UNIT * count * hidden // D,
        moved=14 << 20,
        name="feed_forward",
    )


def cross_backward(layout, tokens, states):
    def body(
        info_ref,
        dlate_ref,
        glate_ref,
        mix_ref,
        w_ref,
        q_ref,
        k_ref,
        v_ref,
        prob_ref,
        c_ref,
        enc_ref,
        mid_ref,
        gains_ref,
        enc_grad_ref,
        gmid_ref,
        dmid_ref,
        norm_ref,
        keep_ref,
        send_ref,
        d_mix,
        dq,
        dk,
        dv,
        grads,
    ):
        grads[3] = mm_tn(mix_ref[...], dlate_ref[...]).astype(BF16)
        d_mix[...] = mm_nt(dlate_ref[...], w_ref[3]).astype(BF16)
        attend_back(q_ref, k_ref, v_ref, prob_ref, d_mix, dq, dk, dv)
        grads[0] = mm_tn(c_ref[...], dq[...]).astype(BF16)
        enc_t = enc_ref[...].T
        grads[1] = mm(enc_t, dk[...]).astype(BF16)
        grads[2] = mm(enc_t, dv[...]).astype(BF16)
        place_grads(info_ref, layout, grads, keep_ref, send_ref)
        enc_grad_ref[...] = (mm_nt(dk[...], w_ref[1]) + mm_nt(dv[...], w_ref[2])).astype(BF16)
        back, gain_grad, shift_grad = norm_backward(
            mm_nt(dq[...], w_ref[0]), mid_ref[...], gains_ref[2:3, :]
        )
        grad_mid = glate_ref[...] + back
        gmid_ref[...] = grad_mid
        dmid_ref[...] = grad_mid.astype(BF16)
        norm_ref[0:1, :] = gain_grad
        norm_ref[1:2, :] = shift_grad

    low = low_shape(tokens, D)
    pieces = low_shape(layout.tensor, layout.planes, layout.rows, layout.width)
    return whole_kernel(
        body,
        (low_shape(states, D), wide_shape(tokens, D), low, wide_shape(2, D), pieces, pieces),
        scratch=[
            pltpu.VMEM((tokens, D), BF16),
            pltpu.VMEM((tokens, D), BF16),
            pltpu.VMEM((states, D), BF16),
            pltpu.VMEM((states, D), BF16),
            pltpu.VMEM((GROUP, D, D), BF16),
        ],
        flops=26 * UNIT,
        moved=14 << 20,
        name="cross_backward",
    )


def self_backward(layout, tokens):
    def body(
        info_ref,
        dmid_ref,
        gmid_ref,
        mix_ref,
        w_ref,
        q_ref,
        k_ref,
        v_ref,
        prob_ref,
        a_ref,
        x_ref,
        gains_ref,
        grad_ref,
        norm_ref,
        keep_ref,
        send_ref,
        d_mix,
        dq,
        dk,
        dv,
        grads,
    ):
        grads[3] = mm_tn(mix_ref[...], dmid_ref[...]).astype(BF16)
        d_mix[...] = mm_nt(dmid_ref[...], w_ref[3]).astype(BF16)
        attend_back(q_ref, k_ref, v_ref, prob_ref, d_mix, dq, dk, dv)
        a_t = a_ref[...].T
        total = None
        for index, ref in enumerate((dq, dk, dv)):
            grads[index] = mm(a_t, ref[...]).astype(BF16)
            part = mm_nt(ref[...], w_ref[index])
            total = part if total is None else total + part
        place_grads(info_ref, layout, grads, keep_ref, send_ref)
        back, gain_grad, shift_grad = norm_backward(
            total, x_ref[...].astype(F32), gains_ref[0:1, :]
        )
        grad_ref[...] = (gmid_ref[...] + back).astype(BF16)
        norm_ref[0:1, :] = gain_grad
        norm_ref[1:2, :] = shift_grad

    low = low_shape(tokens, D)
    pieces = low_shape(layout.tensor, layout.planes, layout.rows, layout.width)
    return whole_kernel(
        body,
        (low, wide_shape(2, D), pieces, pieces),
        scratch=[
            pltpu.VMEM((tokens, D), BF16),
            pltpu.VMEM((tokens, D), BF16),
            pltpu.VMEM((tokens, D), BF16),
            pltpu.VMEM((tokens, D), BF16),
            pltpu.VMEM((GROUP, D, D), BF16),
        ],
        flops=26 * UNIT,
        moved=14 << 20,
        name="self_backward",
    )


def sweep_polynomial(current_low, size):
    gram = mm_nt(current_low, current_low)
    diagonal = lax.broadcasted_iota(jnp.int32, (size, size), 0) == lax.broadcasted_iota(
        jnp.int32, (size, size), 1
    )
    shift = jnp.sum(jnp.where(diagonal, gram, 0.0)) / size
    rest = jnp.where(diagonal, gram - shift, gram)
    rest_low = rest.astype(BF16)
    square = mm(rest_low, rest_low)
    slope = POLY_SECOND + 2.0 * POLY_THIRD * shift
    scale = POLY_FIRST + POLY_SECOND * shift + POLY_THIRD * shift * shift
    return scale, (slope * rest + POLY_THIRD * square).astype(BF16)


def orthogonalize_attention(layout):
    parts = layout.parts

    def body(info_ref, *refs):
        grads, momenta = refs[: 2 * parts], refs[2 * parts : 4 * parts]
        out_ref, current = refs[4 * parts :]
        total = jnp.zeros((), F32)
        for part in range(parts):
            cols = pl.ds(part * layout.width, layout.width)
            for half in range(2):
                grad, momentum = grads[2 * part + half], momenta[2 * part + half]
                for slot in range(layout.planes):
                    nest = (1.0 + MOMENTUM_DECAY) * grad[slot].astype(F32) + (
                        MOMENTUM_DECAY * MOMENTUM_DECAY
                    ) * momentum[slot].astype(F32)
                    start = (half * layout.planes + slot) * layout.rows
                    current[pl.ds(start, layout.rows), cols] = nest
        whole = current[...]
        total = jnp.sqrt(jnp.sum(whole * whole)) + 1e-07
        current[...] = whole * (1.0 / total)

        def sweep(step, carry):
            low = current[...].astype(BF16)
            scale, rest = sweep_polynomial(low, D)
            current[...] = scale * current[...] + mm(rest, low)
            return carry

        lax.fori_loop(0, NS_STEPS, sweep, 0)
        out_ref[...] = current[0 : layout.rows, 0 : layout.width].astype(BF16)

    return whole_kernel(
        body,
        low_shape(layout.rows, layout.width),
        scratch=[pltpu.VMEM((D, D), F32)],
        flops=15 * UNIT,
        moved=2 << 20,
        name="orthogonalize_attention",
    )


def orthogonalize_wide(layout, hidden):
    count = layout.tensor

    def body(info_ref, *refs):
        pieces, out_ref, current, low = refs[:count], refs[count], refs[count + 1], refs[count + 2]
        total = jnp.zeros((), F32)
        for index, ref in enumerate(pieces):
            values = ref[...].astype(F32)
            current[:, pl.ds(index * hidden, hidden)] = values
            total = total + jnp.sum(values * values)
        inverse = 1.0 / (jnp.sqrt(total) + 1e-07)
        current[...] = current[...] * inverse

        def sweep(step, carry):
            low[...] = current[...].astype(BF16)
            scale, rest = sweep_polynomial(low[...], D)
            for index in range(count):
                cols = pl.ds(index * hidden, hidden)
                current[:, cols] = scale * current[:, cols] + mm(rest, low[:, cols])
            return carry

        lax.fori_loop(0, NS_STEPS, sweep, 0)
        out_ref[...] = current[:, 0:hidden].astype(BF16)

    return whole_kernel(
        body,
        low_shape(D, hidden),
        scratch=[
            pltpu.VMEM((D, count * hidden), F32),
            pltpu.VMEM((D, count * hidden), BF16),
        ],
        flops=45 * UNIT,
        moved=3 << 20,
        name="orthogonalize_wide",
    )


def wide_momentum(layout, hidden):
    piece_rows = D // layout.planes

    def body(info_ref, expand_ref, contract_ref, out_ref, turned):
        turned[...] = contract_ref[...].T
        for block in range(layout.planes):
            slot = jnp.bitwise_xor(info_ref[1], block)
            rows = pl.ds(block * piece_rows, piece_rows)
            out_ref[slot] = jnp.where(info_ref[0] == 0, expand_ref[rows, :], turned[rows, :])

    return whole_kernel(
        body,
        wide_shape(layout.planes, piece_rows, hidden),
        scratch=[pltpu.VMEM((D, hidden), F32)],
        moved=3 << 20,
        name="wide_momentum",
    )


def decayed(master, share, scale):
    return master - MUON_RATE * (MUON_DECAY * master + scale * share)


def place_wide(info_ref, layout, slot_of, for_expand, for_contract):
    piece_rows = D // layout.planes
    core, plane = info_ref[0], info_ref[1]
    for slot in range(layout.planes):
        start = pl.multiple_of(jnp.bitwise_xor(plane, slot) * piece_rows, piece_rows)
        mine, other = slot_of(slot)
        for_expand[pl.ds(start, piece_rows), :] = jnp.where(core == 0, mine, other).astype(F32)
        for_contract[pl.ds(start, piece_rows), :] = jnp.where(core == 0, other, mine).astype(F32)


def finish_wide(layout, hidden, full_hidden):
    piece_rows = D // layout.planes
    scale = 0.2 * math.sqrt(max(D, full_hidden))

    def body(info_ref, mine_ref, other_ref, expand_ref, contract_ref, *refs):
        e_new, e_low, c_new, c_low, for_expand, for_contract = refs

        def slot_of(slot):
            rows = pl.ds(slot * piece_rows, piece_rows)
            return mine_ref[rows, :], other_ref[rows, :]

        place_wide(info_ref, layout, slot_of, for_expand, for_contract)
        new = decayed(expand_ref[...], for_expand[...], scale)
        e_new[...] = new
        e_low[...] = new.astype(BF16)
        new = decayed(contract_ref[...], for_contract[...].T, scale)
        c_new[...] = new
        c_low[...] = new.astype(BF16)

    return whole_kernel(
        body,
        (wide_shape(D, hidden), low_shape(D, hidden), wide_shape(hidden, D), low_shape(hidden, D)),
        scratch=[pltpu.VMEM((D, hidden), F32)] * 2,
        moved=6 << 20,
        name="finish_wide",
    )


def wide_velocity(layout, hidden):
    def body(info_ref, *refs):
        mine, other = refs[: layout.planes], refs[layout.planes : 2 * layout.planes]
        expand_ref, contract_ref, e_new, c_new, for_expand, for_contract = refs[
            2 * layout.planes :
        ]

        def slot_of(slot):
            return mine[slot][...], other[slot][...]

        place_wide(info_ref, layout, slot_of, for_expand, for_contract)
        e_new[...] = MOMENTUM_DECAY * expand_ref[...] + for_expand[...]
        c_new[...] = MOMENTUM_DECAY * contract_ref[...] + for_contract[...].T

    return whole_kernel(
        body,
        (wide_shape(D, hidden), wide_shape(hidden, D)),
        scratch=[pltpu.VMEM((D, hidden), F32)] * 2,
        moved=6 << 20,
        name="wide_velocity",
    )


def finish_attention(layout):
    count = layout.tensor
    scale = 0.2 * math.sqrt(D)

    def body(info_ref, *refs):
        ortho, grads = refs[: 2 * count], refs[2 * count : 4 * count]
        master_ref, momentum_ref, new_ref, velocity_ref, low_ref = refs[4 * count :]
        for group in range(2):
            for position in range(count):
                owner = owner_at(info_ref, layout, position)
                index = group * GROUP + lax.div(owner, layout.parts)
                cols = slice(None)
                if layout.parts > 1:
                    part = lax.rem(owner, layout.parts) * layout.width
                    cols = pl.ds(pl.multiple_of(part, layout.width), layout.width)
                share = ortho[group * count + position][...].astype(F32)
                new = decayed(master_ref[index, :, cols], share, scale)
                new_ref[index, :, cols] = new
                low_ref[index, :, cols] = new.astype(BF16)
                grad = grads[group * count + position][...].astype(F32)
                velocity_ref[index, :, cols] = (
                    MOMENTUM_DECAY * momentum_ref[index, :, cols] + grad
                )

    shape = (2 * GROUP, layout.rows, D)
    return whole_kernel(
        body,
        (wide_shape(*shape), wide_shape(*shape), low_shape(*shape)),
        moved=6 << 20,
        name="finish_attention",
    )


def device_program(layout, arguments):
    (
        inputs,
        encoder,
        dec_segments,
        enc_segments,
        cotangent,
        attn_master,
        attn_momentum,
        expand_master,
        expand_momentum,
        contract_master,
        contract_momentum,
        norm_params,
        first_moments,
        second_moments,
    ) = arguments
    tokens, states = inputs.shape[1], encoder.shape[1]
    hidden = expand_master.shape[1]
    full_hidden = hidden * layout.tensor
    dp_at, tensor_at = lax.axis_index("dp"), lax.axis_index("tensor")
    core, plane = dp_at % 2, dp_at // 2
    info = jnp.stack([core, plane, tensor_at]).astype(jnp.int32)
    x, enc, cot = inputs[0], encoder[0], cotangent[0]

    def chunk(source, group):
        matrix = group * GROUP + tensor_at // layout.parts
        rows = lax.dynamic_index_in_dim(source, matrix, 0, keepdims=False)
        if layout.parts > 1:
            start = tensor_at % layout.parts * layout.width
            rows = lax.dynamic_slice_in_dim(rows, start, layout.width, 1)
        return rows.astype(BF16)

    norm_slots = gather_planes(layout, norm_params.astype(BF16))
    norm_blocks = jnp.stack(norm_slots + [swap_cores(layout, slot) for slot in norm_slots])
    block = jnp.arange(layout.dp)
    place = (block % 2) ^ core
    order = place * layout.planes + ((block // 2) ^ plane)
    gains = jnp.take(norm_blocks, order, axis=0).transpose(1, 0, 2).reshape(6, D).astype(F32)

    def gather_weights(group):
        own = gather_inplane(layout, jnp.stack(gather_planes(layout, chunk(attn_master, group))))
        return own + [swap_cores(layout, piece) for piece in own]

    self_pieces = gather_weights(0)
    cross_pieces = gather_weights(1)
    expand_low, contract_low = expand_master.astype(BF16), contract_master.astype(BF16).T
    wide_own = gather_inplane(layout, jnp.where(core == 0, expand_low, contract_low))
    wide_pieces = wide_own + [swap_cores(layout, piece) for piece in wide_own]

    dec_row, dec_column = dec_segments.reshape(1, tokens), dec_segments.reshape(tokens, 1)
    enc_column = enc_segments.reshape(states, 1)
    w_self, a, q, k, v, self_prob, self_mix, mid, c = self_forward(layout, tokens)(
        info, x, gains, dec_row, dec_column, *self_pieces
    )
    w_cross, qc, kc, vc, cross_prob, cross_mix, late, f = cross_forward(layout, tokens, states)(
        info, c, enc, mid, gains, dec_row, enc_column, *cross_pieces
    )
    output, grad_late, late_low, norm_three, wide_keep, wide_send = feed_forward(
        layout, tokens, hidden
    )(info, f, cot, late, gains, *wide_pieces)
    wide_part = reduce_inplane(layout, add_low(wide_keep, swap_cores(layout, wide_send)))
    wide_grad = gather_planes(layout, reduce_planes(layout, wide_part))
    wide_other = [swap_cores(layout, piece) for piece in wide_grad]
    momentum = wide_momentum(layout, hidden)(info, expand_momentum, contract_momentum)
    nest = jnp.concatenate(
        [
            (
                (1.0 + MOMENTUM_DECAY) * piece.astype(F32)
                + MOMENTUM_DECAY * MOMENTUM_DECAY * momentum[slot]
            ).astype(BF16)
            for slot, piece in enumerate(wide_grad)
        ]
    )
    nest_pieces = gather_inplane(layout, nest)

    encoder_grad, grad_mid, mid_low, norm_two, cross_keep, cross_send = cross_backward(
        layout, tokens, states
    )(
        info, late_low, grad_late, cross_mix, w_cross, qc, kc, vc, cross_prob, c, enc, mid, gains
    )
    input_grad, norm_one, self_keep, self_send = self_backward(layout, tokens)(
        info, mid_low, grad_mid, self_mix, w_self, q, k, v, self_prob, a, x, gains
    )

    def reduce_attention(keep, other):
        part = reduce_inplane(layout, add_low(keep, swap_cores(layout, other)))
        rows = reduce_planes(layout, part)
        half = jnp.stack(gather_planes(layout, rows))
        return rows, [half, swap_cores(layout, half)]

    def whole_pieces(halves):
        shared = layout.parts.bit_length() - 1
        gathered = [halves]
        for bit in range(shared):
            pairs = layout.pairs(lambda d, t: d * layout.tensor + (t ^ (1 << bit)))
            gathered = gathered + [[send(half, pairs) for half in one] for one in gathered]
        return [half for one in gathered for half in one]

    momenta = []
    for group in range(2):
        half = jnp.stack(gather_planes(layout, chunk(attn_momentum, group)))
        momenta.append(whole_pieces([half, swap_cores(layout, half)]))
    ortho_pieces, grad_pieces = [[], []], [[], []]
    for group, pair in ((1, (cross_keep, cross_send)), (0, (self_keep, self_send))):
        rows, halves = reduce_attention(*pair)
        grad_pieces[group] = gather_inplane(layout, rows)
        ortho = orthogonalize_attention(layout)(info, *whole_pieces(halves), *momenta[group])
        ortho_pieces[group] = gather_inplane(layout, ortho)
    attn_updated, attn_velocity, attn_copy = finish_attention(layout)(
        info, *ortho_pieces[0], *ortho_pieces[1], *grad_pieces[0], *grad_pieces[1],
        attn_master, attn_momentum,
    )

    wide_mine = orthogonalize_wide(layout, hidden)(info, *nest_pieces)
    expand_updated, expand_copy, contract_updated, contract_copy = finish_wide(
        layout, hidden, full_hidden
    )(info, wide_mine, swap_cores(layout, wide_mine), expand_master, contract_master)
    expand_velocity, contract_velocity = wide_velocity(layout, hidden)(
        info, *wide_grad, *wide_other, expand_momentum, contract_momentum
    )

    norm_sum = jnp.concatenate([norm_one, norm_two, norm_three])
    norm_sum = norm_sum + swap_cores(layout, norm_sum)
    for bit in range(layout.bits):
        norm_sum = norm_sum + send(norm_sum, layout.inplane(bit))
    norm_sum = sum(gather_planes(layout, norm_sum))
    norm_rows = lax.dynamic_slice_in_dim(norm_sum, dp_at * layout.rows, layout.rows, 1)
    first_updated = BETA_FIRST * first_moments + (1.0 - BETA_FIRST) * norm_rows
    second_updated = BETA_SECOND * second_moments + (1.0 - BETA_SECOND) * norm_rows * norm_rows
    corrected = first_updated / (1.0 - BETA_FIRST**STEP)
    denominator = jnp.sqrt(second_updated / (1.0 - BETA_SECOND**STEP)) + ADAM_EPSILON
    norm_updated = norm_params - ADAM_RATE * corrected / denominator
    return (
        output[None],
        input_grad[None],
        encoder_grad[None],
        attn_updated,
        attn_velocity,
        attn_copy,
        expand_updated,
        expand_velocity,
        expand_copy,
        contract_updated,
        contract_velocity,
        contract_copy,
        norm_updated,
        first_updated,
        second_updated,
    )


def solution(mesh):
    layout = Layout(mesh.shape["dp"], mesh.shape["tensor"])

    def local(*arguments):
        return device_program(layout, arguments)

    rows = P(AXES, None, None)
    by_dp, by_column, by_row, norm = P(None, "dp", None), P(None, "tensor"), P("tensor", None), P(None, "dp")
    return jax.shard_map(
        local,
        mesh=mesh,
        in_specs=(rows, rows, P(AXES, None), P(AXES, None), rows)
        + (by_dp, by_dp, by_column, by_column, by_row, by_row, norm, norm, norm),
        out_specs=(rows, rows, rows, by_dp, by_dp, by_dp)
        + (by_column, by_column, by_column, by_row, by_row, by_row, norm, norm, norm),
        check_vma=False,
    )
```

```python
import functools
import math

import jax
import jax.numpy as jnp
from jax import lax
from jax.experimental import pallas as pl
from jax.experimental.pallas import tpu as pltpu
from jax.sharding import PartitionSpec as P

D = 512
HEADS = 8
HEAD = D // HEADS
PAIR = 2 * HEAD
NS_STEPS = 5
STEP = 10

MASKED_SCORE = -1e30
NORM_EPSILON = 1e-05
MOMENTUM_DECAY = 0.95
MUON_RATE = 0.15
MUON_DECAY = 0.01
POLY_FIRST = 3.4445
POLY_SECOND = -4.775
POLY_THIRD = 2.0315
ADAM_RATE = 0.4
BETA_FIRST = 0.9
BETA_SECOND = 0.999
ADAM_EPSILON = 1e-08
GROUP = 4
QUERY_BLOCK = 256

F32 = jnp.float32
BF16 = jnp.bfloat16
AXES = ("dp", "tensor")
MIB = 1 << 20
VMEM_BYTES = 30 * MIB
NORM_ROWS = 16


def mm(left, right):
    return lax.dot_general(left, right, (((1,), (0,)), ((), ())), preferred_element_type=F32)


def mm_nt(left, right):
    return lax.dot_general(left, right, (((1,), (1,)), ((), ())), preferred_element_type=F32)


def mm_tn(left, right):
    return lax.dot_general(left, right, (((0,), (0,)), ((), ())), preferred_element_type=F32)


def normalized(values):
    average = jnp.mean(values, -1, keepdims=True)
    centred = values - average
    inv_std = lax.rsqrt(jnp.mean(centred * centred, -1, keepdims=True) + NORM_EPSILON)
    return centred * inv_std, inv_std


def norm_backward(incoming, values, gain_row):
    normed, inv_std = normalized(values)
    scaled = incoming * gain_row
    inner = (
        scaled
        - jnp.mean(scaled, -1, keepdims=True)
        - normed * jnp.mean(scaled * normed, -1, keepdims=True)
    )
    gain_grad = jnp.sum(incoming * normed, 0, keepdims=True)
    shift_grad = jnp.sum(incoming, 0, keepdims=True)
    return inner * inv_std, gain_grad, shift_grad


def head_mask(half, value):
    lane = lax.broadcasted_iota(jnp.int32, (1, PAIR), 1)
    inside = jnp.logical_and(lane >= half * HEAD, lane < (half + 1) * HEAD)
    return jnp.where(inside, value, 0.0).astype(BF16)


def pair_columns(pair):
    return pl.ds(pl.multiple_of(pair * PAIR, PAIR), PAIR)


def attend(q_ref, k_ref, v_ref, key_seg_ref, query_seg_ref, prob_ref, out_ref):
    queries = q_ref.shape[0]
    block = min(QUERY_BLOCK, queries)

    def one_pair(pair, carry):
        cols = pair_columns(pair)
        keys, values = k_ref[:, cols], v_ref[:, cols]
        for start in range(0, queries, block):
            rows = pl.ds(start, block)
            query = q_ref[rows, cols]
            allowed = key_seg_ref[...] == query_seg_ref[:, rows]
            total = None
            for half in range(2):
                scores = mm_nt(keys * head_mask(half, HEAD**-0.5), query)
                scores = jnp.where(allowed, scores, MASKED_SCORE)
                peak = jnp.max(scores, 0, keepdims=True)
                weights = jnp.exp(scores - peak)
                soft = (weights * (1.0 / jnp.sum(weights, 0, keepdims=True))).astype(BF16)
                prob_ref[pair * 2 + half, :, rows] = soft
                part = mm_tn(soft, values * head_mask(half, 1.0))
                total = part if total is None else total + part
            out_ref[rows, cols] = total.astype(BF16)
        return carry

    lax.fori_loop(0, HEADS // 2, one_pair, 0)


def attend_back(q_ref, k_ref, v_ref, prob_ref, grad_ref, dq_ref, dk_ref, dv_ref):
    queries = q_ref.shape[0]
    block = min(QUERY_BLOCK, queries)
    scaling = HEAD**-0.5

    def one_pair(pair, carry):
        cols = pair_columns(pair)
        keys, values = k_ref[:, cols], v_ref[:, cols]
        key_sum = value_sum = None
        for start in range(0, queries, block):
            rows = pl.ds(start, block)
            query, grad = q_ref[rows, cols], grad_ref[rows, cols]
            query_sum = None
            for half in range(2):
                mask = head_mask(half, 1.0)
                soft = prob_ref[pair * 2 + half, :, rows]
                weights = soft.astype(F32)
                grad_soft = mm_nt(values * mask, grad)
                product = weights * grad_soft
                inner = jnp.sum(product, 0, keepdims=True)
                grad_scores = (product - weights * inner).astype(BF16)
                value_part = mm(soft, grad * mask)
                key_part = mm(grad_scores, query * mask)
                query_part = mm_tn(grad_scores, keys * mask)
                value_sum = value_part if value_sum is None else value_sum + value_part
                key_sum = key_part if key_sum is None else key_sum + key_part
                query_sum = query_part if query_sum is None else query_sum + query_part
            dq_ref[rows, cols] = (query_sum * scaling).astype(BF16)
        dk_ref[:, cols] = (key_sum * scaling).astype(BF16)
        dv_ref[:, cols] = value_sum.astype(BF16)
        return carry

    lax.fori_loop(0, HEADS // 2, one_pair, 0)


def reorder(core, position, bits):
    if core == 0:
        return position
    return sum(((position >> bit) & 1) << (bits - 1 - bit) for bit in range(bits))


class Layout:
    def __init__(self, dp_size, tensor_size):
        self.dp, self.tensor = dp_size, tensor_size
        self.bits = tensor_size.bit_length() - 1
        self.planes = dp_size // 2
        self.parts = tensor_size // GROUP
        self.rows = D // dp_size
        self.quad = tensor_size == 4
        self.width = D // self.parts

    def pairs(self, move):
        return [
            (d * self.tensor + t, move(d, t)) for d in range(self.dp) for t in range(self.tensor)
        ]

    def inplane(self, bit):
        return self.pairs(
            lambda d, t: d * self.tensor + (t ^ reorder(d & 1, 1 << bit, self.bits))
        )

    def inplane_position(self, position):
        return self.pairs(
            lambda d, t: d * self.tensor + (t ^ reorder(d & 1, position, self.bits))
        )

    def plain_inplane(self, offset):
        return self.pairs(lambda d, t: d * self.tensor + (t ^ offset))

    def other_core(self):
        return self.pairs(lambda d, t: (d ^ 1) * self.tensor + t)


def send(values, pairs):
    return lax.ppermute(values, AXES, pairs)


def gather_inplane(layout, piece, forwarded=None):
    pieces = [piece]
    for bit in range(layout.bits):
        if forwarded is not None and bit + 1 == layout.bits:
            pieces = pieces[:1] + [forwarded(one) for one in pieces[1:]]
        pieces = pieces + [send(one, layout.inplane(bit)) for one in pieces]
    return pieces


def gather_inplane_direct(layout, piece):
    return [piece] + [
        send(piece, layout.inplane_position(position)) for position in range(1, layout.tensor)
    ]


def exchange_planes(layout, pieces):
    groups = [list(range(core, layout.dp, 2)) for core in range(2)]
    return lax.all_to_all(pieces, "dp", 0, 0, axis_index_groups=groups, tiled=True)


def exchange_inplane(pieces):
    return lax.all_to_all(pieces, "tensor", 0, 0, tiled=True)


def swap_cores(layout, values):
    return send(values, layout.other_core())


def add_low(*values):
    return sum(one.astype(F32) for one in values).astype(BF16)


def halves_sum(kept, got):
    half = kept.shape[0] // 2
    upper = add_low(kept[half:], got[half:])
    lower = add_low(kept[:half], got[:half])
    return upper, lower


def reduce_last(layout, upper, lower):
    uppers = []
    for bit in reversed(range(1, layout.bits)):
        upper, lower = halves_sum(lower, send(upper, layout.inplane(bit)))
        uppers.append(upper)
    return uppers, lower, send(upper, layout.inplane(0))


def whole_kernel(body, out_shape, scratch=(), flops=0, moved=0, name=None):
    def call(*operands, far=(), after=()):
        near = len(operands)
        operands = operands + tuple(far)
        read = len(operands)

        def without_after(*refs):
            place = lax.axis_index("dp"), lax.axis_index("tensor")
            info = (place[0] % 2, place[0] // 2, place[1])
            body(info, *refs[:read], *refs[read + len(after) :])

        return pl.pallas_call(
            without_after,
            out_shape=out_shape,
            in_specs=[pl.BlockSpec(memory_space=pltpu.VMEM)] * near
            + [pl.BlockSpec(memory_space=pl.ANY)] * (len(far) + len(after)),
            out_specs=jax.tree.map(lambda _: pl.BlockSpec(memory_space=pltpu.VMEM), out_shape),
            scratch_shapes=list(scratch),
            compiler_params=pltpu.CompilerParams(vmem_limit_bytes=VMEM_BYTES),
            cost_estimate=pl.CostEstimate(flops=flops, bytes_accessed=moved, transcendentals=0),
            name=name,
        )(*operands, *after)

    return call


def low_shape(*shape):
    return jax.ShapeDtypeStruct(shape, BF16)


def wide_shape(*shape):
    return jax.ShapeDtypeStruct(shape, F32)


UNIT = 2 * D * D * D


def owner_at(info_ref, layout, position, other=False):
    core = info_ref[0]
    first = 1 if other else 0
    offset = jnp.where(
        core == first, reorder(0, position, layout.bits), reorder(1, position, layout.bits)
    )
    return jnp.bitwise_xor(info_ref[2], offset)


def row_start(info_ref, layout, plane, other=False):
    core = 1 - info_ref[0] if other else info_ref[0]
    return pl.multiple_of((plane * 2 + core) * layout.rows, layout.rows)


def quad_matrix(info_ref, position):
    tensor = info_ref[2]
    side = jnp.bitwise_xor(lax.rem(tensor, 2), lax.div(tensor, 2))
    return jnp.bitwise_xor(side, position // 2) * 2 + position % 2


def weight_chunk(layout):
    rows = layout.rows

    def body(info_ref, source_ref, norm_ref, out_ref, tile):
        for group in range(2):
            for position in range(2):
                start = (2 * group + position) * rows
                block = source_ref[group * GROUP + quad_matrix(info_ref, position)].astype(BF16)
                for plane in range(layout.planes):
                    out_ref[plane, start : start + rows, :] = block
        tile[...] = jnp.zeros_like(tile)
        for block in range(layout.dp):

            @pl.when(info_ref[1] * 2 + info_ref[0] == block)
            def _():
                tile[0:6, block * rows : (block + 1) * rows] = norm_ref[...]

        for plane in range(layout.planes):
            out_ref[plane, 4 * rows :, :] = tile[...].astype(BF16)

    return whole_kernel(
        body,
        low_shape(layout.planes, 4 * rows + NORM_ROWS, D),
        scratch=[pltpu.VMEM((NORM_ROWS, D), F32)],
        moved=1 << 20,
        name="weight_chunk",
    )


def weight_split(layout):
    rows, planes = layout.rows, layout.planes

    def body(info_ref, *refs):
        all_ref, outs, tile_ref = refs[0], refs[1:5], refs[5]
        tile = None
        for slot in range(planes):
            for index in range(4):
                outs[index][slot] = all_ref[slot, index * rows : (index + 1) * rows, :]
            part = all_ref[slot, 4 * rows :, :].astype(F32)
            tile = part if tile is None else tile + part
        tile_ref[...] = tile.astype(BF16)

    one = low_shape(planes, rows, D)
    return whole_kernel(
        body, (one,) * 4 + (low_shape(NORM_ROWS, D),), moved=2 << 20, name="weight_split"
    )


def fetch_weights(info_ref, layout, refs, weights_ref, sems):
    if not layout.quad:
        copies = [pltpu.make_async_copy(refs[0], weights_ref, sems.at[0])]
    else:
        copies = []
        for index, ref in enumerate(refs):
            matrix = quad_matrix(info_ref, index % GROUP)
            for plane in range(layout.planes):
                at = pl.ds(row_start(info_ref, layout, plane, index >= GROUP), layout.rows)
                copies.append(
                    pltpu.make_async_copy(
                        ref.at[plane], weights_ref.at[matrix, at, :], sems.at[len(copies)]
                    )
                )
    for copy in copies:
        copy.start()
    return copies


def weight_pieces(layout):
    return (2 * GROUP, 2 * GROUP * layout.planes) if layout.quad else (1, 1)


def place_grads(info_ref, layout, grads_ref, keep_ref, send_ref):
    for other, ref in ((False, keep_ref), (True, send_ref)):
        for position in range(layout.tensor):
            owner = owner_at(info_ref, layout, position, other)
            for slot in range(layout.planes):
                rows = pl.ds(row_start(info_ref, layout, slot, other), layout.rows)
                if layout.parts == 1:
                    block = grads_ref[owner, rows, :]
                else:
                    part = lax.rem(owner, layout.parts) * layout.width
                    cols = pl.ds(pl.multiple_of(part, layout.width), layout.width)
                    block = grads_ref[lax.div(owner, layout.parts), rows, cols]
                ref[position, slot, 0 : layout.rows, :] = block


def self_forward(layout, tokens):
    count, copies = weight_pieces(layout)

    def body(info_ref, x_ref, query_seg_ref, key_seg_ref, tile_ref, other_tile_ref, *refs):
        w_ref, gains_ref, a_ref, q_ref, k_ref, v_ref = refs[count : count + 6]
        prob_ref, mix_ref, mid_ref, c_ref, sems = refs[count + 6 :]
        moving = fetch_weights(info_ref, layout, refs[:count], w_ref, sems)
        gains_ref[...] = tile_ref[...].astype(F32) + other_tile_ref[...].astype(F32)
        values = x_ref[...].astype(F32)
        normed, _ = normalized(values)
        a_ref[...] = (normed * gains_ref[0:1, :] + gains_ref[1:2, :]).astype(BF16)
        for copy in moving:
            copy.wait()
        for index, ref in enumerate((q_ref, k_ref, v_ref)):
            ref[...] = mm(a_ref[...], w_ref[index]).astype(BF16)
        attend(q_ref, k_ref, v_ref, key_seg_ref, query_seg_ref, prob_ref, mix_ref)
        mid = x_ref[...].astype(F32) + mm(mix_ref[...], w_ref[3])
        mid_ref[...] = mid
        normed, _ = normalized(mid)
        c_ref[...] = (normed * gains_ref[2:3, :] + gains_ref[3:4, :]).astype(BF16)

    low = low_shape(tokens, D)
    return whole_kernel(
        body,
        (
            low_shape(GROUP, D, D),
            wide_shape(NORM_ROWS, D),
            low,
            low,
            low,
            low,
            low_shape(HEADS, tokens, tokens),
            low,
            wide_shape(tokens, D),
            low,
        ),
        scratch=[pltpu.SemaphoreType.DMA((copies,))],
        flops=14 * UNIT,
        moved=12 << 20,
        name="self_forward",
    )


def cross_forward(layout, tokens, states):
    count, copies = weight_pieces(layout)

    def body(
        info_ref, c_ref, enc_ref, mid_ref, gains_ref, query_seg_ref, key_seg_ref, *refs
    ):
        w_ref, q_ref, k_ref, v_ref, prob_ref, mix_ref, late_ref, f_ref, sems = refs[count:]
        for copy in fetch_weights(info_ref, layout, refs[:count], w_ref, sems):
            copy.wait()
        q_ref[...] = mm(c_ref[...], w_ref[0]).astype(BF16)
        k_ref[...] = mm(enc_ref[...], w_ref[1]).astype(BF16)
        v_ref[...] = mm(enc_ref[...], w_ref[2]).astype(BF16)
        attend(q_ref, k_ref, v_ref, key_seg_ref, query_seg_ref, prob_ref, mix_ref)
        late = mid_ref[...] + mm(mix_ref[...], w_ref[3])
        late_ref[...] = late
        normed, _ = normalized(late)
        f_ref[...] = (normed * gains_ref[4:5, :] + gains_ref[5:6, :]).astype(BF16)

    low = low_shape(tokens, D)
    return whole_kernel(
        body,
        (
            low_shape(GROUP, D, D),
            low,
            low_shape(states, D),
            low_shape(states, D),
            low_shape(HEADS, states, tokens),
            low,
            wide_shape(tokens, D),
            low,
        ),
        scratch=[pltpu.SemaphoreType.DMA((copies,))],
        flops=14 * UNIT,
        moved=12 << 20,
        name="cross_forward",
    )


def gelu_parts(pre):
    slope = math.sqrt(2.0 / math.pi)
    square = pre * pre
    bent = jnp.tanh(slope * pre * (1.0 + 0.044715 * square))
    half = 0.5 * (1.0 + bent)
    inner = slope * (1.0 + 3 * 0.044715 * square)
    return pre * half, half + 0.5 * pre * (1.0 - bent * bent) * inner


def feed_forward(layout, tokens, hidden):
    count = layout.tensor
    planes = layout.planes
    piece_rows = D // planes

    def body(info_ref, f_ref, cot_ref, late_ref, gains_ref, *refs):
        mine, others = refs[:count], refs[count : 2 * count]
        out_ref, glate_ref, dlate_ref, norm_ref, keep_ref, send_ref = refs[2 * count : -7]
        w_in, w_out, f_t, cot_t, value_sum, back_sum, sems = refs[-7:]
        core = info_ref[0]

        def fetch(source, target, matrix, position):
            return pltpu.make_async_copy(source, target.at[position], sems.at[matrix, position])

        for position in range(count):
            turned = reorder(1, position, layout.bits)

            @pl.when(core == 0)
            def _():
                fetch(mine[position], w_in, 0, position).start()
                fetch(others[turned], w_out, 1, position).start()

            @pl.when(core != 0)
            def _():
                fetch(others[position], w_in, 0, position).start()
                fetch(mine[turned], w_out, 1, position).start()

        f_t[...] = f_ref[...].T
        cot_t[...] = cot_ref[...].T
        value_sum[...] = jnp.zeros_like(value_sum)
        back_sum[...] = jnp.zeros_like(back_sum)

        def one_block(position, carry):
            turned = sum(
                ((position >> bit) & 1) << (layout.bits - 1 - bit) for bit in range(layout.bits)
            )
            fetch(mine[0], w_in, 0, position).wait()
            fetch(mine[0], w_out, 1, position).wait()
            first, second = w_in[position], w_out[position]
            cot = cot_ref[...]
            pre = mm(f_ref[...], first)
            post, slope = gelu_parts(pre)
            post = post.astype(BF16)
            value_sum[...] += mm_nt(post, second)
            d_pre = (slope * mm(cot, second)).astype(BF16)
            back_sum[...] += mm_nt(d_pre, first)
            grad_in = mm(f_t[...], d_pre).astype(BF16)
            grad_out = mm(cot_t[...], post).astype(BF16)
            for slot in range(planes):
                part = slice(slot * piece_rows, (slot + 1) * piece_rows)

                @pl.when(core == 0)
                def _():
                    keep_ref[position, slot] = grad_in[part]
                    send_ref[turned, slot] = grad_out[part]

                @pl.when(core != 0)
                def _():
                    keep_ref[turned, slot] = grad_out[part]
                    send_ref[position, slot] = grad_in[part]

            return carry

        lax.fori_loop(0, count, one_block, 0)
        late = late_ref[...]
        out_ref[...] = (late + value_sum[...]).astype(BF16)
        back, gain_grad, shift_grad = norm_backward(back_sum[...], late, gains_ref[4:5, :])
        grad_late = cot_ref[...].astype(F32) + back
        glate_ref[...] = grad_late
        dlate_ref[...] = grad_late.astype(BF16)
        norm_ref[0:1, :] = gain_grad
        norm_ref[1:2, :] = shift_grad

    low = low_shape(tokens, D)
    pieces = low_shape(count, planes, piece_rows, hidden)
    return whole_kernel(
        body,
        (low, wide_shape(tokens, D), low, wide_shape(2, D), pieces, pieces),
        scratch=[
            pltpu.VMEM((count, D, hidden), BF16),
            pltpu.VMEM((count, D, hidden), BF16),
            pltpu.VMEM((D, tokens), BF16),
            pltpu.VMEM((D, tokens), BF16),
            pltpu.VMEM((tokens, D), F32),
            pltpu.VMEM((tokens, D), F32),
            pltpu.SemaphoreType.DMA((2, count)),
        ],
        flops=6 * UNIT * count * hidden // D,
        moved=14 << 20,
        name="feed_forward",
    )


def mixed_back(tokens, name):
    def body(info_ref, grad_ref, mix_ref, w_ref, out_ref, d_mix):
        out_ref[...] = mm_tn(mix_ref[...], grad_ref[...]).astype(BF16)
        d_mix[...] = mm_nt(grad_ref[...], w_ref[3]).astype(BF16)

    return whole_kernel(
        body,
        (low_shape(D, D), low_shape(tokens, D)),
        flops=2 * UNIT,
        moved=3 << 20,
        name=name,
    )


def cross_backward(layout, tokens, states):
    def body(
        info_ref,
        out_grad_ref,
        d_mix,
        glate_ref,
        w_ref,
        q_ref,
        k_ref,
        v_ref,
        prob_ref,
        c_ref,
        enc_ref,
        mid_ref,
        gains_ref,
        enc_grad_ref,
        gmid_ref,
        dmid_ref,
        norm_ref,
        keep_ref,
        send_ref,
        dq,
        dk,
        dv,
        grads,
    ):
        grads[3] = out_grad_ref[...]
        attend_back(q_ref, k_ref, v_ref, prob_ref, d_mix, dq, dk, dv)
        grads[0] = mm_tn(c_ref[...], dq[...]).astype(BF16)
        enc_t = enc_ref[...].T
        grads[1] = mm(enc_t, dk[...]).astype(BF16)
        grads[2] = mm(enc_t, dv[...]).astype(BF16)
        place_grads(info_ref, layout, grads, keep_ref, send_ref)
        enc_grad_ref[...] = (mm_nt(dk[...], w_ref[1]) + mm_nt(dv[...], w_ref[2])).astype(BF16)
        back, gain_grad, shift_grad = norm_backward(
            mm_nt(dq[...], w_ref[0]), mid_ref[...], gains_ref[2:3, :]
        )
        grad_mid = glate_ref[...] + back
        gmid_ref[...] = grad_mid
        dmid_ref[...] = grad_mid.astype(BF16)
        norm_ref[0:1, :] = gain_grad
        norm_ref[1:2, :] = shift_grad

    low = low_shape(tokens, D)
    pieces = low_shape(layout.tensor, layout.planes, layout.rows, layout.width)
    return whole_kernel(
        body,
        (low_shape(states, D), wide_shape(tokens, D), low, wide_shape(2, D), pieces, pieces),
        scratch=[
            pltpu.VMEM((tokens, D), BF16),
            pltpu.VMEM((states, D), BF16),
            pltpu.VMEM((states, D), BF16),
            pltpu.VMEM((GROUP, D, D), BF16),
        ],
        flops=24 * UNIT,
        moved=14 << 20,
        name="cross_backward",
    )


def self_attention_back(layout, tokens):
    def body(info_ref, dmid_ref, mix_ref, w_ref, q_ref, k_ref, v_ref, prob_ref, *refs):
        out_ref, dq, dk, dv, d_mix = refs
        out_ref[...] = mm_tn(mix_ref[...], dmid_ref[...]).astype(BF16)
        d_mix[...] = mm_nt(dmid_ref[...], w_ref[3]).astype(BF16)
        attend_back(q_ref, k_ref, v_ref, prob_ref, d_mix, dq, dk, dv)

    low = low_shape(tokens, D)
    return whole_kernel(
        body,
        (low_shape(D, D), low, low, low),
        scratch=[pltpu.VMEM((tokens, D), BF16)],
        flops=18 * UNIT,
        moved=10 << 20,
        name="self_attention_back",
    )


def self_backward(layout, tokens):
    def body(
        info_ref,
        out_grad_ref,
        dq,
        dk,
        dv,
        gmid_ref,
        w_ref,
        a_ref,
        x_ref,
        gains_ref,
        norm_two_ref,
        norm_three_ref,
        grad_ref,
        keep_ref,
        send_ref,
        grads,
        norms,
        tile,
    ):
        grads[3] = out_grad_ref[...]
        a_t = a_ref[...].T
        total = None
        for index, ref in enumerate((dq, dk, dv)):
            grads[index] = mm(a_t, ref[...]).astype(BF16)
            part = mm_nt(ref[...], w_ref[index])
            total = part if total is None else total + part
        place_grads(info_ref, layout, grads, keep_ref, send_ref)
        back, gain_grad, shift_grad = norm_backward(
            total, x_ref[...].astype(F32), gains_ref[0:1, :]
        )
        grad_ref[...] = (gmid_ref[...] + back).astype(BF16)
        tile[...] = jnp.zeros_like(tile)
        for index, row in enumerate((gain_grad, shift_grad)):
            norms[index : index + 1, :] = row
        norms[2:4, :] = norm_two_ref[...]
        norms[4:6, :] = norm_three_ref[...]
        for block in range(layout.dp):
            columns = slice(block * layout.rows, (block + 1) * layout.rows)
            tile[block, 0:6, 0 : layout.rows] = norms[0:6, columns].astype(BF16)
        for other, ref in ((False, keep_ref), (True, send_ref)):
            core = 1 - info_ref[0] if other else info_ref[0]
            for slot in range(layout.planes):
                block = tile[slot * 2 + core]
                for position in range(layout.tensor):
                    ref[position, slot, layout.rows :, :] = block

    low = low_shape(tokens, D)
    pieces = low_shape(
        layout.tensor, layout.planes, layout.rows + NORM_ROWS, layout.width
    )
    return whole_kernel(
        body,
        (low, pieces, pieces),
        scratch=[
            pltpu.VMEM((GROUP, D, D), BF16),
            pltpu.VMEM((8, D), F32),
            pltpu.VMEM((layout.dp, NORM_ROWS, layout.width), BF16),
        ],
        flops=7 * UNIT,
        moved=6 << 20,
        name="self_backward",
    )


def sweep(low_ref, rest_ref, poly_ref, width, kept):
    half = D // 2
    shift = jnp.zeros((), F32)
    for start in range(0, width, D):
        part = low_ref[:, start : start + D].astype(F32)
        shift = shift + jnp.sum(part * part)
    shift = shift * (1.0 / D)
    diagonal = lax.broadcasted_iota(jnp.int32, (half, half), 0) == lax.broadcasted_iota(
        jnp.int32, (half, half), 1
    )
    shifted = jnp.where(diagonal, shift, 0.0)
    top, bottom = slice(0, half), slice(half, D)
    upper, lower = low_ref[top, :], low_ref[bottom, :]
    rest_ref[top, top] = (mm_nt(upper, upper) - shifted).astype(BF16)
    corner = mm_nt(upper, lower).astype(BF16)
    rest_ref[top, bottom] = corner
    rest_ref[bottom, top] = corner.T
    rest_ref[bottom, bottom] = (mm_nt(lower, lower) - shifted).astype(BF16)
    slope = POLY_SECOND + 2.0 * POLY_THIRD * shift
    scale = POLY_FIRST + POLY_SECOND * shift + POLY_THIRD * shift * shift
    for rows in (top, bottom):
        square = mm(rest_ref[rows, :], rest_ref[...])
        poly = slope * rest_ref[rows, :].astype(F32) + POLY_THIRD * square
        poly_ref[rows, :] = poly.astype(BF16)
    for start in range(0, kept, D):
        cols = slice(start, min(start + D, kept))
        part = low_ref[:, cols]
        low_ref[:, cols] = (scale * part.astype(F32) + mm(poly_ref[...], part)).astype(BF16)


def sweeps(low_ref, rest_ref, poly_ref, width, kept):
    def one(step, carry):
        sweep(low_ref, rest_ref, poly_ref, width, width)
        return carry

    lax.fori_loop(0, NS_STEPS - 1, one, 0)
    sweep(low_ref, rest_ref, poly_ref, width, kept)


def orthogonalize_attention(layout):
    parts, rows, planes = layout.parts, layout.rows, layout.planes

    def body(info_ref, *refs):
        pieces = refs[: 2 * parts]
        mine_ref, other_ref, low, rest, poly = refs[2 * parts :]
        cross = info_ref[0] != 0
        for part in range(parts):
            cols = slice(part * layout.width, (part + 1) * layout.width)
            for half in range(2):
                for slot in range(planes):
                    start = (half * planes + slot) * rows
                    both = pieces[2 * part + half]
                    low[start : start + rows, cols] = jnp.where(
                        cross, both[slot, 0:rows, :], both[slot, rows : 2 * rows, :]
                    )
        values = low[...].astype(F32)
        inverse = 1.0 / (jnp.sqrt(jnp.sum(values * values)) + 1e-07)
        low[...] = (values * inverse).astype(BF16)
        sweeps(low, rest, poly, D, D)
        start = pl.multiple_of(info_ref[1] * rows, rows)
        mine_ref[...] = low[pl.ds(start, rows), 0 : layout.width]
        other_ref[...] = low[pl.ds(planes * rows + start, rows), 0 : layout.width]

    return whole_kernel(
        body,
        (low_shape(rows, layout.width), low_shape(rows, layout.width)),
        scratch=[pltpu.VMEM((D, D), BF16)] * 3,
        flops=15 * UNIT,
        moved=2 << 20,
        name="orthogonalize_attention",
    )


def orthogonalize_wide(layout, hidden):
    count = layout.tensor

    def body(info_ref, *refs):
        pieces = refs[:count]
        out_ref, low, rest, poly = refs[count:]
        total = jnp.zeros((), F32)
        for ref in pieces:
            values = ref[...].astype(F32)
            total = total + jnp.sum(values * values)
        inverse = 1.0 / (jnp.sqrt(total) + 1e-07)
        for index, ref in enumerate(pieces):
            low[:, index * hidden : (index + 1) * hidden] = (
                ref[...].astype(F32) * inverse
            ).astype(BF16)
        sweeps(low, rest, poly, count * hidden, hidden)
        out_ref[...] = low[:, 0:hidden]

    return whole_kernel(
        body,
        low_shape(D, hidden),
        scratch=[pltpu.VMEM((D, count * hidden), BF16)] + [pltpu.VMEM((D, D), BF16)] * 2,
        flops=45 * UNIT,
        moved=3 << 20,
        name="orthogonalize_wide",
    )


def wide_shard(hidden):
    def body(info_ref, expand_ref, contract_ref, out_ref):
        @pl.when(info_ref[0] == 0)
        def _():
            out_ref[...] = expand_ref[...].astype(BF16)

        @pl.when(info_ref[0] != 0)
        def _():
            out_ref[...] = contract_ref[...].T.astype(BF16)

    return whole_kernel(body, low_shape(D, hidden), moved=3 << 20, name="wide_shard")


def rounded_rows(layout, group, name):
    def body(info_ref, source_ref, out_ref):
        out_ref[...] = source_ref[group * GROUP : (group + 1) * GROUP].astype(BF16)

    return whole_kernel(body, low_shape(GROUP, layout.rows, D), moved=2 << 20, name=name)


def fence(values, after):
    def body(source_ref, *refs):
        pass

    return pl.pallas_call(
        body,
        out_shape=jax.ShapeDtypeStruct(values.shape, values.dtype),
        in_specs=[pl.BlockSpec(memory_space=pl.ANY)] * (1 + len(after)),
        out_specs=pl.BlockSpec(memory_space=pl.ANY),
        input_output_aliases={0: 0},
        name="fence",
    )(values, *after)


def nest_of(grad, momentum):
    return (1.0 + MOMENTUM_DECAY) * grad + MOMENTUM_DECAY * MOMENTUM_DECAY * momentum


def wide_nest(layout, hidden):
    count = layout.planes

    def body(info_ref, got_ref, momentum_ref, out_ref):
        total = sum(got_ref[plane].astype(F32) for plane in range(count))
        nest = nest_of(total, momentum_ref[...]).astype(BF16)
        for plane in range(count):
            out_ref[plane] = nest

    return whole_kernel(
        body, low_shape(count, D // count, hidden), moved=1 << 20, name="wide_nest"
    )


def wide_slots_sum(layout, hidden):
    def body(info_ref, kept_ref, got_ref, out_ref):
        out_ref[...] = (kept_ref[0].astype(F32) + got_ref[0].astype(F32)).astype(BF16)

    shape = low_shape(layout.planes, D // layout.planes, hidden)
    return whole_kernel(body, shape, moved=1 << 20, name="wide_slots_sum")


def attention_slots(layout):
    rows, planes, width = layout.rows, layout.planes, layout.width

    def body(info_ref, cross_ref, cross_got, self_ref, self_got, out_ref):
        for slot in range(planes):
            for start, kept, got in ((0, cross_ref, cross_got), (rows, self_ref, self_got)):
                total = kept[0, slot].astype(F32) + got[0, slot].astype(F32)
                out_ref[slot, start : start + total.shape[0], :] = total.astype(BF16)

    return whole_kernel(
        body,
        low_shape(planes, 2 * rows + NORM_ROWS, width),
        moved=2 << 20,
        name="attention_slots",
    )


def attention_nest(layout):
    rows, planes, width = layout.rows, layout.planes, layout.width

    def body(info_ref, got_ref, momentum_ref, nest_ref, grad_ref, norm_ref):
        total = sum(got_ref[plane].astype(F32) for plane in range(planes))
        tensor = info_ref[2]
        cols = slice(None)
        if layout.parts > 1:
            part = lax.rem(tensor, layout.parts) * width
            cols = pl.ds(pl.multiple_of(part, width), width)
        for index, group in enumerate((1, 0)):
            here = slice(index * rows, (index + 1) * rows)
            momentum = momentum_ref[group * GROUP + lax.div(tensor, layout.parts), :, cols]
            nest = nest_of(total[here], momentum).astype(BF16)
            for plane in range(planes):
                nest_ref[plane, here, :] = nest
        grad_ref[...] = total[0 : 2 * rows].astype(BF16)
        norm_ref[...] = total[2 * rows : 2 * rows + 8]

    return whole_kernel(
        body,
        (
            low_shape(planes, 2 * rows, width),
            low_shape(2 * rows, width),
            wide_shape(8, width),
        ),
        moved=2 << 20,
        name="attention_nest",
    )


def wide_momentum(layout, hidden):
    piece_rows = D // layout.planes

    def body(info_ref, expand_ref, contract_ref, out_ref, turned):
        rows = pl.ds(pl.multiple_of(info_ref[1] * piece_rows, piece_rows), piece_rows)
        turned[...] = contract_ref[...].T
        out_ref[...] = jnp.where(info_ref[0] == 0, expand_ref[rows, :], turned[rows, :])

    return whole_kernel(
        body,
        wide_shape(piece_rows, hidden),
        scratch=[pltpu.VMEM((D, hidden), F32)],
        moved=3 << 20,
        name="wide_momentum",
    )


def decayed(master, share, scale):
    return master - MUON_RATE * (MUON_DECAY * master + scale * share)


def finish_wide(layout, hidden, full_hidden):
    scale = 0.2 * math.sqrt(max(D, full_hidden))

    def body(info_ref, mine_ref, other_ref, expand_ref, contract_ref, *refs):
        e_new, e_low, c_new, c_low = refs
        first = info_ref[0] == 0
        mine, other = mine_ref[...], other_ref[...]
        new = decayed(expand_ref[...], jnp.where(first, mine, other).astype(F32), scale)
        e_new[...] = new
        e_low[...] = new.astype(BF16)
        new = decayed(contract_ref[...], jnp.where(first, other, mine).T.astype(F32), scale)
        c_new[...] = new
        c_low[...] = new.astype(BF16)

    return whole_kernel(
        body,
        (wide_shape(D, hidden), low_shape(D, hidden), wide_shape(hidden, D), low_shape(hidden, D)),
        moved=6 << 20,
        name="finish_wide",
    )


def wide_velocity(layout, hidden):
    grad_share = 1.0 / (1.0 + MOMENTUM_DECAY)
    momentum_share = MOMENTUM_DECAY - MOMENTUM_DECAY * MOMENTUM_DECAY * grad_share

    def body(info_ref, mine_ref, other_ref, expand_ref, contract_ref, e_new, c_new):
        first = info_ref[0] == 0
        mine, other = mine_ref[...], other_ref[...]
        nest = jnp.where(first, mine, other).astype(F32)
        e_new[...] = momentum_share * expand_ref[...] + grad_share * nest
        nest = jnp.where(first, other, mine).T.astype(F32)
        c_new[...] = momentum_share * contract_ref[...] + grad_share * nest

    return whole_kernel(
        body,
        (wide_shape(D, hidden), wide_shape(hidden, D)),
        moved=6 << 20,
        name="wide_velocity",
    )


def finish_attention(layout):
    count = layout.tensor
    scale = 0.2 * math.sqrt(D)

    def body(info_ref, *refs):
        late, early = refs[:count], refs[count : 2 * count]
        master_ref, momentum_ref, new_ref, velocity_ref, low_ref = refs[2 * count :]
        rows = layout.rows
        for position in range(count):
            owner = owner_at(info_ref, layout, position)
            cols = slice(None)
            if layout.parts > 1:
                part = lax.rem(owner, layout.parts) * layout.width
                cols = pl.ds(pl.multiple_of(part, layout.width), layout.width)
            for group in range(2):
                index = group * GROUP + lax.div(owner, layout.parts)
                at = info_ref[0] if group == 0 else 1 - info_ref[0]
                share = late[position][at].astype(F32)
                new = decayed(master_ref[index, :, cols], share, scale)
                new_ref[index, :, cols] = new
                low_ref[index, :, cols] = new.astype(BF16)
                start = (1 - group) * rows
                grad = early[position][start : start + rows, :].astype(F32)
                velocity_ref[index, :, cols] = (
                    MOMENTUM_DECAY * momentum_ref[index, :, cols] + grad
                )

    shape = (2 * GROUP, layout.rows, D)
    return whole_kernel(
        body,
        (wide_shape(*shape), wide_shape(*shape), low_shape(*shape)),
        moved=6 << 20,
        name="finish_attention",
    )


def device_program(layout, arguments):
    (
        inputs,
        encoder,
        dec_segments,
        enc_segments,
        cotangent,
        attn_master,
        attn_momentum,
        expand_master,
        expand_momentum,
        contract_master,
        contract_momentum,
        norm_params,
        first_moments,
        second_moments,
    ) = arguments
    tokens, states = inputs.shape[1], encoder.shape[1]
    hidden = expand_master.shape[1]
    full_hidden = hidden * layout.tensor
    dp_at, tensor_at = lax.axis_index("dp"), lax.axis_index("tensor")
    x, enc, cot = inputs[0], encoder[0], cotangent[0]

    if layout.quad:
        chunk = weight_chunk(layout)(attn_master, norm_params)
        slots = exchange_planes(layout, chunk)
        shard = wide_shard(hidden)(expand_master, contract_master, after=[chunk])
        near, far = send(shard, layout.inplane(0)), send(shard, layout.inplane(1))
        first, second, cross_first, cross_second, tile = weight_split(layout)(
            slots, after=[near, far]
        )
        wide_own = [shard, near, far]
        wide_other = [swap_cores(layout, piece) for piece in wide_own]
        got_first = send(first, layout.plain_inplane(1))
        got_second = send(second, layout.plain_inplane(2))
        tiles = [tile, swap_cores(layout, tile)]
        self_own = [first, second, got_first, got_second]
        self_pieces = self_own + [swap_cores(layout, piece) for piece in self_own]
        before = wide_other
        wide_own[1] = fence(near, [got_first])
        farthest = send(wide_own[1], layout.inplane(1))
    else:
        low = attn_master.astype(BF16)
        norm_low = lax.all_gather(norm_params.astype(BF16), "dp", axis=1, tiled=True)
        padded = jnp.concatenate([norm_low, jnp.zeros((NORM_ROWS - 6, D), BF16)])
        self_low = lax.all_gather(low[:GROUP], "dp", axis=1, tiled=True)
        cross_low = lax.all_gather(low[GROUP:], "dp", axis=1, tiled=True)
        self_pieces, before = [self_low], []
        tiles = [padded, jnp.zeros_like(padded)]
        shard = wide_shard(hidden)(expand_master, contract_master)
        wide_own = [shard, send(shard, layout.inplane(0))]
        for bit in range(1, layout.bits):
            wide_own = wide_own + [send(piece, layout.inplane(bit)) for piece in wide_own]
        wide_other = [swap_cores(layout, piece) for piece in wide_own]

    dec_row, dec_column = dec_segments.reshape(1, tokens), dec_segments.reshape(tokens, 1)
    enc_column = enc_segments.reshape(states, 1)
    w_self, gains, a, q, k, v, self_prob, self_mix, mid, c = self_forward(layout, tokens)(
        x, dec_row, dec_column, *tiles, far=self_pieces, after=before
    )
    if layout.quad:
        cross_own = [
            cross_first,
            cross_second,
            send(cross_first, layout.plain_inplane(1)),
            send(cross_second, layout.plain_inplane(2)),
        ]
        cross_own = [fence(piece, [c, farthest]) for piece in cross_own]
        cross_pieces = cross_own + [swap_cores(layout, piece) for piece in cross_own]
        wide_own = wide_own + [fence(farthest, [cross_own[0]])]
        wide_other = wide_other + [swap_cores(layout, wide_own[3])]
    else:
        cross_pieces = [cross_low]
    w_cross, qc, kc, vc, cross_prob, cross_mix, late, f = cross_forward(layout, tokens, states)(
        c, enc, mid, gains, dec_row, enc_column, far=cross_pieces, after=[wide_own[-1]],
    )
    wide_pieces = wide_own + wide_other
    output, grad_late, late_low, norm_three, wide_keep, wide_send = feed_forward(
        layout, tokens, hidden
    )(f, cot, late, gains, far=wide_pieces)
    out_grad, d_mix = mixed_back(tokens, "cross_mixed_back")(late_low, cross_mix, w_cross)
    upper, lower = halves_sum(wide_keep, swap_cores(layout, wide_send))
    encoder_grad, grad_mid, mid_low, norm_two, cross_keep, cross_send = cross_backward(
        layout, tokens, states
    )(
        out_grad, d_mix, grad_late, w_cross, qc, kc, vc, cross_prob, c, enc, mid, gains,
        after=[upper],
    )
    wide_uppers, *wide_last = reduce_last(layout, upper, lower)
    self_out_grad, dq, dk, dv = self_attention_back(layout, tokens)(
        mid_low, self_mix, w_self, q, k, v, self_prob, after=wide_uppers
    )
    cross_halves = halves_sum(cross_keep, swap_cores(layout, cross_send))
    input_grad, self_keep, self_send = self_backward(layout, tokens)(
        self_out_grad, dq, dk, dv, grad_mid, w_self, a, x, gains, norm_two, norm_three,
        after=[cross_halves[0]],
    )
    wide_slots = wide_slots_sum(layout, hidden)(*wide_last, after=[self_keep])
    wide_got = exchange_planes(layout, wide_slots)
    self_send = fence(self_send, [wide_slots])
    self_halves = halves_sum(self_keep, swap_cores(layout, self_send))
    cross_uppers, *cross_last = reduce_last(layout, *cross_halves)
    self_uppers, *self_last = reduce_last(layout, *self_halves)

    momentum = wide_momentum(layout, hidden)(expand_momentum, contract_momentum)
    nest_rows = wide_nest(layout, hidden)(
        wide_got, momentum, after=[self_halves[0], *cross_uppers]
    )
    nest = exchange_planes(layout, nest_rows).reshape(D, hidden)
    rows_by_slot = attention_slots(layout)(*cross_last, *self_last, after=[nest])
    attn_nest, attn_grad, norm_rows = attention_nest(layout)(
        exchange_planes(layout, rows_by_slot), attn_momentum
    )
    nest_pieces = gather_inplane(
        layout, nest, lambda piece: fence(piece, [attn_nest])
    )
    nest_pieces = gather_inplane(layout, nest)
    nest_other = swap_cores(layout, nest)

    early = gather_inplane_direct(layout, attn_grad)

    def whole_pieces(halves):
        shared = layout.parts.bit_length() - 1
        gathered = [halves]
        for bit in range(shared):
            pairs = layout.pairs(lambda d, t: d * layout.tensor + (t ^ (1 << bit)))
            gathered = gathered + [[send(half, pairs) for half in one] for one in gathered]
        return [half for one in gathered for half in one]

    wide_ortho = orthogonalize_wide(layout, hidden)(*nest_pieces, after=early[1:])
    half = fence(exchange_planes(layout, attn_nest), [wide_ortho])
    mine, others = orthogonalize_attention(layout)(
        *whole_pieces([half, swap_cores(layout, half)])
    )
    late_pieces = gather_inplane_direct(layout, jnp.stack([mine, swap_cores(layout, others)]))
    attn_updated, attn_velocity, attn_copy = finish_attention(layout)(
        *late_pieces, *early, attn_master, attn_momentum
    )

    expand_updated, expand_copy, contract_updated, contract_copy = finish_wide(
        layout, hidden, full_hidden
    )(wide_ortho, swap_cores(layout, wide_ortho), expand_master, contract_master)
    expand_velocity, contract_velocity = wide_velocity(layout, hidden)(
        nest, nest_other, expand_momentum, contract_momentum
    )

    norm_rows = norm_rows[0:6, 0 : layout.rows].astype(F32)
    first_updated = BETA_FIRST * first_moments + (1.0 - BETA_FIRST) * norm_rows
    second_updated = BETA_SECOND * second_moments + (1.0 - BETA_SECOND) * norm_rows * norm_rows
    corrected = first_updated / (1.0 - BETA_FIRST**STEP)
    denominator = jnp.sqrt(second_updated / (1.0 - BETA_SECOND**STEP)) + ADAM_EPSILON
    norm_updated = norm_params - ADAM_RATE * corrected / denominator
    return (
        output[None],
        input_grad[None],
        encoder_grad[None],
        attn_updated,
        attn_velocity,
        attn_copy,
        expand_updated,
        expand_velocity,
        expand_copy,
        contract_updated,
        contract_velocity,
        contract_copy,
        norm_updated,
        first_updated,
        second_updated,
    )


def solution(mesh):
    layout = Layout(mesh.shape["dp"], mesh.shape["tensor"])

    def local(*arguments):
        return device_program(layout, arguments)

    rows = P(AXES, None, None)
    by_dp, by_column, by_row, norm = P(None, "dp", None), P(None, "tensor"), P("tensor", None), P(None, "dp")
    return jax.shard_map(
        local,
        mesh=mesh,
        in_specs=(rows, rows, P(AXES, None), P(AXES, None), rows)
        + (by_dp, by_dp, by_column, by_column, by_row, by_row, norm, norm, norm),
        out_specs=(rows, rows, rows, by_dp, by_dp, by_dp)
        + (by_column, by_column, by_column, by_row, by_row, by_row, norm, norm, norm),
        check_vma=False,
    )
```

```python
import functools
import math

import jax
import jax.numpy as jnp
from jax import lax
from jax.experimental import pallas as pl
from jax.experimental.pallas import tpu as pltpu
from jax.sharding import PartitionSpec as P

D = 512
HEADS = 8
HEAD = D // HEADS
PAIR = 2 * HEAD
NS_STEPS = 5
STEP = 10

MASKED_SCORE = -1e30
NORM_EPSILON = 1e-05
MOMENTUM_DECAY = 0.95
MUON_RATE = 0.15
MUON_DECAY = 0.01
POLY_FIRST = 3.4445
POLY_SECOND = -4.775
POLY_THIRD = 2.0315
ADAM_RATE = 0.4
BETA_FIRST = 0.9
BETA_SECOND = 0.999
ADAM_EPSILON = 1e-08
GROUP = 4
QUERY_BLOCK = 512

F32 = jnp.float32
BF16 = jnp.bfloat16
AXES = ("dp", "tensor")
MIB = 1 << 20
VMEM_BYTES = 24 * MIB
NORM_ROWS = 16


def mm(left, right):
    return lax.dot_general(left, right, (((1,), (0,)), ((), ())), preferred_element_type=F32)


def mm_nt(left, right):
    return lax.dot_general(left, right, (((1,), (1,)), ((), ())), preferred_element_type=F32)


def mm_tn(left, right):
    return lax.dot_general(left, right, (((0,), (0,)), ((), ())), preferred_element_type=F32)


def normalized(values):
    average = jnp.mean(values, -1, keepdims=True)
    centred = values - average
    inv_std = lax.rsqrt(jnp.mean(centred * centred, -1, keepdims=True) + NORM_EPSILON)
    return centred * inv_std, inv_std


def norm_backward(incoming, values, gain_row):
    normed, inv_std = normalized(values)
    scaled = incoming * gain_row
    inner = (
        scaled
        - jnp.mean(scaled, -1, keepdims=True)
        - normed * jnp.mean(scaled * normed, -1, keepdims=True)
    )
    gain_grad = jnp.sum(incoming * normed, 0, keepdims=True)
    shift_grad = jnp.sum(incoming, 0, keepdims=True)
    return inner * inv_std, gain_grad, shift_grad


def head_mask(half, value):
    lane = lax.broadcasted_iota(jnp.int32, (1, PAIR), 1)
    inside = jnp.logical_and(lane >= half * HEAD, lane < (half + 1) * HEAD)
    return jnp.where(inside, value, 0.0).astype(BF16)


def pair_columns(pair):
    return pl.ds(pl.multiple_of(pair * PAIR, PAIR), PAIR)


def attend(q_ref, k_ref, v_ref, key_seg_ref, query_seg_ref, prob_ref, out_ref, done):
    queries = q_ref.shape[0]
    block = min(QUERY_BLOCK, queries)

    def one_pair(pair, carry):
        cols = pair_columns(pair)
        keys, values = k_ref[:, cols], v_ref[:, cols]
        for start in range(0, queries, block):
            rows = pl.ds(start, block)
            query = q_ref[rows, cols]
            allowed = key_seg_ref[...] == query_seg_ref[:, rows]
            total = None
            for half in range(2):
                scores = mm_nt(keys * head_mask(half, HEAD**-0.5), query)
                scores = jnp.where(allowed, scores, MASKED_SCORE)
                peak = jnp.max(scores, 0, keepdims=True)
                weights = jnp.exp(scores - peak)
                soft = (weights * (1.0 / jnp.sum(weights, 0, keepdims=True))).astype(BF16)
                prob_ref[pair * 2 + half, :, rows] = soft
                part = mm_tn(soft, values * head_mask(half, 1.0))
                total = part if total is None else total + part
            out_ref[rows, cols] = total.astype(BF16)
        done(pair)
        return carry

    lax.fori_loop(0, HEADS // 2, one_pair, 0)


def attend_back(q_ref, k_ref, v_ref, prob_ref, grad_ref, dq_ref, dk_ref, dv_ref, ready):
    queries = q_ref.shape[0]
    block = min(QUERY_BLOCK, queries)
    scaling = HEAD**-0.5

    def one_pair(pair, carry):
        cols = pair_columns(pair)
        keys, values = k_ref[:, cols], v_ref[:, cols]
        key_sum = value_sum = None
        ready(pair)
        for start in range(0, queries, block):
            rows = pl.ds(start, block)
            query, grad = q_ref[rows, cols], grad_ref[rows, cols]
            query_sum = None
            for half in range(2):
                mask = head_mask(half, 1.0)
                soft = prob_ref[pair * 2 + half, :, rows]
                weights = soft.astype(F32)
                grad_soft = mm_nt(values * mask, grad)
                product = weights * grad_soft
                inner = jnp.sum(product, 0, keepdims=True)
                grad_scores = (product - weights * inner).astype(BF16)
                value_part = mm(soft, grad * mask)
                key_part = mm(grad_scores, query * mask)
                query_part = mm_tn(grad_scores, keys * mask)
                value_sum = value_part if value_sum is None else value_sum + value_part
                key_sum = key_part if key_sum is None else key_sum + key_part
                query_sum = query_part if query_sum is None else query_sum + query_part
            dq_ref[rows, cols] = (query_sum * scaling).astype(BF16)
        dk_ref[:, cols] = (key_sum * scaling).astype(BF16)
        dv_ref[:, cols] = value_sum.astype(BF16)
        return carry

    lax.fori_loop(0, HEADS // 2, one_pair, 0)


def pair_copy(source, target, sems, pair):
    heads = pl.ds(pair * 2, 2)
    return pltpu.make_async_copy(source.at[heads], target.at[heads], sems.at[pair])


def reorder(core, position, bits):
    if core == 0:
        return position
    return sum(((position >> bit) & 1) << (bits - 1 - bit) for bit in range(bits))


class Layout:
    def __init__(self, dp_size, tensor_size):
        self.dp, self.tensor = dp_size, tensor_size
        self.bits = tensor_size.bit_length() - 1
        self.planes = dp_size // 2
        self.parts = tensor_size // GROUP
        self.rows = D // dp_size
        self.quad = tensor_size == 4
        self.width = D // self.parts

    def pairs(self, move):
        return [
            (d * self.tensor + t, move(d, t)) for d in range(self.dp) for t in range(self.tensor)
        ]

    def inplane(self, bit):
        return self.pairs(
            lambda d, t: d * self.tensor + (t ^ reorder(d & 1, 1 << bit, self.bits))
        )

    def inplane_position(self, position):
        return self.pairs(
            lambda d, t: d * self.tensor + (t ^ reorder(d & 1, position, self.bits))
        )

    def plain_inplane(self, offset):
        return self.pairs(lambda d, t: d * self.tensor + (t ^ offset))

    def other_core(self):
        return self.pairs(lambda d, t: (d ^ 1) * self.tensor + t)


def send(values, pairs):
    return lax.ppermute(values, AXES, pairs)


def gather_inplane(layout, piece, forwarded=None):
    pieces = [piece]
    for bit in range(layout.bits):
        if forwarded is not None and bit + 1 == layout.bits:
            pieces = pieces[:1] + [forwarded(one) for one in pieces[1:]]
        pieces = pieces + [send(one, layout.inplane(bit)) for one in pieces]
    return pieces


def gather_inplane_direct(layout, piece):
    return [piece] + [
        send(piece, layout.inplane_position(position)) for position in range(1, layout.tensor)
    ]


def exchange_planes(layout, pieces):
    groups = [list(range(core, layout.dp, 2)) for core in range(2)]
    return lax.all_to_all(pieces, "dp", 0, 0, axis_index_groups=groups, tiled=True)


def exchange_inplane(pieces):
    return lax.all_to_all(pieces, "tensor", 0, 0, tiled=True)


def swap_cores(layout, values):
    return send(values, layout.other_core())


def whole_kernel(body, out_shape, scratch=(), flops=0, moved=0, name=None, far_outs=0):
    out_specs = jax.tree.map(lambda _: pl.BlockSpec(memory_space=pltpu.VMEM), out_shape)
    shapes = out_shape
    if far_outs:
        out_specs = (pl.BlockSpec(memory_space=pltpu.HBM),) * far_outs + out_specs[far_outs:]
        shapes = tuple(pltpu.HBM(one.shape, one.dtype) for one in out_shape[:far_outs])
        shapes = shapes + out_shape[far_outs:]

    def call(*operands, far=(), after=()):
        near = len(operands)
        operands = operands + tuple(far)
        read = len(operands)

        def without_after(*refs):
            place = lax.axis_index("dp"), lax.axis_index("tensor")
            info = (place[0] % 2, place[0] // 2, place[1])
            body(info, *refs[:read], *refs[read + len(after) :])

        operands = operands[:near] + tuple(
            pltpu.with_memory_space_constraint(one, pltpu.HBM) for one in operands[near:]
        )
        return pl.pallas_call(
            without_after,
            out_shape=shapes,
            in_specs=[pl.BlockSpec(memory_space=pltpu.VMEM)] * near
            + [pl.BlockSpec(memory_space=pltpu.HBM)] * len(far)
            + [pl.BlockSpec(memory_space=pl.ANY)] * len(after),
            out_specs=out_specs,
            scratch_shapes=list(scratch),
            compiler_params=pltpu.CompilerParams(vmem_limit_bytes=VMEM_BYTES),
            cost_estimate=pl.CostEstimate(flops=flops, bytes_accessed=moved, transcendentals=0),
            name=name,
        )(*operands, *after)

    return call


class Copies:
    def __init__(self, sems):
        self.sems, self.count = sems, 0

    def start(self, source, target):
        copy = pltpu.make_async_copy(source, target, self.sems.at[self.count])
        copy.start()
        self.count += 1
        return copy


def wait_all(copies):
    for copy in copies:
        copy.wait()


def low_shape(*shape):
    return jax.ShapeDtypeStruct(shape, BF16)


def wide_shape(*shape):
    return jax.ShapeDtypeStruct(shape, F32)


UNIT = 2 * D * D * D


def owner_at(info_ref, layout, position, other=False):
    core = info_ref[0]
    first = 1 if other else 0
    offset = jnp.where(
        core == first, reorder(0, position, layout.bits), reorder(1, position, layout.bits)
    )
    return jnp.bitwise_xor(info_ref[2], offset)


def row_start(info_ref, layout, plane, other=False):
    core = 1 - info_ref[0] if other else info_ref[0]
    return pl.multiple_of((plane * 2 + core) * layout.rows, layout.rows)


def quad_matrix(info_ref, position):
    tensor = info_ref[2]
    side = jnp.bitwise_xor(lax.rem(tensor, 2), lax.div(tensor, 2))
    return jnp.bitwise_xor(side, position // 2) * 2 + position % 2


def weight_chunk(layout, group, name):
    rows, planes = layout.rows, layout.planes
    tiles = NORM_ROWS if group == 0 else 0

    def body(info_ref, norm_ref, source_ref, out_ref, tile, blocks, sems):
        copies = Copies(sems)
        moving = [
            copies.start(
                source_ref.at[group * GROUP + quad_matrix(info_ref, position)],
                blocks.at[position],
            )
            for position in range(2)
        ]
        if tiles:
            tile[...] = jnp.zeros_like(tile)
            for block in range(layout.dp):

                @pl.when(info_ref[1] * 2 + info_ref[0] == block)
                def _():
                    tile[0:6, block * rows : (block + 1) * rows] = norm_ref[...]

            for plane in range(planes):
                out_ref[plane, 2 * rows :, :] = tile[...].astype(BF16)
        wait_all(moving)
        for index in range(2):
            block = blocks[index].astype(BF16)
            for plane in range(planes):
                out_ref[plane, index * rows : (index + 1) * rows, :] = block

    return whole_kernel(
        body,
        low_shape(planes, 2 * rows + tiles, D),
        scratch=[
            pltpu.VMEM((NORM_ROWS, D), F32),
            pltpu.VMEM((2, rows, D), F32),
            pltpu.SemaphoreType.DMA((2,)),
        ],
        moved=1 << 20,
        name=name,
    )


def weight_split(layout, group, name):
    rows, planes = layout.rows, layout.planes

    def body(info_ref, all_ref, *outs):
        for plane in range(planes):
            for index in range(2):
                outs[index][plane] = all_ref[plane, index * rows : (index + 1) * rows, :]
        if group == 0:
            tile = sum(all_ref[plane, 2 * rows :, :].astype(F32) for plane in range(planes))
            outs[2][...] = tile.astype(BF16)

    one = low_shape(planes, rows, D)
    shapes = (one, one) + ((low_shape(NORM_ROWS, D),) if group == 0 else ())
    return whole_kernel(body, shapes, moved=2 << 20, name=name)


def fetch_weights(info_ref, layout, refs, weights_ref, copies):
    if not layout.quad:
        return [copies.start(refs[0], weights_ref)]
    moving = []
    for index, ref in enumerate(refs):
        matrix = quad_matrix(info_ref, index % GROUP)
        for plane in range(layout.planes):
            at = pl.ds(row_start(info_ref, layout, plane, index >= GROUP), layout.rows)
            moving.append(copies.start(ref.at[plane], weights_ref.at[matrix, at, :]))
    return moving


def weight_pieces(layout):
    return (2 * GROUP, 2 * GROUP * layout.planes) if layout.quad else (1, 1)


def place_grads(info_ref, layout, grads_ref, keep_ref, send_ref):
    for other, ref in ((False, keep_ref), (True, send_ref)):
        for position in range(layout.tensor):
            owner = owner_at(info_ref, layout, position, other)
            for slot in range(layout.planes):
                rows = pl.ds(row_start(info_ref, layout, slot, other), layout.rows)
                if layout.parts == 1:
                    block = grads_ref[owner, rows, :]
                else:
                    part = lax.rem(owner, layout.parts) * layout.width
                    cols = pl.ds(pl.multiple_of(part, layout.width), layout.width)
                    block = grads_ref[lax.div(owner, layout.parts), rows, cols]
                ref[position, slot, 0 : layout.rows, :] = block


def first_norm(tokens):
    def body(info_ref, tile_ref, other_ref, x_far, a_out, a_ref, gains_ref, x_ref, sems):
        copies = Copies(sems)
        x_copy = copies.start(x_far, x_ref)
        gains_ref[...] = tile_ref[...].astype(F32) + other_ref[...].astype(F32)
        x_copy.wait()
        normed, _ = normalized(x_ref[...].astype(F32))
        a_ref[...] = (normed * gains_ref[0:1, :] + gains_ref[1:2, :]).astype(BF16)
        copies.start(a_ref, a_out).wait()

    return whole_kernel(
        body,
        (low_shape(tokens, D), low_shape(tokens, D), wide_shape(NORM_ROWS, D)),
        scratch=[pltpu.VMEM((tokens, D), BF16), pltpu.SemaphoreType.DMA((2,))],
        moved=1 << 20,
        name="first_norm",
        far_outs=1,
    )


def self_forward(layout, tokens):
    count, pieces = weight_pieces(layout)

    def body(info_ref, a_ref, gains_ref, query_seg_ref, key_seg_ref, x_far, *refs):
        w_out, q_out, k_out, v_out, prob_out, mix_out, mid_out, c_ref = refs[count : count + 8]
        x_ref, w_ref, q_ref, k_ref, v_ref, prob_ref, mix_ref, mid_ref = refs[count + 8 : -2]
        sems, pair_sems = refs[-2:]
        copies = Copies(sems)
        arriving = fetch_weights(info_ref, layout, refs[:count], w_ref, copies)
        x_copy = copies.start(x_far, x_ref)
        wait_all(arriving)
        leaving = [copies.start(w_ref, w_out)]
        for index, (ref, out) in enumerate(((q_ref, q_out), (k_ref, k_out), (v_ref, v_out))):
            ref[...] = mm(a_ref[...], w_ref[index]).astype(BF16)
            leaving.append(copies.start(ref, out))
        attend(
            q_ref, k_ref, v_ref, key_seg_ref, query_seg_ref, prob_ref, mix_ref,
            lambda pair: pair_copy(prob_ref, prob_out, pair_sems, pair).start(),
        )
        leaving.append(copies.start(mix_ref, mix_out))
        x_copy.wait()
        mid = x_ref[...].astype(F32) + mm(mix_ref[...], w_ref[3])
        mid_ref[...] = mid
        leaving.append(copies.start(mid_ref, mid_out))
        normed, _ = normalized(mid)
        c_ref[...] = (normed * gains_ref[2:3, :] + gains_ref[3:4, :]).astype(BF16)
        wait_all(leaving)
        for pair in range(HEADS // 2):
            pair_copy(prob_ref, prob_out, pair_sems, pair).wait()

    low, rows = low_shape(tokens, D), pltpu.VMEM((tokens, D), BF16)
    probs = (HEADS, tokens, tokens)
    return whole_kernel(
        body,
        (
            low_shape(GROUP, D, D),
            low,
            low,
            low,
            low_shape(*probs),
            low,
            wide_shape(tokens, D),
            low,
        ),
        scratch=[rows, pltpu.VMEM((GROUP, D, D), BF16), rows, rows, rows]
        + [pltpu.VMEM(probs, BF16), rows, pltpu.VMEM((tokens, D), F32)]
        + [pltpu.SemaphoreType.DMA((pieces + 8,)), pltpu.SemaphoreType.DMA((HEADS // 2,))],
        flops=14 * UNIT,
        moved=12 << 20,
        name="self_forward",
        far_outs=7,
    )


def cross_forward(layout, tokens, states):
    count, pieces = weight_pieces(layout)

    def body(info_ref, c_ref, gains_ref, query_seg_ref, key_seg_ref, enc_far, mid_far, *refs):
        w_ref, q_ref, k_ref, v_ref, prob_ref, mix_ref, late_ref, f_ref = refs[count : count + 8]
        enc_ref, mid_ref, sems = refs[count + 8 :]
        copies = Copies(sems)
        arriving = fetch_weights(info_ref, layout, refs[:count], w_ref, copies)
        arriving.append(copies.start(enc_far, enc_ref))
        mid_copy = copies.start(mid_far, mid_ref)
        wait_all(arriving)
        for index, (source, ref) in enumerate(
            ((c_ref, q_ref), (enc_ref, k_ref), (enc_ref, v_ref))
        ):
            ref[...] = mm(source[...], w_ref[index]).astype(BF16)
        attend(
            q_ref, k_ref, v_ref, key_seg_ref, query_seg_ref, prob_ref, mix_ref, lambda pair: None
        )
        mid_copy.wait()
        late = mid_ref[...] + mm(mix_ref[...], w_ref[3])
        late_ref[...] = late
        normed, _ = normalized(late)
        f_ref[...] = (normed * gains_ref[4:5, :] + gains_ref[5:6, :]).astype(BF16)

    low = low_shape(tokens, D)
    return whole_kernel(
        body,
        (
            low_shape(GROUP, D, D),
            low,
            low_shape(states, D),
            low_shape(states, D),
            low_shape(HEADS, states, tokens),
            low,
            wide_shape(tokens, D),
            low,
        ),
        scratch=[pltpu.VMEM((states, D), BF16), pltpu.VMEM((tokens, D), F32)]
        + [pltpu.SemaphoreType.DMA((pieces + 2,))],
        flops=14 * UNIT,
        moved=12 << 20,
        name="cross_forward",
    )


def gelu_parts(pre):
    slope = math.sqrt(2.0 / math.pi)
    square = pre * pre
    bent = jnp.tanh(slope * pre * (1.0 + 0.044715 * square))
    half = 0.5 * (1.0 + bent)
    inner = slope * (1.0 + 3 * 0.044715 * square)
    return pre * half, half + 0.5 * pre * (1.0 - bent * bent) * inner


def feed_forward(layout, tokens, hidden):
    count, planes = layout.tensor, layout.planes
    piece_rows, full = D // planes, layout.tensor * hidden

    def body(info_ref, f_ref, cot_far, *refs):
        mine, others = refs[:count], refs[count : 2 * count]
        w_in, w_out, post_ref, d_pre_ref, keep_ref, send_ref = refs[2 * count : -5]
        cot_ref, f_t, cot_t, sems, cot_sem = refs[-5:]
        first_core = info_ref[0] == 0

        def columns(position):
            return slice(position * hidden, (position + 1) * hidden)

        def fetch(source, target, matrix, position):
            return pltpu.make_async_copy(
                source, target.at[:, columns(position)], sems.at[matrix, position]
            )

        cot_copy = pltpu.make_async_copy(cot_far, cot_ref, cot_sem)
        cot_copy.start()
        for position in range(count):
            turned = reorder(1, position, layout.bits)

            @pl.when(first_core)
            def _():
                fetch(mine[position], w_in, 0, position).start()
                fetch(others[turned], w_out, 1, position).start()

            @pl.when(jnp.logical_not(first_core))
            def _():
                fetch(others[position], w_in, 0, position).start()
                fetch(mine[turned], w_out, 1, position).start()

        f_t[...] = f_ref[...].T
        cot_copy.wait()
        cot_t[...] = cot_ref[...].T
        for position in range(count):
            cols = columns(position)
            fetch(mine[0], w_in, 0, position).wait()
            fetch(mine[0], w_out, 1, position).wait()
            pre = mm(f_ref[...], w_in[:, cols])
            grad_post = mm(cot_ref[...], w_out[:, cols])
            post, slope = gelu_parts(pre)
            post_ref[:, cols] = post.astype(BF16)
            d_pre_ref[:, cols] = (slope * grad_post).astype(BF16)
        for position in range(count):
            cols = columns(position)
            turned = reorder(1, position, layout.bits)
            keep_at = jnp.where(first_core, position, turned)
            send_at = jnp.where(first_core, turned, position)
            grad_in = mm(f_t[...], d_pre_ref[:, cols]).astype(BF16)
            grad_out = mm(cot_t[...], post_ref[:, cols]).astype(BF16)
            for slot in range(planes):
                part = slice(slot * piece_rows, (slot + 1) * piece_rows)
                keep_ref[keep_at, slot] = jnp.where(first_core, grad_in[part], grad_out[part])
                send_ref[send_at, slot] = jnp.where(first_core, grad_out[part], grad_in[part])

    pieces = low_shape(count, planes, piece_rows, hidden)
    return whole_kernel(
        body,
        (low_shape(D, full), low_shape(D, full), low_shape(tokens, full), low_shape(tokens, full))
        + (pieces, pieces),
        scratch=[
            pltpu.VMEM((tokens, D), BF16),
            pltpu.VMEM((D, tokens), BF16),
            pltpu.VMEM((D, tokens), BF16),
            pltpu.SemaphoreType.DMA((2, count)),
            pltpu.SemaphoreType.DMA,
        ],
        flops=4 * UNIT * full // D,
        moved=14 << 20,
        name="feed_forward",
    )


def feed_forward_sums(layout, tokens, hidden):
    def body(info_ref, w_in, w_out, post_ref, d_pre_ref, late_ref, gains_ref, cot_far, *refs):
        out_ref, glate_ref, dlate_ref, norm_ref, cot_ref, sem = refs
        cot_copy = pltpu.make_async_copy(cot_far, cot_ref, sem)
        cot_copy.start()
        late = late_ref[...]
        back = mm_nt(d_pre_ref[...], w_in[...])
        back, gain_grad, shift_grad = norm_backward(back, late, gains_ref[4:5, :])
        cot_copy.wait()
        grad_late = cot_ref[...].astype(F32) + back
        glate_ref[...] = grad_late
        dlate_ref[...] = grad_late.astype(BF16)
        norm_ref[0:1, :] = gain_grad
        norm_ref[1:2, :] = shift_grad
        out_ref[...] = (late + mm_nt(post_ref[...], w_out[...])).astype(BF16)

    low = low_shape(tokens, D)
    return whole_kernel(
        body,
        (low, wide_shape(tokens, D), low, wide_shape(2, D)),
        scratch=[pltpu.VMEM((tokens, D), BF16), pltpu.SemaphoreType.DMA],
        flops=2 * UNIT * layout.tensor * hidden // D,
        moved=4 << 20,
        name="feed_forward_sums",
    )


def cross_backward(layout, tokens, states):
    def body(info_ref, dlate_ref, mix_ref, glate_ref, gains_ref, *refs):
        q_ref, k_ref, v_ref, prob_ref, c_ref, w_ref, enc_far, mid_far = refs[:8]
        enc_grad_ref, gmid_ref, dmid_ref, norm_ref, keep_ref, send_ref = refs[8:14]
        enc_ref, mid_ref, dq, dk, dv, grads, d_mix, sems = refs[14:]
        copies = Copies(sems)
        later = [copies.start(enc_far, enc_ref), copies.start(mid_far, mid_ref)]
        d_mix[...] = mm_nt(dlate_ref[...], w_ref[3]).astype(BF16)
        grads[3] = mm_tn(mix_ref[...], dlate_ref[...]).astype(BF16)
        attend_back(
            q_ref, k_ref, v_ref, prob_ref, d_mix, dq, dk, dv, lambda pair: None
        )
        wait_all(later)
        grads[0] = mm_tn(c_ref[...], dq[...]).astype(BF16)
        enc_t = enc_ref[...].T
        grads[1] = mm(enc_t, dk[...]).astype(BF16)
        grads[2] = mm(enc_t, dv[...]).astype(BF16)
        place_grads(info_ref, layout, grads, keep_ref, send_ref)
        enc_grad_ref[...] = (mm_nt(dk[...], w_ref[1]) + mm_nt(dv[...], w_ref[2])).astype(BF16)
        back, gain_grad, shift_grad = norm_backward(
            mm_nt(dq[...], w_ref[0]), mid_ref[...], gains_ref[2:3, :]
        )
        grad_mid = glate_ref[...] + back
        gmid_ref[...] = grad_mid
        dmid_ref[...] = grad_mid.astype(BF16)
        norm_ref[0:1, :] = gain_grad
        norm_ref[1:2, :] = shift_grad

    low, rows = low_shape(tokens, D), pltpu.VMEM((tokens, D), BF16)
    keys = pltpu.VMEM((states, D), BF16)
    pieces = low_shape(layout.tensor, layout.planes, layout.rows, layout.width)
    return whole_kernel(
        body,
        (low_shape(states, D), wide_shape(tokens, D), low, wide_shape(2, D), pieces, pieces),
        scratch=[keys, pltpu.VMEM((tokens, D), F32), rows, keys, keys]
        + [pltpu.VMEM((GROUP, D, D), BF16), rows, pltpu.SemaphoreType.DMA((2,))],
        flops=26 * UNIT,
        moved=14 << 20,
        name="cross_backward",
    )


def self_attention_back(layout, tokens):
    def body(info_ref, dmid_ref, w_ref, mix_ref, q_ref, k_ref, v_ref, prob_ref, *refs):
        out_ref, dq, dk, dv, d_mix = refs
        d_mix[...] = mm_nt(dmid_ref[...], w_ref[3]).astype(BF16)
        attend_back(
            q_ref, k_ref, v_ref, prob_ref, d_mix, dq, dk, dv, lambda pair: None
        )
        out_ref[...] = mm_tn(mix_ref[...], dmid_ref[...]).astype(BF16)

    low = low_shape(tokens, D)
    return whole_kernel(
        body,
        (low_shape(D, D), low, low, low),
        scratch=[pltpu.VMEM((tokens, D), BF16)],
        flops=18 * UNIT,
        moved=10 << 20,
        name="self_attention_back",
    )


def self_backward(layout, tokens):
    def body(info_ref, out_grad_ref, dq, dk, dv, gmid_ref, gains_ref, *refs):
        norm_two_ref, norm_three_ref, w_far, a_far, x_far = refs[:5]
        grad_ref, keep_ref, send_ref, w_ref, a_ref, x_ref, grads, norms, tile, sems = refs[5:]
        copies = Copies(sems)
        moving = [
            copies.start(*one)
            for one in ((a_far, a_ref), (w_far.at[0:3], w_ref), (x_far, x_ref))
        ]
        grads[3] = out_grad_ref[...]
        moving[0].wait()
        a_t = a_ref[...].T
        for index, ref in enumerate((dq, dk, dv)):
            grads[index] = mm(a_t, ref[...]).astype(BF16)
        moving[1].wait()
        total = None
        for index, ref in enumerate((dq, dk, dv)):
            part = mm_nt(ref[...], w_ref[index])
            total = part if total is None else total + part
        place_grads(info_ref, layout, grads, keep_ref, send_ref)
        moving[2].wait()
        back, gain_grad, shift_grad = norm_backward(
            total, x_ref[...].astype(F32), gains_ref[0:1, :]
        )
        grad_ref[...] = (gmid_ref[...] + back).astype(BF16)
        tile[...] = jnp.zeros_like(tile)
        for index, row in enumerate((gain_grad, shift_grad)):
            norms[index : index + 1, :] = row
        norms[2:4, :] = norm_two_ref[...]
        norms[4:6, :] = norm_three_ref[...]
        for block in range(layout.dp):
            columns = slice(block * layout.rows, (block + 1) * layout.rows)
            tile[block, 0:6, 0 : layout.rows] = norms[0:6, columns].astype(BF16)
        for other, ref in ((False, keep_ref), (True, send_ref)):
            core = 1 - info_ref[0] if other else info_ref[0]
            for slot in range(layout.planes):
                block = tile[slot * 2 + core]
                for position in range(layout.tensor):
                    ref[position, slot, layout.rows :, :] = block

    low, rows = low_shape(tokens, D), pltpu.VMEM((tokens, D), BF16)
    pieces = low_shape(layout.tensor, layout.planes, layout.rows + NORM_ROWS, layout.width)
    return whole_kernel(
        body,
        (low, pieces, pieces),
        scratch=[
            pltpu.VMEM((3, D, D), BF16),
            rows,
            rows,
            pltpu.VMEM((GROUP, D, D), BF16),
            pltpu.VMEM((8, D), F32),
            pltpu.VMEM((layout.dp, NORM_ROWS, layout.width), BF16),
            pltpu.SemaphoreType.DMA((3,)),
        ],
        flops=7 * UNIT,
        moved=6 << 20,
        name="self_backward",
    )


def sweep(low_ref, rest_ref, poly_ref, width, kept):
    half = D // 2
    shift = jnp.zeros((), F32)
    for start in range(0, width, D):
        part = low_ref[:, start : start + D].astype(F32)
        shift = shift + jnp.sum(part * part)
    shift = shift * (1.0 / D)
    diagonal = lax.broadcasted_iota(jnp.int32, (half, half), 0) == lax.broadcasted_iota(
        jnp.int32, (half, half), 1
    )
    shifted = jnp.where(diagonal, shift, 0.0)
    top, bottom = slice(0, half), slice(half, D)
    upper, lower = low_ref[top, :], low_ref[bottom, :]
    rest_ref[top, top] = (mm_nt(upper, upper) - shifted).astype(BF16)
    corner = mm_nt(upper, lower).astype(BF16)
    rest_ref[top, bottom] = corner
    rest_ref[bottom, top] = corner.T
    rest_ref[bottom, bottom] = (mm_nt(lower, lower) - shifted).astype(BF16)
    slope = POLY_SECOND + 2.0 * POLY_THIRD * shift
    scale = POLY_FIRST + POLY_SECOND * shift + POLY_THIRD * shift * shift
    for rows in (top, bottom):
        square = mm(rest_ref[rows, :], rest_ref[...])
        poly = slope * rest_ref[rows, :].astype(F32) + POLY_THIRD * square
        poly_ref[rows, :] = poly.astype(BF16)
    for start in range(0, kept, D):
        cols = slice(start, min(start + D, kept))
        part = low_ref[:, cols]
        low_ref[:, cols] = (scale * part.astype(F32) + mm(poly_ref[...], part)).astype(BF16)


def sweeps(low_ref, rest_ref, poly_ref, width, kept):
    def one(step, carry):
        sweep(low_ref, rest_ref, poly_ref, width, width)
        return carry

    lax.fori_loop(0, NS_STEPS - 1, one, 0)
    sweep(low_ref, rest_ref, poly_ref, width, kept)


def orthogonalize_attention(layout):
    parts, rows, planes = layout.parts, layout.rows, layout.planes

    def body(info_ref, *refs):
        pieces = refs[: 2 * parts]
        mine_ref, other_ref, low, rest, poly = refs[2 * parts :]
        cross = info_ref[0] != 0
        for part in range(parts):
            cols = slice(part * layout.width, (part + 1) * layout.width)
            for half in range(2):
                for slot in range(planes):
                    start = (half * planes + slot) * rows
                    both = pieces[2 * part + half]
                    low[start : start + rows, cols] = jnp.where(
                        cross, both[slot, 0:rows, :], both[slot, rows : 2 * rows, :]
                    )
        values = low[...].astype(F32)
        inverse = 1.0 / (jnp.sqrt(jnp.sum(values * values)) + 1e-07)
        low[...] = (values * inverse).astype(BF16)
        sweeps(low, rest, poly, D, D)
        start = pl.multiple_of(info_ref[1] * rows, rows)
        mine_ref[...] = low[pl.ds(start, rows), 0 : layout.width]
        other_ref[...] = low[pl.ds(planes * rows + start, rows), 0 : layout.width]

    return whole_kernel(
        body,
        (low_shape(rows, layout.width), low_shape(rows, layout.width)),
        scratch=[pltpu.VMEM((D, D), BF16)] * 3,
        flops=15 * UNIT,
        moved=2 << 20,
        name="orthogonalize_attention",
    )


def orthogonalize_wide(layout, hidden):
    count = layout.tensor

    def body(info_ref, *refs):
        pieces = refs[:count]
        out_ref, low, rest, poly = refs[count:]
        total = jnp.zeros((), F32)
        for ref in pieces:
            values = ref[...].astype(F32)
            total = total + jnp.sum(values * values)
        inverse = 1.0 / (jnp.sqrt(total) + 1e-07)
        for index, ref in enumerate(pieces):
            low[:, index * hidden : (index + 1) * hidden] = (
                ref[...].astype(F32) * inverse
            ).astype(BF16)
        sweeps(low, rest, poly, count * hidden, hidden)
        out_ref[...] = low[:, 0:hidden]

    return whole_kernel(
        body,
        low_shape(D, hidden),
        scratch=[pltpu.VMEM((D, count * hidden), BF16)] + [pltpu.VMEM((D, D), BF16)] * 2,
        flops=45 * UNIT,
        moved=3 << 20,
        name="orthogonalize_wide",
    )


def wide_shard(hidden):
    def body(info_ref, expand_far, contract_far, out_ref, block, sem):
        @pl.when(info_ref[0] == 0)
        def _():
            copy = pltpu.make_async_copy(expand_far, block.at[:, 0:hidden], sem)
            copy.start()
            copy.wait()
            out_ref[...] = block[:, 0:hidden].astype(BF16)

        @pl.when(info_ref[0] != 0)
        def _():
            copy = pltpu.make_async_copy(contract_far, block.at[0:hidden, :], sem)
            copy.start()
            copy.wait()
            out_ref[...] = block[0:hidden, :].T.astype(BF16)

    return whole_kernel(
        body,
        low_shape(D, hidden),
        scratch=[pltpu.VMEM((D, D), F32), pltpu.SemaphoreType.DMA],
        moved=3 << 20,
        name="wide_shard",
    )


def fence(values, after):
    def body(source_ref, *refs):
        pass

    return pl.pallas_call(
        body,
        out_shape=jax.ShapeDtypeStruct(values.shape, values.dtype),
        in_specs=[pl.BlockSpec(memory_space=pl.ANY)] * (1 + len(after)),
        out_specs=pl.BlockSpec(memory_space=pl.ANY),
        input_output_aliases={0: 0},
        name="fence",
    )(values, *after)


def halves_sum(layout, kept, got, name, after=()):
    half = kept.shape[0] // 2

    def body(info_ref, kept_ref, got_ref, upper_ref, lower_ref):
        for position in range(half):
            for ref, at in ((upper_ref, half + position), (lower_ref, position)):
                ref[position] = (kept_ref[at].astype(F32) + got_ref[at].astype(F32)).astype(BF16)

    part = low_shape(half, *kept.shape[1:])
    return whole_kernel(body, (part, part), moved=4 * kept.size, name=name)(
        kept, got, after=after
    )


def nest_of(grad, momentum):
    return (1.0 + MOMENTUM_DECAY) * grad + MOMENTUM_DECAY * MOMENTUM_DECAY * momentum


def wide_nest(layout, hidden):
    count = layout.planes

    def body(info_ref, got_ref, momentum_ref, out_ref):
        total = sum(got_ref[plane].astype(F32) for plane in range(count))
        nest = nest_of(total, momentum_ref[...]).astype(BF16)
        for plane in range(count):
            out_ref[plane] = nest

    return whole_kernel(
        body, low_shape(count, D // count, hidden), moved=1 << 20, name="wide_nest"
    )


def wide_slots_sum(layout, hidden):
    def body(info_ref, kept_ref, got_ref, out_ref):
        out_ref[...] = (kept_ref[0].astype(F32) + got_ref[0].astype(F32)).astype(BF16)

    shape = low_shape(layout.planes, D // layout.planes, hidden)
    return whole_kernel(body, shape, moved=1 << 20, name="wide_slots_sum")


def attention_slots(layout):
    rows, planes, width = layout.rows, layout.planes, layout.width

    def body(info_ref, cross_ref, cross_got, self_ref, self_got, out_ref):
        for slot in range(planes):
            for start, kept, got in ((0, cross_ref, cross_got), (rows, self_ref, self_got)):
                total = kept[0, slot].astype(F32) + got[0, slot].astype(F32)
                out_ref[slot, start : start + total.shape[0], :] = total.astype(BF16)

    return whole_kernel(
        body,
        low_shape(planes, 2 * rows + NORM_ROWS, width),
        moved=2 << 20,
        name="attention_slots",
    )


def attention_nest(layout):
    rows, planes, width = layout.rows, layout.planes, layout.width

    def body(info_ref, got_ref, momentum_ref, nest_ref, grad_ref, norm_ref):
        total = sum(got_ref[plane].astype(F32) for plane in range(planes))
        tensor = info_ref[2]
        cols = slice(None)
        if layout.parts > 1:
            part = lax.rem(tensor, layout.parts) * width
            cols = pl.ds(pl.multiple_of(part, width), width)
        for index, group in enumerate((1, 0)):
            here = slice(index * rows, (index + 1) * rows)
            momentum = momentum_ref[group * GROUP + lax.div(tensor, layout.parts), :, cols]
            nest = nest_of(total[here], momentum).astype(BF16)
            for plane in range(planes):
                nest_ref[plane, here, :] = nest
        grad_ref[...] = total[0 : 2 * rows].astype(BF16)
        norm_ref[...] = total[2 * rows : 2 * rows + 8]

    return whole_kernel(
        body,
        (
            low_shape(planes, 2 * rows, width),
            low_shape(2 * rows, width),
            wide_shape(8, width),
        ),
        moved=2 << 20,
        name="attention_nest",
    )


def wide_momentum(layout, hidden):
    piece_rows = D // layout.planes

    def body(info_ref, expand_ref, contract_ref, out_ref, turned):
        rows = pl.ds(pl.multiple_of(info_ref[1] * piece_rows, piece_rows), piece_rows)
        turned[...] = contract_ref[...].T
        out_ref[...] = jnp.where(info_ref[0] == 0, expand_ref[rows, :], turned[rows, :])

    return whole_kernel(
        body,
        wide_shape(piece_rows, hidden),
        scratch=[pltpu.VMEM((D, hidden), F32)],
        moved=3 << 20,
        name="wide_momentum",
    )


def decayed(master, share, scale):
    return master - MUON_RATE * (MUON_DECAY * master + scale * share)


def finish_wide(layout, hidden, full_hidden):
    scale = 0.2 * math.sqrt(max(D, full_hidden))

    def body(info_ref, mine_ref, other_ref, expand_ref, contract_ref, *refs):
        e_new, e_low, c_new, c_low = refs
        first = info_ref[0] == 0
        mine, other = mine_ref[...], other_ref[...]
        new = decayed(expand_ref[...], jnp.where(first, mine, other).astype(F32), scale)
        e_new[...] = new
        e_low[...] = new.astype(BF16)
        new = decayed(contract_ref[...], jnp.where(first, other, mine).T.astype(F32), scale)
        c_new[...] = new
        c_low[...] = new.astype(BF16)

    return whole_kernel(
        body,
        (wide_shape(D, hidden), low_shape(D, hidden), wide_shape(hidden, D), low_shape(hidden, D)),
        moved=6 << 20,
        name="finish_wide",
    )


def wide_velocity(layout, hidden):
    grad_share = 1.0 / (1.0 + MOMENTUM_DECAY)
    momentum_share = MOMENTUM_DECAY - MOMENTUM_DECAY * MOMENTUM_DECAY * grad_share

    def body(info_ref, mine_ref, other_ref, expand_ref, contract_ref, e_new, c_new):
        first = info_ref[0] == 0
        mine, other = mine_ref[...], other_ref[...]
        nest = jnp.where(first, mine, other).astype(F32)
        e_new[...] = momentum_share * expand_ref[...] + grad_share * nest
        nest = jnp.where(first, other, mine).T.astype(F32)
        c_new[...] = momentum_share * contract_ref[...] + grad_share * nest

    return whole_kernel(
        body,
        (wide_shape(D, hidden), wide_shape(hidden, D)),
        moved=6 << 20,
        name="wide_velocity",
    )


def finish_attention(layout):
    count = layout.tensor
    scale = 0.2 * math.sqrt(D)

    def body(info_ref, *refs):
        late, early = refs[:count], refs[count : 2 * count]
        master_ref, momentum_ref, new_ref, velocity_ref, low_ref = refs[2 * count :]
        rows = layout.rows
        for position in range(count):
            owner = owner_at(info_ref, layout, position)
            cols = slice(None)
            if layout.parts > 1:
                part = lax.rem(owner, layout.parts) * layout.width
                cols = pl.ds(pl.multiple_of(part, layout.width), layout.width)
            for group in range(2):
                index = group * GROUP + lax.div(owner, layout.parts)
                at = info_ref[0] if group == 0 else 1 - info_ref[0]
                share = late[position][at].astype(F32)
                new = decayed(master_ref[index, :, cols], share, scale)
                new_ref[index, :, cols] = new
                low_ref[index, :, cols] = new.astype(BF16)
                start = (1 - group) * rows
                grad = early[position][start : start + rows, :].astype(F32)
                velocity_ref[index, :, cols] = (
                    MOMENTUM_DECAY * momentum_ref[index, :, cols] + grad
                )

    shape = (2 * GROUP, layout.rows, D)
    return whole_kernel(
        body,
        (wide_shape(*shape), wide_shape(*shape), low_shape(*shape)),
        moved=6 << 20,
        name="finish_attention",
    )


def device_program(layout, arguments):
    (
        inputs,
        encoder,
        dec_segments,
        enc_segments,
        cotangent,
        attn_master,
        attn_momentum,
        expand_master,
        expand_momentum,
        contract_master,
        contract_momentum,
        norm_params,
        first_moments,
        second_moments,
    ) = arguments
    tokens, states = inputs.shape[1], encoder.shape[1]
    hidden = expand_master.shape[1]
    full_hidden = hidden * layout.tensor
    dp_at, tensor_at = lax.axis_index("dp"), lax.axis_index("tensor")
    x, enc, cot = inputs[0], encoder[0], cotangent[0]

    if layout.quad:
        chunk = weight_chunk(layout, 0, "self_chunk")(norm_params, far=[attn_master])
        slots = exchange_planes(layout, chunk)
        shard = wide_shard(hidden)(far=[expand_master, contract_master], after=[chunk])
        near, far = send(shard, layout.inplane(0)), send(shard, layout.inplane(1))
        cross_chunk = weight_chunk(layout, 1, "cross_chunk")(
            norm_params, far=[attn_master], after=[chunk]
        )
        first, second, tile = weight_split(layout, 0, "self_split")(slots, after=[cross_chunk])
        cross_first, cross_second = weight_split(layout, 1, "cross_split")(
            exchange_planes(layout, cross_chunk)
        )
        wide_own = [shard, near, far]
        wide_other = [swap_cores(layout, piece) for piece in wide_own]
        got_first = send(first, layout.plain_inplane(1))
        got_second = send(second, layout.plain_inplane(2))
        tiles = [tile, swap_cores(layout, tile)]
        a_saved, a, gains = first_norm(tokens)(*tiles, far=[x])
        got_first, got_second = fence(got_first, [a]), fence(got_second, [a])
        self_own = [first, second, got_first, got_second]
        self_pieces = self_own + [swap_cores(layout, piece) for piece in self_own]
        wide_own[1] = fence(near, [got_first])
        farthest = send(wide_own[1], layout.inplane(1))
        before = wide_other + [cross_first]
    else:
        low = attn_master.astype(BF16)
        norm_low = lax.all_gather(norm_params.astype(BF16), "dp", axis=1, tiled=True)
        padded = jnp.concatenate([norm_low, jnp.zeros((NORM_ROWS - 6, D), BF16)])
        self_low = lax.all_gather(low[:GROUP], "dp", axis=1, tiled=True)
        cross_low = lax.all_gather(low[GROUP:], "dp", axis=1, tiled=True)
        self_pieces, before = [self_low], []
        tiles = [padded, jnp.zeros_like(padded)]
        shard = wide_shard(hidden)(far=[expand_master, contract_master])
        wide_own = gather_inplane(layout, shard)
        wide_other = [swap_cores(layout, piece) for piece in wide_own]

    dec_row, dec_column = dec_segments.reshape(1, tokens), dec_segments.reshape(tokens, 1)
    enc_column = enc_segments.reshape(states, 1)
    if not layout.quad:
        a_saved, a, gains = first_norm(tokens)(*tiles, far=[x])
    w_self, q, k, v, self_prob, self_mix, mid, c = self_forward(layout, tokens)(
        a, gains, dec_row, dec_column, far=[x, *self_pieces], after=before
    )
    if layout.quad:
        cross_own = [
            cross_first,
            cross_second,
            send(cross_first, layout.plain_inplane(1)),
            send(cross_second, layout.plain_inplane(2)),
        ]
        cross_own = [fence(piece, [c, farthest]) for piece in cross_own]
        cross_pieces = cross_own + [swap_cores(layout, piece) for piece in cross_own]
        wide_own = wide_own + [fence(farthest, [cross_own[0]])]
        wide_other = wide_other + [swap_cores(layout, wide_own[3])]
    else:
        cross_pieces = [cross_low]
    w_cross, qc, kc, vc, cross_prob, cross_mix, late, f = cross_forward(layout, tokens, states)(
        c, gains, dec_row, enc_column, far=[enc, mid, *cross_pieces], after=[wide_own[-1]]
    )
    w_in, w_out, post, d_pre, wide_keep, wide_send = feed_forward(layout, tokens, hidden)(
        f, far=[cot, *wide_own, *wide_other]
    )
    output, grad_late, late_low, norm_three = feed_forward_sums(layout, tokens, hidden)(
        w_in, w_out, post, d_pre, late, gains, far=[cot]
    )
    top = layout.bits - 1
    upper, lower = halves_sum(
        layout, wide_keep, swap_cores(layout, wide_send), "wide_sum", after=[late_low]
    )
    encoder_grad, grad_mid, mid_low, norm_two, cross_keep, cross_send = cross_backward(
        layout, tokens, states
    )(
        late_low, cross_mix, grad_late, gains, qc, kc, vc, cross_prob, c, w_cross,
        far=[enc, mid], after=[upper],
    )
    got = send(upper, layout.inplane(top))
    for bit in reversed(range(top)):
        upper, lower = halves_sum(layout, lower, got, "wide_sum", after=[mid_low])
        got = send(upper, layout.inplane(bit))
    self_out_grad, dq, dk, dv = self_attention_back(layout, tokens)(
        mid_low, w_self, self_mix, q, k, v, self_prob, after=[upper]
    )
    input_grad, self_keep, self_send = self_backward(layout, tokens)(
        self_out_grad, dq, dk, dv, grad_mid, gains, norm_two, norm_three,
        far=[w_self, a_saved, x],
    )
    wide_slots = wide_slots_sum(layout, hidden)(lower, got, after=[self_keep])
    wide_got = exchange_planes(layout, wide_slots)
    self_upper, self_lower = halves_sum(
        layout, self_keep, swap_cores(layout, fence(self_send, [wide_slots])), "self_sum"
    )
    cross_upper, cross_lower = halves_sum(
        layout, cross_keep, swap_cores(layout, cross_send), "cross_sum", after=[wide_slots]
    )
    got_cross = send(cross_upper, layout.inplane(top))
    momentum = wide_momentum(layout, hidden)(expand_momentum, contract_momentum)
    got_self = send(self_upper, layout.inplane(top))
    for bit in reversed(range(top)):
        cross_upper, cross_lower = halves_sum(layout, cross_lower, got_cross, "cross_sum")
        got_cross = send(cross_upper, layout.inplane(bit))
    nest_rows = wide_nest(layout, hidden)(wide_got, momentum, after=[self_upper, cross_upper])
    nest = exchange_planes(layout, nest_rows).reshape(D, hidden)
    for bit in reversed(range(top)):
        self_upper, self_lower = halves_sum(layout, self_lower, got_self, "self_sum")
        got_self = send(self_upper, layout.inplane(bit))
    rows_by_slot = attention_slots(layout)(cross_lower, got_cross, self_lower, got_self)
    nest_pieces = gather_inplane(layout, nest, lambda piece: fence(piece, [rows_by_slot]))
    attn_nest, attn_grad, norm_rows = attention_nest(layout)(
        exchange_planes(layout, rows_by_slot), attn_momentum, after=[nest_pieces[layout.tensor // 2 - 1]]
    )
    nest_other = swap_cores(layout, nest)

    early = gather_inplane_direct(layout, attn_grad)

    def whole_pieces(halves):
        shared = layout.parts.bit_length() - 1
        gathered = [halves]
        for bit in range(shared):
            pairs = layout.pairs(lambda d, t: d * layout.tensor + (t ^ (1 << bit)))
            gathered = gathered + [[send(half, pairs) for half in one] for one in gathered]
        return [half for one in gathered for half in one]

    wide_ortho = orthogonalize_wide(layout, hidden)(*nest_pieces, after=[attn_nest])
    half = fence(exchange_planes(layout, attn_nest), [wide_ortho, *early[1:]])
    mine, others = orthogonalize_attention(layout)(
        *whole_pieces([half, swap_cores(layout, half)])
    )
    late_pieces = gather_inplane_direct(layout, jnp.stack([mine, swap_cores(layout, others)]))
    attn_updated, attn_velocity, attn_copy = finish_attention(layout)(
        *late_pieces, *early, attn_master, attn_momentum
    )

    expand_updated, expand_copy, contract_updated, contract_copy = finish_wide(
        layout, hidden, full_hidden
    )(wide_ortho, swap_cores(layout, wide_ortho), expand_master, contract_master)
    expand_velocity, contract_velocity = wide_velocity(layout, hidden)(
        nest, nest_other, expand_momentum, contract_momentum
    )

    norm_rows = norm_rows[0:6, 0 : layout.rows].astype(F32)
    first_updated = BETA_FIRST * first_moments + (1.0 - BETA_FIRST) * norm_rows
    second_updated = BETA_SECOND * second_moments + (1.0 - BETA_SECOND) * norm_rows * norm_rows
    corrected = first_updated / (1.0 - BETA_FIRST**STEP)
    denominator = jnp.sqrt(second_updated / (1.0 - BETA_SECOND**STEP)) + ADAM_EPSILON
    norm_updated = norm_params - ADAM_RATE * corrected / denominator
    return (
        output[None],
        input_grad[None],
        encoder_grad[None],
        attn_updated,
        attn_velocity,
        attn_copy,
        expand_updated,
        expand_velocity,
        expand_copy,
        contract_updated,
        contract_velocity,
        contract_copy,
        norm_updated,
        first_updated,
        second_updated,
    )


def solution(mesh):
    layout = Layout(mesh.shape["dp"], mesh.shape["tensor"])

    def local(*arguments):
        return device_program(layout, arguments)

    rows = P(AXES, None, None)
    by_dp, by_column, by_row, norm = P(None, "dp", None), P(None, "tensor"), P("tensor", None), P(None, "dp")
    return jax.shard_map(
        local,
        mesh=mesh,
        in_specs=(rows, rows, P(AXES, None), P(AXES, None), rows)
        + (by_dp, by_dp, by_column, by_column, by_row, by_row, norm, norm, norm),
        out_specs=(rows, rows, rows, by_dp, by_dp, by_dp)
        + (by_column, by_column, by_column, by_row, by_row, by_row, norm, norm, norm),
        check_vma=False,
    )
```

```python
import functools
import math

import jax
import jax.numpy as jnp
from jax import lax
from jax.experimental import pallas as pl
from jax.experimental.pallas import tpu as pltpu
from jax.sharding import PartitionSpec as P

D = 512
HEADS = 8
HEAD = D // HEADS
PAIR = 2 * HEAD
NS_STEPS = 5
GRAM_STEPS = 3
STEP = 10

MASKED_SCORE = -1e30
NORM_EPSILON = 1e-05
MOMENTUM_DECAY = 0.95
MUON_RATE = 0.15
MUON_DECAY = 0.01
POLY_FIRST = 3.4445
POLY_SECOND = -4.775
POLY_THIRD = 2.0315
ADAM_RATE = 0.4
BETA_FIRST = 0.9
BETA_SECOND = 0.999
ADAM_EPSILON = 1e-08
GROUP = 4
QUERY_BLOCK = 512

F32 = jnp.float32
BF16 = jnp.bfloat16
AXES = ("dp", "tensor")
MIB = 1 << 20
VMEM_BYTES = 24 * MIB
NORM_ROWS = 16


def mm(left, right):
    return lax.dot_general(left, right, (((1,), (0,)), ((), ())), preferred_element_type=F32)


def mm_nt(left, right):
    return lax.dot_general(left, right, (((1,), (1,)), ((), ())), preferred_element_type=F32)


def mm_tn(left, right):
    return lax.dot_general(left, right, (((0,), (0,)), ((), ())), preferred_element_type=F32)


def normalized(values):
    average = jnp.mean(values, -1, keepdims=True)
    centred = values - average
    inv_std = lax.rsqrt(jnp.mean(centred * centred, -1, keepdims=True) + NORM_EPSILON)
    return centred * inv_std, inv_std


def norm_backward(incoming, values, gain_row):
    normed, inv_std = normalized(values)
    scaled = incoming * gain_row
    inner = (
        scaled
        - jnp.mean(scaled, -1, keepdims=True)
        - normed * jnp.mean(scaled * normed, -1, keepdims=True)
    )
    gain_grad = jnp.sum(incoming * normed, 0, keepdims=True)
    shift_grad = jnp.sum(incoming, 0, keepdims=True)
    return inner * inv_std, gain_grad, shift_grad


def head_mask(half, value):
    lane = lax.broadcasted_iota(jnp.int32, (1, PAIR), 1)
    inside = jnp.logical_and(lane >= half * HEAD, lane < (half + 1) * HEAD)
    return jnp.where(inside, value, 0.0).astype(BF16)


def pair_columns(pair):
    return pl.ds(pl.multiple_of(pair * PAIR, PAIR), PAIR)


def attend(q_ref, k_ref, v_ref, key_seg_ref, query_seg_ref, prob_ref, out_ref, done):
    queries = q_ref.shape[0]
    block = min(QUERY_BLOCK, queries)

    def one_pair(pair, carry):
        cols = pair_columns(pair)
        keys, values = k_ref[:, cols], v_ref[:, cols]
        for start in range(0, queries, block):
            rows = pl.ds(start, block)
            query = q_ref[rows, cols]
            allowed = key_seg_ref[...] == query_seg_ref[:, rows]
            total = None
            for half in range(2):
                scores = mm_nt(keys * head_mask(half, HEAD**-0.5), query)
                scores = jnp.where(allowed, scores, MASKED_SCORE)
                peak = jnp.max(scores, 0, keepdims=True)
                weights = jnp.exp(scores - peak)
                soft = (weights * (1.0 / jnp.sum(weights, 0, keepdims=True))).astype(BF16)
                prob_ref[pair * 2 + half, :, rows] = soft
                part = mm_tn(soft, values * head_mask(half, 1.0))
                total = part if total is None else total + part
            out_ref[rows, cols] = total.astype(BF16)
        done(pair)
        return carry

    lax.fori_loop(0, HEADS // 2, one_pair, 0)


def attend_back(q_ref, k_ref, v_ref, prob_ref, grad_ref, dq_ref, dk_ref, dv_ref, ready):
    queries = q_ref.shape[0]
    block = min(QUERY_BLOCK, queries)
    scaling = HEAD**-0.5

    def one_pair(pair, carry):
        cols = pair_columns(pair)
        keys, values = k_ref[:, cols], v_ref[:, cols]
        key_sum = value_sum = None
        ready(pair)
        for start in range(0, queries, block):
            rows = pl.ds(start, block)
            query, grad = q_ref[rows, cols], grad_ref[rows, cols]
            query_sum = None
            for half in range(2):
                mask = head_mask(half, 1.0)
                soft = prob_ref[pair * 2 + half, :, rows]
                weights = soft.astype(F32)
                grad_soft = mm_nt(values * mask, grad)
                product = weights * grad_soft
                inner = jnp.sum(product, 0, keepdims=True)
                grad_scores = (product - weights * inner).astype(BF16)
                value_part = mm(soft, grad * mask)
                key_part = mm(grad_scores, query * mask)
                query_part = mm_tn(grad_scores, keys * mask)
                value_sum = value_part if value_sum is None else value_sum + value_part
                key_sum = key_part if key_sum is None else key_sum + key_part
                query_sum = query_part if query_sum is None else query_sum + query_part
            dq_ref[rows, cols] = (query_sum * scaling).astype(BF16)
        dk_ref[:, cols] = (key_sum * scaling).astype(BF16)
        dv_ref[:, cols] = value_sum.astype(BF16)
        return carry

    lax.fori_loop(0, HEADS // 2, one_pair, 0)


def pair_copy(source, target, sems, pair):
    heads = pl.ds(pair * 2, 2)
    return pltpu.make_async_copy(source.at[heads], target.at[heads], sems.at[pair])


def reorder(core, position, bits):
    if core == 0:
        return position
    return sum(((position >> bit) & 1) << (bits - 1 - bit) for bit in range(bits))


class Layout:
    def __init__(self, dp_size, tensor_size):
        self.dp, self.tensor = dp_size, tensor_size
        self.bits = tensor_size.bit_length() - 1
        self.planes = dp_size // 2
        self.parts = tensor_size // GROUP
        self.rows = D // dp_size
        self.quad = tensor_size == 4
        self.width = D // self.parts

    def pairs(self, move):
        return [
            (d * self.tensor + t, move(d, t)) for d in range(self.dp) for t in range(self.tensor)
        ]

    def inplane(self, bit):
        return self.pairs(
            lambda d, t: d * self.tensor + (t ^ reorder(d & 1, 1 << bit, self.bits))
        )

    def inplane_position(self, position):
        return self.pairs(
            lambda d, t: d * self.tensor + (t ^ reorder(d & 1, position, self.bits))
        )

    def plain_inplane(self, offset):
        return self.pairs(lambda d, t: d * self.tensor + (t ^ offset))

    def plane(self, slot):
        return self.pairs(lambda d, t: (d ^ (2 * slot)) * self.tensor + t)

    def other_core(self):
        return self.pairs(lambda d, t: (d ^ 1) * self.tensor + t)


def send(values, pairs):
    return lax.ppermute(values, AXES, pairs)


def gather_inplane(layout, piece, forwarded=None):
    pieces = [piece]
    for bit in range(layout.bits):
        if forwarded is not None and bit + 1 == layout.bits:
            pieces = pieces[:1] + [forwarded(one) for one in pieces[1:]]
        pieces = pieces + [send(one, layout.inplane(bit)) for one in pieces]
    return pieces


def gather_inplane_direct(layout, piece):
    return [piece] + [
        send(piece, layout.inplane_position(position)) for position in range(1, layout.tensor)
    ]


def send_planes(layout, piece):
    return [piece] + [send(piece, layout.plane(slot)) for slot in range(1, layout.planes)]


def exchange_planes(layout, pieces):
    groups = [list(range(core, layout.dp, 2)) for core in range(2)]
    return lax.all_to_all(pieces, "dp", 0, 0, axis_index_groups=groups, tiled=True)


def exchange_inplane(pieces):
    return lax.all_to_all(pieces, "tensor", 0, 0, tiled=True)


def swap_cores(layout, values):
    return send(values, layout.other_core())


def whole_kernel(body, out_shape, scratch=(), flops=0, moved=0, name=None, far_outs=0):
    out_specs = jax.tree.map(lambda _: pl.BlockSpec(memory_space=pltpu.VMEM), out_shape)
    shapes = out_shape
    if far_outs:
        out_specs = (pl.BlockSpec(memory_space=pltpu.HBM),) * far_outs + out_specs[far_outs:]
        shapes = tuple(pltpu.HBM(one.shape, one.dtype) for one in out_shape[:far_outs])
        shapes = shapes + out_shape[far_outs:]

    def call(*operands, far=(), after=()):
        near = len(operands)
        operands = operands + tuple(far)
        read = len(operands)

        def without_after(*refs):
            place = lax.axis_index("dp"), lax.axis_index("tensor")
            info = (place[0] % 2, place[0] // 2, place[1])
            body(info, *refs[:read], *refs[read + len(after) :])

        operands = operands[:near] + tuple(
            pltpu.with_memory_space_constraint(one, pltpu.HBM) for one in operands[near:]
        )
        return pl.pallas_call(
            without_after,
            out_shape=shapes,
            in_specs=[pl.BlockSpec(memory_space=pltpu.VMEM)] * near
            + [pl.BlockSpec(memory_space=pltpu.HBM)] * len(far)
            + [pl.BlockSpec(memory_space=pl.ANY)] * len(after),
            out_specs=out_specs,
            scratch_shapes=list(scratch),
            compiler_params=pltpu.CompilerParams(vmem_limit_bytes=VMEM_BYTES),
            cost_estimate=pl.CostEstimate(flops=flops, bytes_accessed=moved, transcendentals=0),
            name=name,
        )(*operands, *after)

    return call


class Copies:
    def __init__(self, sems):
        self.sems, self.count = sems, 0

    def start(self, source, target):
        copy = pltpu.make_async_copy(source, target, self.sems.at[self.count])
        copy.start()
        self.count += 1
        return copy


def wait_all(copies):
    for copy in copies:
        copy.wait()


def low_shape(*shape):
    return jax.ShapeDtypeStruct(shape, BF16)


def wide_shape(*shape):
    return jax.ShapeDtypeStruct(shape, F32)


UNIT = 2 * D * D * D


def owner_at(info_ref, layout, position, other=False):
    core = info_ref[0]
    first = 1 if other else 0
    offset = jnp.where(
        core == first, reorder(0, position, layout.bits), reorder(1, position, layout.bits)
    )
    return jnp.bitwise_xor(info_ref[2], offset)


def row_start(info_ref, layout, plane, other=False):
    core = 1 - info_ref[0] if other else info_ref[0]
    return pl.multiple_of((plane * 2 + core) * layout.rows, layout.rows)


def quad_matrix(info_ref, position):
    tensor = info_ref[2]
    side = jnp.bitwise_xor(lax.rem(tensor, 2), lax.div(tensor, 2))
    return jnp.bitwise_xor(side, position // 2) * 2 + position % 2


def weight_chunk(layout, group, name, copies_out):
    rows = layout.rows
    tiles = NORM_ROWS if group == 0 else 0

    def body(info_ref, norm_ref, source_ref, out_ref, tile, blocks, sems):
        copies = Copies(sems)
        moving = [
            copies.start(
                source_ref.at[group * GROUP + quad_matrix(info_ref, position)],
                blocks.at[position],
            )
            for position in range(2)
        ]
        if tiles:
            tile[...] = jnp.zeros_like(tile)
            for block in range(layout.dp):

                @pl.when(info_ref[1] * 2 + info_ref[0] == block)
                def _():
                    tile[0:6, block * rows : (block + 1) * rows] = norm_ref[...]

            for plane in range(copies_out):
                out_ref[plane, 2 * rows :, :] = tile[...].astype(BF16)
        wait_all(moving)
        for index in range(2):
            block = blocks[index].astype(BF16)
            for plane in range(copies_out):
                out_ref[plane, index * rows : (index + 1) * rows, :] = block

    return whole_kernel(
        body,
        low_shape(copies_out, 2 * rows + tiles, D),
        scratch=[
            pltpu.VMEM((NORM_ROWS, D), F32),
            pltpu.VMEM((2, rows, D), F32),
            pltpu.SemaphoreType.DMA((2,)),
        ],
        moved=1 << 20,
        name=name,
    )


def self_split(layout):
    rows, planes = layout.rows, layout.planes

    def body(info_ref, *refs):
        slots, outs, tile_ref = refs[:planes], refs[planes : planes + 2], refs[-1]
        tile = None
        for slot, ref in enumerate(slots):
            plane = jnp.bitwise_xor(info_ref[1], slot)
            for index in range(2):
                outs[index][plane] = ref[0, index * rows : (index + 1) * rows, :]
            part = ref[0, 2 * rows :, :].astype(F32)
            tile = part if tile is None else tile + part
        tile_ref[...] = tile.astype(BF16)

    one = low_shape(planes, rows, D)
    return whole_kernel(
        body, (one, one, low_shape(NORM_ROWS, D)), moved=2 << 20, name="self_split"
    )


def cross_rows(layout):
    rows, planes = layout.rows, layout.planes

    def body(info_ref, source_far, out_ref, blocks, sem):
        copy = pltpu.make_async_copy(source_far.at[GROUP : 2 * GROUP], blocks, sem)
        copy.start()
        copy.wait()
        for matrix in range(GROUP):
            block = blocks[matrix].astype(BF16)
            for plane in range(planes):
                out_ref[plane, matrix * rows : (matrix + 1) * rows, :] = block

    return whole_kernel(
        body,
        low_shape(planes, GROUP * rows, D),
        scratch=[pltpu.VMEM((GROUP, rows, D), F32), pltpu.SemaphoreType.DMA],
        moved=2 << 20,
        name="cross_rows",
    )


def fetch_weights(info_ref, layout, refs, weights_ref, copies):
    if not layout.quad:
        return [copies.start(refs[0], weights_ref)]
    moving = []
    for index, ref in enumerate(refs):
        matrix = quad_matrix(info_ref, index % GROUP)
        for plane in range(layout.planes):
            at = pl.ds(row_start(info_ref, layout, plane, index >= GROUP), layout.rows)
            moving.append(copies.start(ref.at[plane], weights_ref.at[matrix, at, :]))
    return moving


def fetch_cross(info_ref, layout, refs, weights_ref, copies):
    if not layout.quad:
        return [copies.start(refs[0], weights_ref)]
    moving, rows = [], layout.rows
    for index, ref in enumerate(refs):
        for plane in range(layout.planes):
            at = pl.ds(row_start(info_ref, layout, plane, index == 1), rows)
            for matrix in range(GROUP):
                here = slice(matrix * rows, (matrix + 1) * rows)
                moving.append(
                    copies.start(ref.at[plane, here, :], weights_ref.at[matrix, at, :])
                )
    return moving


def weight_pieces(layout):
    return (2 * GROUP, 2 * GROUP * layout.planes) if layout.quad else (1, 1)


def place_grads(info_ref, layout, grads_ref, keep_ref, send_ref):
    for other, ref in ((False, keep_ref), (True, send_ref)):
        for position in range(layout.tensor):
            owner = owner_at(info_ref, layout, position, other)
            for slot in range(layout.planes):
                rows = pl.ds(row_start(info_ref, layout, slot, other), layout.rows)
                if layout.parts == 1:
                    block = grads_ref[owner, rows, :]
                else:
                    part = lax.rem(owner, layout.parts) * layout.width
                    cols = pl.ds(pl.multiple_of(part, layout.width), layout.width)
                    block = grads_ref[lax.div(owner, layout.parts), rows, cols]
                ref[position, slot, 0 : layout.rows, :] = block


def first_norm(tokens):
    def body(info_ref, tile_ref, other_ref, x_far, a_out, a_ref, gains_ref, x_ref, sems):
        copies = Copies(sems)
        x_copy = copies.start(x_far, x_ref)
        gains_ref[...] = tile_ref[...].astype(F32) + other_ref[...].astype(F32)
        x_copy.wait()
        normed, _ = normalized(x_ref[...].astype(F32))
        a_ref[...] = (normed * gains_ref[0:1, :] + gains_ref[1:2, :]).astype(BF16)
        copies.start(a_ref, a_out).wait()

    return whole_kernel(
        body,
        (low_shape(tokens, D), low_shape(tokens, D), wide_shape(NORM_ROWS, D)),
        scratch=[pltpu.VMEM((tokens, D), BF16), pltpu.SemaphoreType.DMA((2,))],
        moved=1 << 20,
        name="first_norm",
        far_outs=1,
    )


def self_forward(layout, tokens):
    count, pieces = weight_pieces(layout)

    def body(info_ref, a_ref, gains_ref, query_seg_ref, key_seg_ref, x_far, *refs):
        w_out, q_out, k_out, v_out, prob_out, mix_out, mid_out, c_ref = refs[count : count + 8]
        x_ref, w_ref, q_ref, k_ref, v_ref, prob_ref, mix_ref, mid_ref = refs[count + 8 : -2]
        sems, pair_sems = refs[-2:]
        copies = Copies(sems)
        arriving = fetch_weights(info_ref, layout, refs[:count], w_ref, copies)
        x_copy = copies.start(x_far, x_ref)
        wait_all(arriving)
        leaving = [copies.start(w_ref, w_out)]
        for index, (ref, out) in enumerate(((q_ref, q_out), (k_ref, k_out), (v_ref, v_out))):
            ref[...] = mm(a_ref[...], w_ref[index]).astype(BF16)
            leaving.append(copies.start(ref, out))
        attend(
            q_ref, k_ref, v_ref, key_seg_ref, query_seg_ref, prob_ref, mix_ref,
            lambda pair: pair_copy(prob_ref, prob_out, pair_sems, pair).start(),
        )
        leaving.append(copies.start(mix_ref, mix_out))
        x_copy.wait()
        mid = x_ref[...].astype(F32) + mm(mix_ref[...], w_ref[3])
        mid_ref[...] = mid
        leaving.append(copies.start(mid_ref, mid_out))
        normed, _ = normalized(mid)
        c_ref[...] = (normed * gains_ref[2:3, :] + gains_ref[3:4, :]).astype(BF16)
        wait_all(leaving)
        for pair in range(HEADS // 2):
            pair_copy(prob_ref, prob_out, pair_sems, pair).wait()

    low, rows = low_shape(tokens, D), pltpu.VMEM((tokens, D), BF16)
    probs = (HEADS, tokens, tokens)
    return whole_kernel(
        body,
        (
            low_shape(GROUP, D, D),
            low,
            low,
            low,
            low_shape(*probs),
            low,
            wide_shape(tokens, D),
            low,
        ),
        scratch=[rows, pltpu.VMEM((GROUP, D, D), BF16), rows, rows, rows]
        + [pltpu.VMEM(probs, BF16), rows, pltpu.VMEM((tokens, D), F32)]
        + [pltpu.SemaphoreType.DMA((pieces + 8,)), pltpu.SemaphoreType.DMA((HEADS // 2,))],
        flops=14 * UNIT,
        moved=12 << 20,
        name="self_forward",
        far_outs=7,
    )


def cross_forward(layout, tokens, states):
    count, pieces = (2, weight_pieces(layout)[1]) if layout.quad else (1, 1)

    def body(info_ref, c_ref, gains_ref, query_seg_ref, key_seg_ref, enc_far, mid_far, *refs):
        w_ref, q_ref, k_ref, v_ref, prob_ref, mix_ref, late_ref, f_ref = refs[count : count + 8]
        enc_ref, mid_ref, sems = refs[count + 8 :]
        copies = Copies(sems)
        arriving = fetch_cross(info_ref, layout, refs[:count], w_ref, copies)
        arriving.append(copies.start(enc_far, enc_ref))
        mid_copy = copies.start(mid_far, mid_ref)
        wait_all(arriving)
        for index, (source, ref) in enumerate(
            ((c_ref, q_ref), (enc_ref, k_ref), (enc_ref, v_ref))
        ):
            ref[...] = mm(source[...], w_ref[index]).astype(BF16)
        attend(
            q_ref, k_ref, v_ref, key_seg_ref, query_seg_ref, prob_ref, mix_ref, lambda pair: None
        )
        mid_copy.wait()
        late = mid_ref[...] + mm(mix_ref[...], w_ref[3])
        late_ref[...] = late
        normed, _ = normalized(late)
        f_ref[...] = (normed * gains_ref[4:5, :] + gains_ref[5:6, :]).astype(BF16)

    low = low_shape(tokens, D)
    return whole_kernel(
        body,
        (
            low_shape(GROUP, D, D),
            low,
            low_shape(states, D),
            low_shape(states, D),
            low_shape(HEADS, states, tokens),
            low,
            wide_shape(tokens, D),
            low,
        ),
        scratch=[pltpu.VMEM((states, D), BF16), pltpu.VMEM((tokens, D), F32)]
        + [pltpu.SemaphoreType.DMA((pieces + 2,))],
        flops=14 * UNIT,
        moved=12 << 20,
        name="cross_forward",
    )


def gelu_parts(pre):
    slope = math.sqrt(2.0 / math.pi)
    square = pre * pre
    bent = jnp.tanh(slope * pre * (1.0 + 0.044715 * square))
    half = 0.5 * (1.0 + bent)
    inner = slope * (1.0 + 3 * 0.044715 * square)
    return pre * half, half + 0.5 * pre * (1.0 - bent * bent) * inner


def feed_forward(layout, tokens, hidden):
    count, planes = layout.tensor, layout.planes
    piece_rows, full = D // planes, layout.tensor * hidden

    def body(info_ref, f_ref, cot_far, *refs):
        mine, others = refs[:count], refs[count : 2 * count]
        w_in, w_out, post_ref, d_pre_ref, keep_ref, send_ref = refs[2 * count : -5]
        cot_ref, f_t, cot_t, sems, cot_sem = refs[-5:]
        first_core = info_ref[0] == 0

        def columns(position):
            return slice(position * hidden, (position + 1) * hidden)

        def fetch(source, target, matrix, position):
            return pltpu.make_async_copy(
                source, target.at[:, columns(position)], sems.at[matrix, position]
            )

        cot_copy = pltpu.make_async_copy(cot_far, cot_ref, cot_sem)
        cot_copy.start()
        for position in range(count):
            turned = reorder(1, position, layout.bits)

            @pl.when(first_core)
            def _():
                fetch(mine[position], w_in, 0, position).start()
                fetch(others[turned], w_out, 1, position).start()

            @pl.when(jnp.logical_not(first_core))
            def _():
                fetch(others[position], w_in, 0, position).start()
                fetch(mine[turned], w_out, 1, position).start()

        f_t[...] = f_ref[...].T
        cot_copy.wait()
        cot_t[...] = cot_ref[...].T
        for position in range(count):
            cols = columns(position)
            fetch(mine[0], w_in, 0, position).wait()
            fetch(mine[0], w_out, 1, position).wait()
            pre = mm(f_ref[...], w_in[:, cols])
            grad_post = mm(cot_ref[...], w_out[:, cols])
            post, slope = gelu_parts(pre)
            post_ref[:, cols] = post.astype(BF16)
            d_pre_ref[:, cols] = (slope * grad_post).astype(BF16)
        for position in range(count):
            cols = columns(position)
            turned = reorder(1, position, layout.bits)
            keep_at = jnp.where(first_core, position, turned)
            send_at = jnp.where(first_core, turned, position)
            grad_in = mm(f_t[...], d_pre_ref[:, cols]).astype(BF16)
            grad_out = mm(cot_t[...], post_ref[:, cols]).astype(BF16)
            for slot in range(planes):
                part = slice(slot * piece_rows, (slot + 1) * piece_rows)
                keep_ref[keep_at, slot] = jnp.where(first_core, grad_in[part], grad_out[part])
                send_ref[send_at, slot] = jnp.where(first_core, grad_out[part], grad_in[part])

    pieces = low_shape(count, planes, piece_rows, hidden)
    return whole_kernel(
        body,
        (low_shape(D, full), low_shape(D, full), low_shape(tokens, full), low_shape(tokens, full))
        + (pieces, pieces),
        scratch=[
            pltpu.VMEM((tokens, D), BF16),
            pltpu.VMEM((D, tokens), BF16),
            pltpu.VMEM((D, tokens), BF16),
            pltpu.SemaphoreType.DMA((2, count)),
            pltpu.SemaphoreType.DMA,
        ],
        flops=4 * UNIT * full // D,
        moved=14 << 20,
        name="feed_forward",
    )


def feed_forward_sums(layout, tokens, hidden):
    def body(info_ref, w_in, w_out, post_ref, d_pre_ref, late_ref, gains_ref, cot_far, *refs):
        out_ref, glate_ref, dlate_ref, norm_ref, cot_ref, sem = refs
        cot_copy = pltpu.make_async_copy(cot_far, cot_ref, sem)
        cot_copy.start()
        late = late_ref[...]
        back = mm_nt(d_pre_ref[...], w_in[...])
        back, gain_grad, shift_grad = norm_backward(back, late, gains_ref[4:5, :])
        cot_copy.wait()
        grad_late = cot_ref[...].astype(F32) + back
        glate_ref[...] = grad_late
        dlate_ref[...] = grad_late.astype(BF16)
        norm_ref[0:1, :] = gain_grad
        norm_ref[1:2, :] = shift_grad
        out_ref[...] = (late + mm_nt(post_ref[...], w_out[...])).astype(BF16)

    low = low_shape(tokens, D)
    return whole_kernel(
        body,
        (low, wide_shape(tokens, D), low, wide_shape(2, D)),
        scratch=[pltpu.VMEM((tokens, D), BF16), pltpu.SemaphoreType.DMA],
        flops=2 * UNIT * layout.tensor * hidden // D,
        moved=4 << 20,
        name="feed_forward_sums",
    )


def cross_backward(layout, tokens, states):
    def body(info_ref, dlate_ref, mix_ref, glate_ref, gains_ref, *refs):
        q_ref, k_ref, v_ref, prob_ref, c_ref, w_ref, enc_far, mid_far = refs[:8]
        enc_grad_ref, gmid_ref, dmid_ref, norm_ref, keep_ref, send_ref = refs[8:14]
        enc_ref, mid_ref, dq, dk, dv, grads, d_mix, sems = refs[14:]
        copies = Copies(sems)
        later = [copies.start(enc_far, enc_ref), copies.start(mid_far, mid_ref)]
        d_mix[...] = mm_nt(dlate_ref[...], w_ref[3]).astype(BF16)
        grads[3] = mm_tn(mix_ref[...], dlate_ref[...]).astype(BF16)
        attend_back(
            q_ref, k_ref, v_ref, prob_ref, d_mix, dq, dk, dv, lambda pair: None
        )
        wait_all(later)
        grads[0] = mm_tn(c_ref[...], dq[...]).astype(BF16)
        enc_t = enc_ref[...].T
        grads[1] = mm(enc_t, dk[...]).astype(BF16)
        grads[2] = mm(enc_t, dv[...]).astype(BF16)
        place_grads(info_ref, layout, grads, keep_ref, send_ref)
        enc_grad_ref[...] = (mm_nt(dk[...], w_ref[1]) + mm_nt(dv[...], w_ref[2])).astype(BF16)
        back, gain_grad, shift_grad = norm_backward(
            mm_nt(dq[...], w_ref[0]), mid_ref[...], gains_ref[2:3, :]
        )
        grad_mid = glate_ref[...] + back
        gmid_ref[...] = grad_mid
        dmid_ref[...] = grad_mid.astype(BF16)
        norm_ref[0:1, :] = gain_grad
        norm_ref[1:2, :] = shift_grad

    low, rows = low_shape(tokens, D), pltpu.VMEM((tokens, D), BF16)
    keys = pltpu.VMEM((states, D), BF16)
    pieces = low_shape(layout.tensor, layout.planes, layout.rows, layout.width)
    return whole_kernel(
        body,
        (low_shape(states, D), wide_shape(tokens, D), low, wide_shape(2, D), pieces, pieces),
        scratch=[keys, pltpu.VMEM((tokens, D), F32), rows, keys, keys]
        + [pltpu.VMEM((GROUP, D, D), BF16), rows, pltpu.SemaphoreType.DMA((2,))],
        flops=26 * UNIT,
        moved=14 << 20,
        name="cross_backward",
    )


def self_attention_back(layout, tokens):
    def body(info_ref, dmid_ref, w_ref, mix_ref, q_ref, k_ref, v_ref, prob_ref, *refs):
        out_ref, dq, dk, dv, d_mix = refs
        d_mix[...] = mm_nt(dmid_ref[...], w_ref[3]).astype(BF16)
        attend_back(
            q_ref, k_ref, v_ref, prob_ref, d_mix, dq, dk, dv, lambda pair: None
        )
        out_ref[...] = mm_tn(mix_ref[...], dmid_ref[...]).astype(BF16)

    low = low_shape(tokens, D)
    return whole_kernel(
        body,
        (low_shape(D, D), low, low, low),
        scratch=[pltpu.VMEM((tokens, D), BF16)],
        flops=18 * UNIT,
        moved=10 << 20,
        name="self_attention_back",
    )


def self_backward(layout, tokens):
    def body(info_ref, out_grad_ref, dq, dk, dv, gmid_ref, gains_ref, *refs):
        norm_two_ref, norm_three_ref, w_far, a_far, x_far = refs[:5]
        grad_ref, keep_ref, send_ref, w_ref, a_ref, x_ref, grads, norms, tile, sems = refs[5:]
        copies = Copies(sems)
        moving = [
            copies.start(*one)
            for one in ((a_far, a_ref), (w_far.at[0:3], w_ref), (x_far, x_ref))
        ]
        grads[3] = out_grad_ref[...]
        moving[0].wait()
        a_t = a_ref[...].T
        for index, ref in enumerate((dq, dk, dv)):
            grads[index] = mm(a_t, ref[...]).astype(BF16)
        moving[1].wait()
        total = None
        for index, ref in enumerate((dq, dk, dv)):
            part = mm_nt(ref[...], w_ref[index])
            total = part if total is None else total + part
        place_grads(info_ref, layout, grads, keep_ref, send_ref)
        moving[2].wait()
        back, gain_grad, shift_grad = norm_backward(
            total, x_ref[...].astype(F32), gains_ref[0:1, :]
        )
        grad_ref[...] = (gmid_ref[...] + back).astype(BF16)
        tile[...] = jnp.zeros_like(tile)
        for index, row in enumerate((gain_grad, shift_grad)):
            norms[index : index + 1, :] = row
        norms[2:4, :] = norm_two_ref[...]
        norms[4:6, :] = norm_three_ref[...]
        for block in range(layout.dp):
            columns = slice(block * layout.rows, (block + 1) * layout.rows)
            tile[block, 0:6, 0 : layout.rows] = norms[0:6, columns].astype(BF16)
        for other, ref in ((False, keep_ref), (True, send_ref)):
            core = 1 - info_ref[0] if other else info_ref[0]
            for slot in range(layout.planes):
                block = tile[slot * 2 + core]
                for position in range(layout.tensor):
                    ref[position, slot, layout.rows :, :] = block

    low, rows = low_shape(tokens, D), pltpu.VMEM((tokens, D), BF16)
    pieces = low_shape(layout.tensor, layout.planes, layout.rows + NORM_ROWS, layout.width)
    return whole_kernel(
        body,
        (low, pieces, pieces),
        scratch=[
            pltpu.VMEM((3, D, D), BF16),
            rows,
            rows,
            pltpu.VMEM((GROUP, D, D), BF16),
            pltpu.VMEM((8, D), F32),
            pltpu.VMEM((layout.dp, NORM_ROWS, layout.width), BF16),
            pltpu.SemaphoreType.DMA((3,)),
        ],
        flops=7 * UNIT,
        moved=6 << 20,
        name="self_backward",
    )


def gram_rest(low_ref, rest_ref, ratio, shift):
    half = D // 2
    diagonal = lax.broadcasted_iota(jnp.int32, (half, half), 0) == lax.broadcasted_iota(
        jnp.int32, (half, half), 1
    )
    shifted = jnp.where(diagonal, shift, 0.0)
    top, bottom = slice(0, half), slice(half, D)
    upper, lower = low_ref[top, :], low_ref[bottom, :]
    rest_ref[top, top] = (ratio * mm_nt(upper, upper) - shifted).astype(BF16)
    corner = (ratio * mm_nt(upper, lower)).astype(BF16)
    rest_ref[top, bottom] = corner
    rest_ref[bottom, top] = corner.T
    rest_ref[bottom, bottom] = (ratio * mm_nt(lower, lower) - shifted).astype(BF16)


def apply_factor(low_ref, poly_ref, scale, kept):
    for start in range(0, kept, D):
        cols = slice(start, min(start + D, kept))
        part = low_ref[:, cols]
        low_ref[:, cols] = (scale * part.astype(F32) + mm(poly_ref[...], part)).astype(BF16)


def sweep(low_ref, rest_ref, poly_ref, width, kept, first=False):
    shift = jnp.zeros((), F32)
    for start in range(0, width, D):
        part = low_ref[:, start : start + D].astype(F32)
        shift = shift + jnp.sum(part * part)
    inverse = 1.0 / (jnp.sqrt(shift) + 1e-07) if first else 1.0
    shift = shift * (inverse * inverse * (1.0 / D))
    gram_rest(low_ref, rest_ref, inverse * inverse, shift)
    slope = POLY_SECOND + 2.0 * POLY_THIRD * shift
    scale = POLY_FIRST + POLY_SECOND * shift + POLY_THIRD * shift * shift
    half = D // 2
    for rows in (slice(0, half), slice(half, D)):
        square = mm(rest_ref[rows, :], rest_ref[...])
        poly = slope * rest_ref[rows, :].astype(F32) + POLY_THIRD * square
        poly_ref[rows, :] = (inverse * poly).astype(BF16)
    apply_factor(low_ref, poly_ref, inverse * scale, kept)


def orthogonalize_attention(layout):
    parts, rows, planes = layout.parts, layout.rows, layout.planes

    def body(info_ref, *refs):
        pieces = refs[: 2 * parts]
        mine_ref, other_ref, low, rest, poly, sems = refs[2 * parts :]
        copies, moving = Copies(sems), []
        first = pl.multiple_of((1 - info_ref[0]) * rows, rows)
        for part in range(parts):
            cols = slice(part * layout.width, (part + 1) * layout.width)
            for half in range(2):
                for slot in range(planes):
                    start = (half * planes + slot) * rows
                    moving.append(
                        copies.start(
                            pieces[2 * part + half].at[slot, pl.ds(first, rows), :],
                            low.at[start : start + rows, cols],
                        )
                    )
        wait_all(moving)
        sweep(low, rest, poly, D, D, first=True)

        def one(step, carry):
            sweep(low, rest, poly, D, D)
            return carry

        lax.fori_loop(1, NS_STEPS, one, 0)
        start = pl.multiple_of(info_ref[1] * rows, rows)
        mine_ref[...] = low[pl.ds(start, rows), 0 : layout.width]
        other_ref[...] = low[pl.ds(planes * rows + start, rows), 0 : layout.width]

    return whole_kernel(
        body,
        (low_shape(rows, layout.width), low_shape(rows, layout.width)),
        scratch=[pltpu.VMEM((D, D), BF16)] * 3
        + [pltpu.SemaphoreType.DMA((2 * parts * planes,))],
        flops=15 * UNIT,
        moved=2 << 20,
        name="orthogonalize_attention",
    )


def gram_sweeps(rest_ref, poly_ref, square_ref, sum_ref, shift):
    diagonal = lax.broadcasted_iota(jnp.int32, (D, D), 0) == lax.broadcasted_iota(
        jnp.int32, (D, D), 1
    )
    scale = None
    for step in range(GRAM_STEPS):
        rest = rest_ref[...]
        slope = POLY_SECOND + 2.0 * POLY_THIRD * shift
        here = POLY_FIRST + POLY_SECOND * shift + POLY_THIRD * shift * shift
        poly = slope * rest.astype(F32) + POLY_THIRD * mm(rest, rest)
        poly_ref[...] = poly.astype(BF16)
        low = poly_ref[...]
        if scale is None:
            scale = here
            sum_ref[...] = poly
        else:
            before = sum_ref[...]
            sum_ref[...] = here * before + scale * poly + mm(low, before.astype(BF16))
            scale = scale * here
        if step + 1 < GRAM_STEPS:
            square = 2.0 * here * poly + mm(low, low)
            square_ref[...] = square.astype(BF16)
            twice = here * here
            rest = twice * rest.astype(F32) + shift * square + mm(square_ref[...], rest)
            more = jnp.sum(jnp.where(diagonal, rest, 0.0)) * (1.0 / D)
            rest_ref[...] = jnp.where(diagonal, rest - more, rest).astype(BF16)
            shift = twice * shift + more
    return scale


def orthogonalize_wide(layout, hidden):
    count = layout.tensor
    width = count * hidden

    def body(info_ref, *refs):
        pieces = refs[:count]
        out_ref, low, rest, poly, square, total_ref, sem = refs[count:]
        total = jnp.zeros((), F32)
        own = pltpu.make_async_copy(pieces[-1], low.at[:, 0:hidden], sem)
        own.start()
        for index in reversed(range(count)):
            cols = slice(index * hidden, (index + 1) * hidden)
            if index == 0:
                own.wait()
                part = low[:, cols]
            else:
                part = pieces[index - 1][...]
                low[:, cols] = part
            values = part.astype(F32)
            total = total + jnp.sum(values * values)
        inverse = 1.0 / (jnp.sqrt(total) + 1e-07)
        ratio = inverse * inverse
        shift = total * ratio * (1.0 / D)
        gram_rest(low, rest, ratio, shift)
        scale = gram_sweeps(rest, poly, square, total_ref, shift)
        poly[...] = (inverse * total_ref[...]).astype(BF16)
        apply_factor(low, poly, inverse * scale, width)
        for step in range(GRAM_STEPS, NS_STEPS):
            sweep(low, rest, poly, width, width if step + 1 < NS_STEPS else hidden)
        out_ref[...] = low[:, 0:hidden]

    return whole_kernel(
        body,
        low_shape(D, hidden),
        scratch=[pltpu.VMEM((D, width), BF16)]
        + [pltpu.VMEM((D, D), BF16)] * 3
        + [pltpu.VMEM((D, D), F32), pltpu.SemaphoreType.DMA],
        flops=30 * UNIT,
        moved=3 << 20,
        name="orthogonalize_wide",
    )


def wide_shard(hidden):
    def body(info_ref, expand_far, contract_far, out_ref, block, sem):
        @pl.when(info_ref[0] == 0)
        def _():
            copy = pltpu.make_async_copy(expand_far, block.at[:, 0:hidden], sem)
            copy.start()
            copy.wait()
            out_ref[...] = block[:, 0:hidden].astype(BF16)

        @pl.when(info_ref[0] != 0)
        def _():
            copy = pltpu.make_async_copy(contract_far, block.at[0:hidden, :], sem)
            copy.start()
            copy.wait()
            out_ref[...] = block[0:hidden, :].T.astype(BF16)

    return whole_kernel(
        body,
        low_shape(D, hidden),
        scratch=[pltpu.VMEM((D, D), F32), pltpu.SemaphoreType.DMA],
        moved=3 << 20,
        name="wide_shard",
    )


def fence(values, after):
    def body(source_ref, *refs):
        pass

    return pl.pallas_call(
        body,
        out_shape=jax.ShapeDtypeStruct(values.shape, values.dtype),
        in_specs=[pl.BlockSpec(memory_space=pl.ANY)] * (1 + len(after)),
        out_specs=pl.BlockSpec(memory_space=pl.ANY),
        input_output_aliases={0: 0},
        name="fence",
    )(values, *after)


def halves_sum(layout, kept, got, name, after=()):
    half = kept.shape[0] // 2

    def body(info_ref, kept_ref, got_ref, upper_ref, lower_ref):
        for position in range(half):
            for ref, at in ((upper_ref, half + position), (lower_ref, position)):
                ref[position] = (kept_ref[at].astype(F32) + got_ref[at].astype(F32)).astype(BF16)

    part = low_shape(half, *kept.shape[1:])
    return whole_kernel(body, (part, part), moved=4 * kept.size, name=name)(
        kept, got, after=after
    )


def nest_of(grad, momentum):
    return (1.0 + MOMENTUM_DECAY) * grad + MOMENTUM_DECAY * MOMENTUM_DECAY * momentum


def wide_nest(layout, hidden):
    count = layout.planes

    def body(info_ref, got_ref, momentum_ref, out_ref):
        total = sum(got_ref[plane].astype(F32) for plane in range(count))
        nest = nest_of(total, momentum_ref[...]).astype(BF16)
        for plane in range(count):
            out_ref[plane] = nest

    return whole_kernel(
        body, low_shape(count, D // count, hidden), moved=1 << 20, name="wide_nest"
    )


def wide_slots_sum(layout, hidden):
    def body(info_ref, kept_ref, got_ref, out_ref):
        out_ref[...] = (kept_ref[0].astype(F32) + got_ref[0].astype(F32)).astype(BF16)

    shape = low_shape(layout.planes, D // layout.planes, hidden)
    return whole_kernel(body, shape, moved=1 << 20, name="wide_slots_sum")


def attention_slots(layout):
    rows, planes, width = layout.rows, layout.planes, layout.width

    def body(info_ref, cross_ref, cross_got, self_ref, self_got, out_ref):
        for slot in range(planes):
            for start, kept, got in ((0, cross_ref, cross_got), (rows, self_ref, self_got)):
                total = kept[0, slot].astype(F32) + got[0, slot].astype(F32)
                out_ref[slot, start : start + total.shape[0], :] = total.astype(BF16)

    return whole_kernel(
        body,
        low_shape(planes, 2 * rows + NORM_ROWS, width),
        moved=2 << 20,
        name="attention_slots",
    )


def attention_nest(layout):
    rows, planes, width = layout.rows, layout.planes, layout.width

    def body(info_ref, got_ref, momentum_far, nest_ref, grad_ref, norm_ref, momentum, sems):
        tensor, copies = info_ref[2], Copies(sems)
        cols = slice(None)
        if layout.parts > 1:
            part = lax.rem(tensor, layout.parts) * width
            cols = pl.ds(pl.multiple_of(part, width), width)
        moving = [
            copies.start(
                momentum_far.at[group * GROUP + lax.div(tensor, layout.parts), :, cols],
                momentum.at[index],
            )
            for index, group in enumerate((1, 0))
        ]
        total = sum(got_ref[plane].astype(F32) for plane in range(planes))
        wait_all(moving)
        for index in range(2):
            here = slice(index * rows, (index + 1) * rows)
            nest = nest_of(total[here], momentum[index]).astype(BF16)
            for plane in range(planes):
                nest_ref[plane, here, :] = nest
        grad_ref[...] = total[0 : 2 * rows].astype(BF16)
        norm_ref[...] = total[2 * rows : 2 * rows + 8]

    return whole_kernel(
        body,
        (
            low_shape(planes, 2 * rows, width),
            low_shape(2 * rows, width),
            wide_shape(8, width),
        ),
        scratch=[pltpu.VMEM((2, rows, width), F32), pltpu.SemaphoreType.DMA((2,))],
        moved=2 << 20,
        name="attention_nest",
    )


def wide_momentum(layout, hidden):
    piece_rows = D // layout.planes

    def body(info_ref, expand_ref, contract_ref, out_ref, turned):
        rows = pl.ds(pl.multiple_of(info_ref[1] * piece_rows, piece_rows), piece_rows)
        turned[...] = contract_ref[...].T
        out_ref[...] = jnp.where(info_ref[0] == 0, expand_ref[rows, :], turned[rows, :])

    return whole_kernel(
        body,
        wide_shape(piece_rows, hidden),
        scratch=[pltpu.VMEM((D, hidden), F32)],
        moved=3 << 20,
        name="wide_momentum",
    )


def decayed(master, share, scale):
    return master - MUON_RATE * (MUON_DECAY * master + scale * share)


def finish_wide(layout, hidden, full_hidden):
    scale = 0.2 * math.sqrt(max(D, full_hidden))

    def body(info_ref, mine_ref, other_ref, expand_ref, contract_ref, *refs):
        e_new, e_low, c_new, c_low = refs
        first = info_ref[0] == 0
        mine, other = mine_ref[...], other_ref[...]
        new = decayed(expand_ref[...], jnp.where(first, mine, other).astype(F32), scale)
        e_new[...] = new
        e_low[...] = new.astype(BF16)
        new = decayed(contract_ref[...], jnp.where(first, other, mine).T.astype(F32), scale)
        c_new[...] = new
        c_low[...] = new.astype(BF16)

    return whole_kernel(
        body,
        (wide_shape(D, hidden), low_shape(D, hidden), wide_shape(hidden, D), low_shape(hidden, D)),
        moved=6 << 20,
        name="finish_wide",
    )


def wide_velocity(layout, hidden):
    grad_share = 1.0 / (1.0 + MOMENTUM_DECAY)
    momentum_share = MOMENTUM_DECAY - MOMENTUM_DECAY * MOMENTUM_DECAY * grad_share

    def body(info_ref, mine_ref, other_ref, expand_ref, contract_ref, e_new, c_new, token):
        token[...] = jnp.zeros_like(token)
        first = info_ref[0] == 0
        mine, other = mine_ref[...], other_ref[...]
        nest = jnp.where(first, mine, other).astype(F32)
        e_new[...] = momentum_share * expand_ref[...] + grad_share * nest
        nest = jnp.where(first, other, mine).T.astype(F32)
        c_new[...] = momentum_share * contract_ref[...] + grad_share * nest

    return whole_kernel(
        body,
        (wide_shape(D, hidden), wide_shape(hidden, D), wide_shape(8, 128)),
        moved=6 << 20,
        name="wide_velocity",
    )


def owner_columns(info_ref, layout, position, other=False):
    owner = owner_at(info_ref, layout, position, other)
    if layout.parts == 1:
        return owner, slice(None)
    part = lax.rem(owner, layout.parts) * layout.width
    return lax.div(owner, layout.parts), pl.ds(pl.multiple_of(part, layout.width), layout.width)


def attention_velocity(layout):
    count, rows = layout.tensor, layout.rows

    def body(info_ref, *refs):
        momentum_ref, velocity_ref = refs[count:]
        for position in range(count):
            matrix, cols = owner_columns(info_ref, layout, position)
            for group in range(2):
                index, start = group * GROUP + matrix, (1 - group) * rows
                grad = refs[position][start : start + rows, :].astype(F32)
                velocity_ref[index, :, cols] = (
                    MOMENTUM_DECAY * momentum_ref[index, :, cols] + grad
                )

    return whole_kernel(
        body, wide_shape(2 * GROUP, rows, D), moved=3 << 20, name="attention_velocity"
    )


def finish_attention(layout):
    count = layout.tensor
    scale = 0.2 * math.sqrt(D)

    def body(info_ref, *refs):
        late = refs[:count]
        master_ref, new_ref, low_ref = refs[count:]
        for position in range(count):
            matrix, cols = owner_columns(info_ref, layout, position)
            for group in range(2):
                index = group * GROUP + matrix
                at = info_ref[0] if group == 0 else 1 - info_ref[0]
                new = decayed(
                    master_ref[index, :, cols], late[position][at].astype(F32), scale
                )
                new_ref[index, :, cols] = new
                low_ref[index, :, cols] = new.astype(BF16)

    shape = (2 * GROUP, layout.rows, D)
    return whole_kernel(
        body, (wide_shape(*shape), low_shape(*shape)), moved=4 << 20, name="finish_attention"
    )


def finish_norms(layout):
    def body(info_ref, grad_ref, params_ref, first_ref, second_ref, new, first_new, second_new):
        grad = grad_ref[0:6, 0 : layout.rows]
        first = BETA_FIRST * first_ref[...] + (1.0 - BETA_FIRST) * grad
        second = BETA_SECOND * second_ref[...] + (1.0 - BETA_SECOND) * grad * grad
        corrected = first / (1.0 - BETA_FIRST**STEP)
        denominator = jnp.sqrt(second / (1.0 - BETA_SECOND**STEP)) + ADAM_EPSILON
        new[...] = params_ref[...] - ADAM_RATE * corrected / denominator
        first_new[...] = first
        second_new[...] = second

    return whole_kernel(body, (wide_shape(6, layout.rows),) * 3, moved=1 << 14, name="norms")


def device_program(layout, arguments):
    (
        inputs,
        encoder,
        dec_segments,
        enc_segments,
        cotangent,
        attn_master,
        attn_momentum,
        expand_master,
        expand_momentum,
        contract_master,
        contract_momentum,
        norm_params,
        first_moments,
        second_moments,
    ) = arguments
    tokens, states = inputs.shape[1], encoder.shape[1]
    hidden = expand_master.shape[1]
    full_hidden = hidden * layout.tensor
    dp_at, tensor_at = lax.axis_index("dp"), lax.axis_index("tensor")
    x, enc, cot = inputs[0], encoder[0], cotangent[0]

    if layout.quad:
        chunk = weight_chunk(layout, 0, "self_chunk", 1)(norm_params, far=[attn_master])
        cross_own = cross_rows(layout)(far=[attn_master], after=[chunk])
        shard = wide_shard(hidden)(far=[expand_master, contract_master], after=[cross_own])
        near = send(shard, layout.inplane(0))
        first, second, tile = self_split(layout)(*send_planes(layout, chunk), after=[near])
        cross_own = exchange_planes(layout, fence(cross_own, [tile]))
        got_first = send(first, layout.plain_inplane(1))
        got_second = send(second, layout.plain_inplane(2))
        tiles = [tile, swap_cores(layout, tile)]
        a_saved, a, gains = first_norm(tokens)(*tiles, far=[x])
        got_first, got_second = fence(got_first, [a]), fence(got_second, [a])
        self_own = [first, second, got_first, got_second]
        self_pieces = self_own + [swap_cores(layout, piece) for piece in self_own]
        near = fence(near, [got_first])
        far = send(fence(shard, [got_first]), layout.inplane(1))
        farthest = send(near, layout.inplane(1))
        before = []
    else:
        low = attn_master.astype(BF16)
        norm_low = lax.all_gather(norm_params.astype(BF16), "dp", axis=1, tiled=True)
        padded = jnp.concatenate([norm_low, jnp.zeros((NORM_ROWS - 6, D), BF16)])
        self_low = lax.all_gather(low[:GROUP], "dp", axis=1, tiled=True)
        cross_low = lax.all_gather(low[GROUP:], "dp", axis=1, tiled=True)
        self_pieces, before = [self_low], []
        tiles = [padded, jnp.zeros_like(padded)]
        shard = wide_shard(hidden)(far=[expand_master, contract_master])
        wide_own = gather_inplane(layout, shard)
        wide_other = [swap_cores(layout, piece) for piece in wide_own]

    dec_row, dec_column = dec_segments.reshape(1, tokens), dec_segments.reshape(tokens, 1)
    enc_column = enc_segments.reshape(states, 1)
    if not layout.quad:
        a_saved, a, gains = first_norm(tokens)(*tiles, far=[x])
    w_self, q, k, v, self_prob, self_mix, mid, c = self_forward(layout, tokens)(
        a, gains, dec_row, dec_column, far=[x, *self_pieces], after=before
    )
    if layout.quad:
        far, farthest = fence(far, [c]), fence(farthest, [c])
        cross_own = fence(cross_own, [far, farthest])
        cross_pieces = [cross_own, swap_cores(layout, cross_own)]
        wide_own = [shard, near, far, farthest]
        wide_other = [swap_cores(layout, piece) for piece in wide_own]
    else:
        cross_pieces = [cross_low]
    w_cross, qc, kc, vc, cross_prob, cross_mix, late, f = cross_forward(layout, tokens, states)(
        c, gains, dec_row, enc_column, far=[enc, mid, *cross_pieces], after=[wide_own[-1]]
    )
    w_in, w_out, post, d_pre, wide_keep, wide_send = feed_forward(layout, tokens, hidden)(
        f, far=[cot, *wide_own, *wide_other]
    )
    output, grad_late, late_low, norm_three = feed_forward_sums(layout, tokens, hidden)(
        w_in, w_out, post, d_pre, late, gains, far=[cot]
    )
    top = layout.bits - 1
    upper, lower = halves_sum(
        layout, wide_keep, swap_cores(layout, wide_send), "wide_sum", after=[late_low]
    )
    encoder_grad, grad_mid, mid_low, norm_two, cross_keep, cross_send = cross_backward(
        layout, tokens, states
    )(
        late_low, cross_mix, grad_late, gains, qc, kc, vc, cross_prob, c, w_cross,
        far=[enc, mid], after=[upper],
    )
    got = send(upper, layout.inplane(top))
    for bit in reversed(range(top)):
        upper, lower = halves_sum(layout, lower, got, "wide_sum", after=[mid_low])
        got = send(upper, layout.inplane(bit))
    cross_upper, cross_lower = halves_sum(
        layout, cross_keep, swap_cores(layout, cross_send), "cross_sum", after=[upper]
    )
    got_cross = send(cross_upper, layout.inplane(top))
    self_out_grad, dq, dk, dv = self_attention_back(layout, tokens)(
        mid_low, w_self, self_mix, q, k, v, self_prob, after=[upper, cross_upper]
    )
    input_grad, self_keep, self_send = self_backward(layout, tokens)(
        self_out_grad, dq, dk, dv, grad_mid, gains, norm_two, norm_three,
        far=[w_self, a_saved, x],
    )
    wide_slots = wide_slots_sum(layout, hidden)(lower, got, after=[self_keep])
    wide_got = exchange_planes(layout, wide_slots)
    self_upper, self_lower = halves_sum(
        layout, self_keep, swap_cores(layout, fence(self_send, [wide_slots])), "self_sum"
    )
    momentum = wide_momentum(layout, hidden)(expand_momentum, contract_momentum)
    got_self = send(self_upper, layout.inplane(top))
    for bit in reversed(range(top)):
        cross_upper, cross_lower = halves_sum(layout, cross_lower, got_cross, "cross_sum")
        got_cross = send(cross_upper, layout.inplane(bit))
    nest_rows = wide_nest(layout, hidden)(wide_got, momentum, after=[self_upper, cross_upper])
    nest = exchange_planes(layout, nest_rows).reshape(D, hidden)
    for bit in reversed(range(top)):
        self_upper, self_lower = halves_sum(layout, self_lower, got_self, "self_sum")
        got_self = send(self_upper, layout.inplane(bit))
    rows_by_slot = attention_slots(layout)(cross_lower, got_cross, self_lower, got_self)
    nest = fence(nest, [rows_by_slot])
    nest_other = swap_cores(layout, nest)
    expand_velocity, contract_velocity, velocity_done = wide_velocity(layout, hidden)(
        nest, nest_other, expand_momentum, contract_momentum
    )
    nest_pieces = gather_inplane(
        layout, nest, lambda piece: fence(piece, [rows_by_slot, velocity_done])
    )
    attn_nest, attn_grad, norm_rows = attention_nest(layout)(
        exchange_planes(layout, rows_by_slot), far=[attn_momentum], after=[nest_pieces[layout.tensor // 2 - 1]]
    )

    early = gather_inplane_direct(layout, attn_grad)

    def whole_pieces(halves):
        shared = layout.parts.bit_length() - 1
        gathered = [halves]
        for bit in range(shared):
            pairs = layout.pairs(lambda d, t: d * layout.tensor + (t ^ (1 << bit)))
            gathered = gathered + [[send(half, pairs) for half in one] for one in gathered]
        return [half for one in gathered for half in one]

    wide_ortho = orthogonalize_wide(layout, hidden)(
        *nest_pieces[1:], far=nest_pieces[:1], after=[attn_nest])
    half = fence(exchange_planes(layout, attn_nest), [wide_ortho, *early[1:]])
    mine, others = orthogonalize_attention(layout)(
        far=whole_pieces([half, swap_cores(layout, half)])
    )
    late_pieces = gather_inplane_direct(layout, jnp.stack([mine, swap_cores(layout, others)]))
    attn_velocity = attention_velocity(layout)(*early, attn_momentum)
    norm_updated, first_updated, second_updated = finish_norms(layout)(
        norm_rows, norm_params, first_moments, second_moments
    )

    expand_updated, expand_copy, contract_updated, contract_copy = finish_wide(
        layout, hidden, full_hidden
    )(wide_ortho, swap_cores(layout, wide_ortho), expand_master, contract_master)
    attn_updated, attn_copy = finish_attention(layout)(
        *late_pieces, attn_master
    )
    return (
        output[None],
        input_grad[None],
        encoder_grad[None],
        attn_updated,
        attn_velocity,
        attn_copy,
        expand_updated,
        expand_velocity,
        expand_copy,
        contract_updated,
        contract_velocity,
        contract_copy,
        norm_updated,
        first_updated,
        second_updated,
    )


def solution(mesh):
    layout = Layout(mesh.shape["dp"], mesh.shape["tensor"])

    def local(*arguments):
        return device_program(layout, arguments)

    rows = P(AXES, None, None)
    by_dp, by_column, by_row, norm = P(None, "dp", None), P(None, "tensor"), P("tensor", None), P(None, "dp")
    return jax.shard_map(
        local,
        mesh=mesh,
        in_specs=(rows, rows, P(AXES, None), P(AXES, None), rows)
        + (by_dp, by_dp, by_column, by_column, by_row, by_row, norm, norm, norm),
        out_specs=(rows, rows, rows, by_dp, by_dp, by_dp)
        + (by_column, by_column, by_column, by_row, by_row, by_row, norm, norm, norm),
        check_vma=False,
    )
```

```python
import functools
import math

import jax
import jax.numpy as jnp
from jax import lax
from jax.experimental import pallas as pl
from jax.experimental.pallas import tpu as pltpu
from jax.sharding import PartitionSpec as P

D = 512
HEADS = 8
HEAD = D // HEADS
PAIR = 2 * HEAD
NS_STEPS = 5
GRAM_STEPS = 3
STEP = 10

MASKED_SCORE = -1e30
NORM_EPSILON = 1e-05
MOMENTUM_DECAY = 0.95
MUON_RATE = 0.15
MUON_DECAY = 0.01
POLY_FIRST = 3.4445
POLY_SECOND = -4.775
POLY_THIRD = 2.0315
ADAM_RATE = 0.4
BETA_FIRST = 0.9
BETA_SECOND = 0.999
ADAM_EPSILON = 1e-08
GROUP = 4
QUERY_BLOCK = 512

F32 = jnp.float32
BF16 = jnp.bfloat16
AXES = ("dp", "tensor")
MIB = 1 << 20
VMEM_BYTES = 24 * MIB
NORM_ROWS = 16


def mm(left, right):
    return lax.dot_general(left, right, (((1,), (0,)), ((), ())), preferred_element_type=F32)


def mm_nt(left, right):
    return lax.dot_general(left, right, (((1,), (1,)), ((), ())), preferred_element_type=F32)


def mm_tn(left, right):
    return lax.dot_general(left, right, (((0,), (0,)), ((), ())), preferred_element_type=F32)


def normalized(values):
    average = jnp.mean(values, -1, keepdims=True)
    centred = values - average
    inv_std = lax.rsqrt(jnp.mean(centred * centred, -1, keepdims=True) + NORM_EPSILON)
    return centred * inv_std, inv_std


def norm_backward(incoming, values, gain_row):
    normed, inv_std = normalized(values)
    scaled = incoming * gain_row
    inner = (
        scaled
        - jnp.mean(scaled, -1, keepdims=True)
        - normed * jnp.mean(scaled * normed, -1, keepdims=True)
    )
    gain_grad = jnp.sum(incoming * normed, 0, keepdims=True)
    shift_grad = jnp.sum(incoming, 0, keepdims=True)
    return inner * inv_std, gain_grad, shift_grad


def head_mask(half, value):
    lane = lax.broadcasted_iota(jnp.int32, (1, PAIR), 1)
    inside = jnp.logical_and(lane >= half * HEAD, lane < (half + 1) * HEAD)
    return jnp.where(inside, value, 0.0).astype(BF16)


def pair_columns(pair):
    return pl.ds(pl.multiple_of(pair * PAIR, PAIR), PAIR)


def attend(q_ref, k_ref, v_ref, key_seg_ref, query_seg_ref, prob_ref, out_ref, done):
    queries = q_ref.shape[0]
    block = min(QUERY_BLOCK, queries)

    def one_pair(pair, carry):
        cols = pair_columns(pair)
        keys, values = k_ref[:, cols], v_ref[:, cols]
        for start in range(0, queries, block):
            rows = pl.ds(start, block)
            query = q_ref[rows, cols]
            allowed = key_seg_ref[...] == query_seg_ref[:, rows]
            total = None
            for half in range(2):
                scores = mm_nt(keys * head_mask(half, HEAD**-0.5), query)
                scores = jnp.where(allowed, scores, MASKED_SCORE)
                peak = jnp.max(scores, 0, keepdims=True)
                weights = jnp.exp(scores - peak)
                soft = (weights * (1.0 / jnp.sum(weights, 0, keepdims=True))).astype(BF16)
                prob_ref[pair * 2 + half, :, rows] = soft
                part = mm_tn(soft, values * head_mask(half, 1.0))
                total = part if total is None else total + part
            out_ref[rows, cols] = total.astype(BF16)
        done(pair)
        return carry

    lax.fori_loop(0, HEADS // 2, one_pair, 0)


def attend_back(q_ref, k_ref, v_ref, prob_ref, grad_ref, dq_ref, dk_ref, dv_ref, ready):
    queries = q_ref.shape[0]
    block = min(QUERY_BLOCK, queries)
    scaling = HEAD**-0.5

    def one_pair(pair, carry):
        cols = pair_columns(pair)
        keys, values = k_ref[:, cols], v_ref[:, cols]
        key_sum = value_sum = None
        ready(pair)
        for start in range(0, queries, block):
            rows = pl.ds(start, block)
            query, grad = q_ref[rows, cols], grad_ref[rows, cols]
            query_sum = None
            for half in range(2):
                mask = head_mask(half, 1.0)
                soft = prob_ref[pair * 2 + half, :, rows]
                weights = soft.astype(F32)
                grad_soft = mm_nt(values * mask, grad)
                product = weights * grad_soft
                inner = jnp.sum(product, 0, keepdims=True)
                grad_scores = (product - weights * inner).astype(BF16)
                value_part = mm(soft, grad * mask)
                key_part = mm(grad_scores, query * mask)
                query_part = mm_tn(grad_scores, keys * mask)
                value_sum = value_part if value_sum is None else value_sum + value_part
                key_sum = key_part if key_sum is None else key_sum + key_part
                query_sum = query_part if query_sum is None else query_sum + query_part
            dq_ref[rows, cols] = (query_sum * scaling).astype(BF16)
        dk_ref[:, cols] = (key_sum * scaling).astype(BF16)
        dv_ref[:, cols] = value_sum.astype(BF16)
        return carry

    lax.fori_loop(0, HEADS // 2, one_pair, 0)


def pair_copy(source, target, sems, pair):
    heads = pl.ds(pair * 2, 2)
    return pltpu.make_async_copy(source.at[heads], target.at[heads], sems.at[pair])


def reorder(core, position, bits):
    if core == 0:
        return position
    return sum(((position >> bit) & 1) << (bits - 1 - bit) for bit in range(bits))


class Layout:
    def __init__(self, dp_size, tensor_size):
        self.dp, self.tensor = dp_size, tensor_size
        self.bits = tensor_size.bit_length() - 1
        self.planes = dp_size // 2
        self.parts = tensor_size // GROUP
        self.rows = D // dp_size
        self.quad = tensor_size == 4
        self.width = D // self.parts

    def pairs(self, move):
        return [
            (d * self.tensor + t, move(d, t)) for d in range(self.dp) for t in range(self.tensor)
        ]

    def inplane(self, bit):
        return self.pairs(
            lambda d, t: d * self.tensor + (t ^ reorder(d & 1, 1 << bit, self.bits))
        )

    def inplane_position(self, position):
        return self.pairs(
            lambda d, t: d * self.tensor + (t ^ reorder(d & 1, position, self.bits))
        )

    def plain_inplane(self, offset):
        return self.pairs(lambda d, t: d * self.tensor + (t ^ offset))

    def plane(self, slot):
        return self.pairs(lambda d, t: (d ^ (2 * slot)) * self.tensor + t)

    def other_core(self):
        return self.pairs(lambda d, t: (d ^ 1) * self.tensor + t)


def send(values, pairs):
    return lax.ppermute(values, AXES, pairs)


def gather_inplane(layout, piece, forwarded=None):
    pieces = [piece]
    for bit in range(layout.bits):
        if forwarded is not None and bit + 1 == layout.bits:
            pieces = pieces[:1] + [forwarded(one) for one in pieces[1:]]
        pieces = pieces + [send(one, layout.inplane(bit)) for one in pieces]
    return pieces


def gather_inplane_direct(layout, piece):
    return [piece] + [
        send(piece, layout.inplane_position(position)) for position in range(1, layout.tensor)
    ]


def send_planes(layout, piece):
    return [piece] + [send(piece, layout.plane(slot)) for slot in range(1, layout.planes)]


def exchange_planes(layout, pieces):
    groups = [list(range(core, layout.dp, 2)) for core in range(2)]
    return lax.all_to_all(pieces, "dp", 0, 0, axis_index_groups=groups, tiled=True)


def exchange_inplane(pieces):
    return lax.all_to_all(pieces, "tensor", 0, 0, tiled=True)


def swap_cores(layout, values):
    return send(values, layout.other_core())


def whole_kernel(body, out_shape, scratch=(), flops=0, moved=0, name=None, far_outs=0):
    out_specs = jax.tree.map(lambda _: pl.BlockSpec(memory_space=pltpu.VMEM), out_shape)
    shapes = out_shape
    if far_outs:
        out_specs = (pl.BlockSpec(memory_space=pltpu.HBM),) * far_outs + out_specs[far_outs:]
        shapes = tuple(pltpu.HBM(one.shape, one.dtype) for one in out_shape[:far_outs])
        shapes = shapes + out_shape[far_outs:]

    def call(*operands, far=(), loose=(), after=()):
        near = len(operands)
        operands = operands + tuple(far) + tuple(loose)
        read = len(operands)

        def without_after(*refs):
            place = lax.axis_index("dp"), lax.axis_index("tensor")
            info = (place[0] % 2, place[0] // 2, place[1])
            body(info, *refs[:read], *refs[read + len(after) :])

        operands = operands[:near] + tuple(
            pltpu.with_memory_space_constraint(one, pltpu.HBM) for one in far
        ) + tuple(loose)
        return pl.pallas_call(
            without_after,
            out_shape=shapes,
            in_specs=[pl.BlockSpec(memory_space=pltpu.VMEM)] * near
            + [pl.BlockSpec(memory_space=pltpu.HBM)] * len(far)
            + [pl.BlockSpec(memory_space=pl.ANY)] * (len(loose) + len(after)),
            out_specs=out_specs,
            scratch_shapes=list(scratch),
            compiler_params=pltpu.CompilerParams(vmem_limit_bytes=VMEM_BYTES),
            cost_estimate=pl.CostEstimate(flops=flops, bytes_accessed=moved, transcendentals=0),
            name=name,
        )(*operands, *after)

    return call


class Copies:
    def __init__(self, sems):
        self.sems, self.count = sems, 0

    def start(self, source, target):
        copy = pltpu.make_async_copy(source, target, self.sems.at[self.count])
        copy.start()
        self.count += 1
        return copy


def wait_all(copies):
    for copy in copies:
        copy.wait()


def low_shape(*shape):
    return jax.ShapeDtypeStruct(shape, BF16)


def wide_shape(*shape):
    return jax.ShapeDtypeStruct(shape, F32)


UNIT = 2 * D * D * D


def owner_at(info_ref, layout, position, other=False):
    core = info_ref[0]
    first = 1 if other else 0
    offset = jnp.where(
        core == first, reorder(0, position, layout.bits), reorder(1, position, layout.bits)
    )
    return jnp.bitwise_xor(info_ref[2], offset)


def row_start(info_ref, layout, plane, other=False):
    core = 1 - info_ref[0] if other else info_ref[0]
    return pl.multiple_of((plane * 2 + core) * layout.rows, layout.rows)


def quad_matrix(info_ref, position):
    tensor = info_ref[2]
    side = jnp.bitwise_xor(lax.rem(tensor, 2), lax.div(tensor, 2))
    return jnp.bitwise_xor(side, position // 2) * 2 + position % 2


def weight_chunk(layout, group, name, copies_out):
    rows = layout.rows
    tiles = NORM_ROWS if group == 0 else 0

    def body(info_ref, norm_ref, source_ref, out_ref, tile, blocks, sems):
        copies = Copies(sems)
        moving = [
            copies.start(
                source_ref.at[group * GROUP + quad_matrix(info_ref, position)],
                blocks.at[position],
            )
            for position in range(2)
        ]
        if tiles:
            tile[...] = jnp.zeros_like(tile)
            for block in range(layout.dp):

                @pl.when(info_ref[1] * 2 + info_ref[0] == block)
                def _():
                    tile[0:6, block * rows : (block + 1) * rows] = norm_ref[...]

            for plane in range(copies_out):
                out_ref[plane, 2 * rows :, :] = tile[...].astype(BF16)
        wait_all(moving)
        for index in range(2):
            block = blocks[index].astype(BF16)
            for plane in range(copies_out):
                out_ref[plane, index * rows : (index + 1) * rows, :] = block

    return whole_kernel(
        body,
        low_shape(copies_out, 2 * rows + tiles, D),
        scratch=[
            pltpu.VMEM((NORM_ROWS, D), F32),
            pltpu.VMEM((2, rows, D), F32),
            pltpu.SemaphoreType.DMA((2,)),
        ],
        moved=1 << 20,
        name=name,
    )


def self_split(layout):
    rows, planes = layout.rows, layout.planes

    def body(info_ref, *refs):
        slots, outs, tile_ref = refs[:planes], refs[planes : planes + 2], refs[-1]
        tile = None
        for slot, ref in enumerate(slots):
            plane = jnp.bitwise_xor(info_ref[1], slot)
            for index in range(2):
                outs[index][plane] = ref[0, index * rows : (index + 1) * rows, :]
            part = ref[0, 2 * rows :, :].astype(F32)
            tile = part if tile is None else tile + part
        tile_ref[...] = tile.astype(BF16)

    one = low_shape(planes, rows, D)
    return whole_kernel(
        body, (one, one, low_shape(NORM_ROWS, D)), moved=2 << 20, name="self_split"
    )


def cross_rows(layout):
    rows, planes = layout.rows, layout.planes

    def body(info_ref, source_far, out_ref, blocks, sem):
        copy = pltpu.make_async_copy(source_far.at[GROUP : 2 * GROUP], blocks, sem)
        copy.start()
        copy.wait()
        for matrix in range(GROUP):
            block = blocks[matrix].astype(BF16)
            for plane in range(planes):
                out_ref[plane, matrix * rows : (matrix + 1) * rows, :] = block

    return whole_kernel(
        body,
        low_shape(planes, GROUP * rows, D),
        scratch=[pltpu.VMEM((GROUP, rows, D), F32), pltpu.SemaphoreType.DMA],
        moved=2 << 20,
        name="cross_rows",
    )


def fetch_weights(info_ref, layout, refs, weights_ref, copies):
    if not layout.quad:
        return [copies.start(refs[0], weights_ref)]
    moving = []
    for index, ref in enumerate(refs):
        matrix = quad_matrix(info_ref, index % GROUP)
        for plane in range(layout.planes):
            at = pl.ds(row_start(info_ref, layout, plane, index >= GROUP), layout.rows)
            moving.append(copies.start(ref.at[plane], weights_ref.at[matrix, at, :]))
    return moving


def fetch_cross(info_ref, layout, refs, weights_ref, copies):
    if not layout.quad:
        return [copies.start(refs[0], weights_ref)]
    moving, rows = [], layout.rows
    for index, ref in enumerate(refs):
        for plane in range(layout.planes):
            at = pl.ds(row_start(info_ref, layout, plane, index == 1), rows)
            for matrix in range(GROUP):
                here = slice(matrix * rows, (matrix + 1) * rows)
                moving.append(
                    copies.start(ref.at[plane, here, :], weights_ref.at[matrix, at, :])
                )
    return moving


def weight_pieces(layout):
    return (2 * GROUP, 2 * GROUP * layout.planes) if layout.quad else (1, 1)


def place_grads(info_ref, layout, grads_ref, keep_ref, send_ref):
    for other, ref in ((False, keep_ref), (True, send_ref)):
        for position in range(layout.tensor):
            owner = owner_at(info_ref, layout, position, other)
            for slot in range(layout.planes):
                rows = pl.ds(row_start(info_ref, layout, slot, other), layout.rows)
                if layout.parts == 1:
                    block = grads_ref[owner, rows, :]
                else:
                    part = lax.rem(owner, layout.parts) * layout.width
                    cols = pl.ds(pl.multiple_of(part, layout.width), layout.width)
                    block = grads_ref[lax.div(owner, layout.parts), rows, cols]
                ref[position, slot, 0 : layout.rows, :] = block


def first_norm(tokens):
    def body(info_ref, tile_ref, other_ref, x_far, a_out, a_ref, gains_ref, x_ref, sems):
        copies = Copies(sems)
        x_copy = copies.start(x_far, x_ref)
        gains_ref[...] = tile_ref[...].astype(F32) + other_ref[...].astype(F32)
        x_copy.wait()
        normed, _ = normalized(x_ref[...].astype(F32))
        a_ref[...] = (normed * gains_ref[0:1, :] + gains_ref[1:2, :]).astype(BF16)
        copies.start(a_ref, a_out).wait()

    return whole_kernel(
        body,
        (low_shape(tokens, D), low_shape(tokens, D), wide_shape(NORM_ROWS, D)),
        scratch=[pltpu.VMEM((tokens, D), BF16), pltpu.SemaphoreType.DMA((2,))],
        moved=1 << 20,
        name="first_norm",
        far_outs=1,
    )


def self_forward(layout, tokens):
    count, pieces = weight_pieces(layout)

    def body(info_ref, a_ref, gains_ref, query_seg_ref, key_seg_ref, x_far, *refs):
        w_out, q_out, k_out, v_out, prob_out, mix_out, mid_out, c_ref = refs[count : count + 8]
        x_ref, w_ref, q_ref, k_ref, v_ref, prob_ref, mix_ref, mid_ref = refs[count + 8 : -2]
        sems, pair_sems = refs[-2:]
        copies = Copies(sems)
        arriving = fetch_weights(info_ref, layout, refs[:count], w_ref, copies)
        x_copy = copies.start(x_far, x_ref)
        wait_all(arriving)
        leaving = [copies.start(w_ref, w_out)]
        for index, (ref, out) in enumerate(((q_ref, q_out), (k_ref, k_out), (v_ref, v_out))):
            ref[...] = mm(a_ref[...], w_ref[index]).astype(BF16)
            leaving.append(copies.start(ref, out))
        attend(
            q_ref, k_ref, v_ref, key_seg_ref, query_seg_ref, prob_ref, mix_ref,
            lambda pair: pair_copy(prob_ref, prob_out, pair_sems, pair).start(),
        )
        leaving.append(copies.start(mix_ref, mix_out))
        x_copy.wait()
        mid = x_ref[...].astype(F32) + mm(mix_ref[...], w_ref[3])
        mid_ref[...] = mid
        leaving.append(copies.start(mid_ref, mid_out))
        normed, _ = normalized(mid)
        c_ref[...] = (normed * gains_ref[2:3, :] + gains_ref[3:4, :]).astype(BF16)
        wait_all(leaving)
        for pair in range(HEADS // 2):
            pair_copy(prob_ref, prob_out, pair_sems, pair).wait()

    low, rows = low_shape(tokens, D), pltpu.VMEM((tokens, D), BF16)
    probs = (HEADS, tokens, tokens)
    return whole_kernel(
        body,
        (
            low_shape(GROUP, D, D),
            low,
            low,
            low,
            low_shape(*probs),
            low,
            wide_shape(tokens, D),
            low,
        ),
        scratch=[rows, pltpu.VMEM((GROUP, D, D), BF16), rows, rows, rows]
        + [pltpu.VMEM(probs, BF16), rows, pltpu.VMEM((tokens, D), F32)]
        + [pltpu.SemaphoreType.DMA((pieces + 8,)), pltpu.SemaphoreType.DMA((HEADS // 2,))],
        flops=14 * UNIT,
        moved=12 << 20,
        name="self_forward",
        far_outs=7,
    )


def cross_forward(layout, tokens, states):
    count, pieces = (2, weight_pieces(layout)[1]) if layout.quad else (1, 1)

    def body(info_ref, c_ref, gains_ref, query_seg_ref, key_seg_ref, enc_far, mid_far, *refs):
        w_ref, q_ref, k_ref, v_ref, prob_ref, mix_ref, late_ref, f_ref = refs[count : count + 8]
        enc_ref, mid_ref, sems = refs[count + 8 :]
        copies = Copies(sems)
        arriving = fetch_cross(info_ref, layout, refs[:count], w_ref, copies)
        arriving.append(copies.start(enc_far, enc_ref))
        mid_copy = copies.start(mid_far, mid_ref)
        wait_all(arriving)
        for index, (source, ref) in enumerate(
            ((c_ref, q_ref), (enc_ref, k_ref), (enc_ref, v_ref))
        ):
            ref[...] = mm(source[...], w_ref[index]).astype(BF16)
        attend(
            q_ref, k_ref, v_ref, key_seg_ref, query_seg_ref, prob_ref, mix_ref, lambda pair: None
        )
        mid_copy.wait()
        late = mid_ref[...] + mm(mix_ref[...], w_ref[3])
        late_ref[...] = late
        normed, _ = normalized(late)
        f_ref[...] = (normed * gains_ref[4:5, :] + gains_ref[5:6, :]).astype(BF16)

    low = low_shape(tokens, D)
    return whole_kernel(
        body,
        (
            low_shape(GROUP, D, D),
            low,
            low_shape(states, D),
            low_shape(states, D),
            low_shape(HEADS, states, tokens),
            low,
            wide_shape(tokens, D),
            low,
        ),
        scratch=[pltpu.VMEM((states, D), BF16), pltpu.VMEM((tokens, D), F32)]
        + [pltpu.SemaphoreType.DMA((pieces + 2,))],
        flops=14 * UNIT,
        moved=12 << 20,
        name="cross_forward",
    )


def gelu_parts(pre):
    slope = math.sqrt(2.0 / math.pi)
    square = pre * pre
    bent = jnp.tanh(slope * pre * (1.0 + 0.044715 * square))
    half = 0.5 * (1.0 + bent)
    inner = slope * (1.0 + 3 * 0.044715 * square)
    return pre * half, half + 0.5 * pre * (1.0 - bent * bent) * inner


def feed_forward(layout, tokens, hidden):
    count, planes = layout.tensor, layout.planes
    piece_rows, full = D // planes, layout.tensor * hidden

    def body(info_ref, f_ref, cot_far, *refs):
        mine, others = refs[:count], refs[count : 2 * count]
        w_in, w_out, post_ref, d_pre_ref, keep_ref, send_ref = refs[2 * count : -5]
        cot_ref, f_t, cot_t, sems, cot_sem = refs[-5:]
        first_core = info_ref[0] == 0

        def columns(position):
            return slice(position * hidden, (position + 1) * hidden)

        def fetch(source, target, matrix, position):
            return pltpu.make_async_copy(
                source, target.at[:, columns(position)], sems.at[matrix, position]
            )

        cot_copy = pltpu.make_async_copy(cot_far, cot_ref, cot_sem)
        cot_copy.start()
        for position in range(count):
            turned = reorder(1, position, layout.bits)

            @pl.when(first_core)
            def _():
                fetch(mine[position], w_in, 0, position).start()
                fetch(others[turned], w_out, 1, position).start()

            @pl.when(jnp.logical_not(first_core))
            def _():
                fetch(others[position], w_in, 0, position).start()
                fetch(mine[turned], w_out, 1, position).start()

        f_t[...] = f_ref[...].T
        cot_copy.wait()
        cot_t[...] = cot_ref[...].T
        for position in range(count):
            cols = columns(position)
            fetch(mine[0], w_in, 0, position).wait()
            fetch(mine[0], w_out, 1, position).wait()
            pre = mm(f_ref[...], w_in[:, cols])
            grad_post = mm(cot_ref[...], w_out[:, cols])
            post, slope = gelu_parts(pre)
            post_ref[:, cols] = post.astype(BF16)
            d_pre_ref[:, cols] = (slope * grad_post).astype(BF16)
        for position in range(count):
            cols = columns(position)
            turned = reorder(1, position, layout.bits)
            keep_at = jnp.where(first_core, position, turned)
            send_at = jnp.where(first_core, turned, position)
            grad_in = mm(f_t[...], d_pre_ref[:, cols]).astype(BF16)
            grad_out = mm(cot_t[...], post_ref[:, cols]).astype(BF16)
            for slot in range(planes):
                part = slice(slot * piece_rows, (slot + 1) * piece_rows)
                keep_ref[keep_at, slot] = jnp.where(first_core, grad_in[part], grad_out[part])
                send_ref[send_at, slot] = jnp.where(first_core, grad_out[part], grad_in[part])

    pieces = low_shape(count, planes, piece_rows, hidden)
    return whole_kernel(
        body,
        (low_shape(D, full), low_shape(D, full), low_shape(tokens, full), low_shape(tokens, full))
        + (pieces, pieces),
        scratch=[
            pltpu.VMEM((tokens, D), BF16),
            pltpu.VMEM((D, tokens), BF16),
            pltpu.VMEM((D, tokens), BF16),
            pltpu.SemaphoreType.DMA((2, count)),
            pltpu.SemaphoreType.DMA,
        ],
        flops=4 * UNIT * full // D,
        moved=14 << 20,
        name="feed_forward",
    )


def feed_forward_sums(layout, tokens, hidden):
    def body(info_ref, w_in, w_out, post_ref, d_pre_ref, late_ref, gains_ref, cot_far, *refs):
        out_ref, glate_ref, dlate_ref, norm_ref, cot_ref, sem = refs
        cot_copy = pltpu.make_async_copy(cot_far, cot_ref, sem)
        cot_copy.start()
        late = late_ref[...]
        back = mm_nt(d_pre_ref[...], w_in[...])
        back, gain_grad, shift_grad = norm_backward(back, late, gains_ref[4:5, :])
        cot_copy.wait()
        grad_late = cot_ref[...].astype(F32) + back
        glate_ref[...] = grad_late
        dlate_ref[...] = grad_late.astype(BF16)
        norm_ref[0:1, :] = gain_grad
        norm_ref[1:2, :] = shift_grad
        out_ref[...] = (late + mm_nt(post_ref[...], w_out[...])).astype(BF16)

    low = low_shape(tokens, D)
    return whole_kernel(
        body,
        (low, wide_shape(tokens, D), low, wide_shape(2, D)),
        scratch=[pltpu.VMEM((tokens, D), BF16), pltpu.SemaphoreType.DMA],
        flops=2 * UNIT * layout.tensor * hidden // D,
        moved=4 << 20,
        name="feed_forward_sums",
    )


def cross_backward(layout, tokens, states):
    def body(info_ref, dlate_ref, mix_ref, glate_ref, gains_ref, *refs):
        q_ref, k_ref, v_ref, prob_ref, c_ref, w_ref, enc_far, mid_far = refs[:8]
        enc_grad_ref, gmid_ref, dmid_ref, norm_ref, keep_ref, send_ref = refs[8:14]
        enc_ref, mid_ref, dq, dk, dv, grads, d_mix, sems = refs[14:]
        copies = Copies(sems)
        later = [copies.start(enc_far, enc_ref), copies.start(mid_far, mid_ref)]
        d_mix[...] = mm_nt(dlate_ref[...], w_ref[3]).astype(BF16)
        grads[3] = mm_tn(mix_ref[...], dlate_ref[...]).astype(BF16)
        attend_back(
            q_ref, k_ref, v_ref, prob_ref, d_mix, dq, dk, dv, lambda pair: None
        )
        wait_all(later)
        grads[0] = mm_tn(c_ref[...], dq[...]).astype(BF16)
        enc_t = enc_ref[...].T
        grads[1] = mm(enc_t, dk[...]).astype(BF16)
        grads[2] = mm(enc_t, dv[...]).astype(BF16)
        place_grads(info_ref, layout, grads, keep_ref, send_ref)
        enc_grad_ref[...] = (mm_nt(dk[...], w_ref[1]) + mm_nt(dv[...], w_ref[2])).astype(BF16)
        back, gain_grad, shift_grad = norm_backward(
            mm_nt(dq[...], w_ref[0]), mid_ref[...], gains_ref[2:3, :]
        )
        grad_mid = glate_ref[...] + back
        gmid_ref[...] = grad_mid
        dmid_ref[...] = grad_mid.astype(BF16)
        norm_ref[0:1, :] = gain_grad
        norm_ref[1:2, :] = shift_grad

    low, rows = low_shape(tokens, D), pltpu.VMEM((tokens, D), BF16)
    keys = pltpu.VMEM((states, D), BF16)
    pieces = low_shape(layout.tensor, layout.planes, layout.rows, layout.width)
    return whole_kernel(
        body,
        (low_shape(states, D), wide_shape(tokens, D), low, wide_shape(2, D), pieces, pieces),
        scratch=[keys, pltpu.VMEM((tokens, D), F32), rows, keys, keys]
        + [pltpu.VMEM((GROUP, D, D), BF16), rows, pltpu.SemaphoreType.DMA((2,))],
        flops=26 * UNIT,
        moved=14 << 20,
        name="cross_backward",
    )


def self_attention_back(layout, tokens):
    def body(info_ref, dmid_ref, w_ref, mix_ref, q_ref, k_ref, v_ref, prob_ref, *refs):
        out_ref, dq, dk, dv, d_mix = refs
        d_mix[...] = mm_nt(dmid_ref[...], w_ref[3]).astype(BF16)
        attend_back(
            q_ref, k_ref, v_ref, prob_ref, d_mix, dq, dk, dv, lambda pair: None
        )
        out_ref[...] = mm_tn(mix_ref[...], dmid_ref[...]).astype(BF16)

    low = low_shape(tokens, D)
    return whole_kernel(
        body,
        (low_shape(D, D), low, low, low),
        scratch=[pltpu.VMEM((tokens, D), BF16)],
        flops=18 * UNIT,
        moved=10 << 20,
        name="self_attention_back",
    )


def self_backward(layout, tokens):
    def body(info_ref, out_grad_ref, dq, dk, dv, gmid_ref, gains_ref, *refs):
        norm_two_ref, norm_three_ref, w_ref, a_ref, x_ref = refs[:5]
        grad_ref, keep_ref, send_ref, grads, norms, tile = refs[5:]
        grads[3] = out_grad_ref[...]
        a_t = a_ref[...].T
        for index, ref in enumerate((dq, dk, dv)):
            grads[index] = mm(a_t, ref[...]).astype(BF16)
        total = None
        for index, ref in enumerate((dq, dk, dv)):
            part = mm_nt(ref[...], w_ref[index])
            total = part if total is None else total + part
        place_grads(info_ref, layout, grads, keep_ref, send_ref)
        back, gain_grad, shift_grad = norm_backward(
            total, x_ref[...].astype(F32), gains_ref[0:1, :]
        )
        grad_ref[...] = (gmid_ref[...] + back).astype(BF16)
        tile[...] = jnp.zeros_like(tile)
        for index, row in enumerate((gain_grad, shift_grad)):
            norms[index : index + 1, :] = row
        norms[2:4, :] = norm_two_ref[...]
        norms[4:6, :] = norm_three_ref[...]
        for block in range(layout.dp):
            columns = slice(block * layout.rows, (block + 1) * layout.rows)
            tile[block, 0:6, 0 : layout.rows] = norms[0:6, columns].astype(BF16)
        for other, ref in ((False, keep_ref), (True, send_ref)):
            core = 1 - info_ref[0] if other else info_ref[0]
            for slot in range(layout.planes):
                block = tile[slot * 2 + core]
                for position in range(layout.tensor):
                    ref[position, slot, layout.rows :, :] = block

    low = low_shape(tokens, D)
    pieces = low_shape(layout.tensor, layout.planes, layout.rows + NORM_ROWS, layout.width)
    return whole_kernel(
        body,
        (low, pieces, pieces),
        scratch=[
            pltpu.VMEM((GROUP, D, D), BF16),
            pltpu.VMEM((8, D), F32),
            pltpu.VMEM((layout.dp, NORM_ROWS, layout.width), BF16),
        ],
        flops=7 * UNIT,
        moved=6 << 20,
        name="self_backward",
    )


def gram_rest(low_ref, rest_ref, ratio, shift):
    half = D // 2
    diagonal = lax.broadcasted_iota(jnp.int32, (half, half), 0) == lax.broadcasted_iota(
        jnp.int32, (half, half), 1
    )
    shifted = jnp.where(diagonal, shift, 0.0)
    top, bottom = slice(0, half), slice(half, D)
    upper, lower = low_ref[top, :], low_ref[bottom, :]
    rest_ref[top, top] = (ratio * mm_nt(upper, upper) - shifted).astype(BF16)
    corner = (ratio * mm_nt(upper, lower)).astype(BF16)
    rest_ref[top, bottom] = corner
    rest_ref[bottom, top] = corner.T
    rest_ref[bottom, bottom] = (ratio * mm_nt(lower, lower) - shifted).astype(BF16)


def apply_factor(low_ref, poly_ref, scale, kept):
    for start in range(0, kept, D):
        cols = slice(start, min(start + D, kept))
        part = low_ref[:, cols]
        low_ref[:, cols] = (scale * part.astype(F32) + mm(poly_ref[...], part)).astype(BF16)


def sweep(low_ref, rest_ref, poly_ref, width, kept, first=False):
    shift = jnp.zeros((), F32)
    for start in range(0, width, D):
        part = low_ref[:, start : start + D].astype(F32)
        shift = shift + jnp.sum(part * part)
    inverse = 1.0 / (jnp.sqrt(shift) + 1e-07) if first else 1.0
    shift = shift * (inverse * inverse * (1.0 / D))
    gram_rest(low_ref, rest_ref, inverse * inverse, shift)
    slope = POLY_SECOND + 2.0 * POLY_THIRD * shift
    scale = POLY_FIRST + POLY_SECOND * shift + POLY_THIRD * shift * shift
    half = D // 2
    for rows in (slice(0, half), slice(half, D)):
        square = mm(rest_ref[rows, :], rest_ref[...])
        poly = slope * rest_ref[rows, :].astype(F32) + POLY_THIRD * square
        poly_ref[rows, :] = (inverse * poly).astype(BF16)
    apply_factor(low_ref, poly_ref, inverse * scale, kept)


def orthogonalize_attention(layout):
    parts, rows = layout.parts, layout.rows

    def body(info_ref, *refs):
        pieces = refs[:parts]
        mine_ref, other_ref, low, rest, poly = refs[parts:]
        for part, ref in enumerate(pieces):
            low[:, part * layout.width : (part + 1) * layout.width] = ref[...]
        sweep(low, rest, poly, D, D, first=True)

        def one(step, carry):
            sweep(low, rest, poly, D, D)
            return carry

        lax.fori_loop(1, NS_STEPS, one, 0)
        for ref, core in ((mine_ref, info_ref[0]), (other_ref, 1 - info_ref[0])):
            start = pl.multiple_of((2 * info_ref[1] + core) * rows, rows)
            ref[...] = low[pl.ds(start, rows), 0 : layout.width]

    return whole_kernel(
        body,
        (low_shape(rows, layout.width), low_shape(rows, layout.width)),
        scratch=[pltpu.VMEM((D, D), BF16)] * 3,
        flops=15 * UNIT,
        moved=2 << 20,
        name="orthogonalize_attention",
    )


def gram_sweeps(rest_ref, poly_ref, square_ref, sum_ref, shift):
    diagonal = lax.broadcasted_iota(jnp.int32, (D, D), 0) == lax.broadcasted_iota(
        jnp.int32, (D, D), 1
    )
    scale = None
    for step in range(GRAM_STEPS):
        rest = rest_ref[...]
        slope = POLY_SECOND + 2.0 * POLY_THIRD * shift
        here = POLY_FIRST + POLY_SECOND * shift + POLY_THIRD * shift * shift
        poly = slope * rest.astype(F32) + POLY_THIRD * mm(rest, rest)
        poly_ref[...] = poly.astype(BF16)
        low = poly_ref[...]
        if scale is None:
            scale = here
            sum_ref[...] = poly
        else:
            before = sum_ref[...]
            sum_ref[...] = here * before + scale * poly + mm(low, before.astype(BF16))
            scale = scale * here
        if step + 1 < GRAM_STEPS:
            square = 2.0 * here * poly + mm(low, low)
            square_ref[...] = square.astype(BF16)
            twice = here * here
            rest = twice * rest.astype(F32) + shift * square + mm(square_ref[...], rest)
            more = jnp.sum(jnp.where(diagonal, rest, 0.0)) * (1.0 / D)
            rest_ref[...] = jnp.where(diagonal, rest - more, rest).astype(BF16)
            shift = twice * shift + more
    return scale


def orthogonalize_wide(layout, hidden):
    count = layout.tensor
    width = count * hidden

    def body(info_ref, *refs):
        pieces = refs[:count]
        out_ref, low, rest, poly, square, total_ref, sem = refs[count:]
        total = jnp.zeros((), F32)
        own = pltpu.make_async_copy(pieces[-1], low.at[:, 0:hidden], sem)
        own.start()
        for index in reversed(range(count)):
            cols = slice(index * hidden, (index + 1) * hidden)
            if index == 0:
                own.wait()
                part = low[:, cols]
            else:
                part = pieces[index - 1][...]
                low[:, cols] = part
            values = part.astype(F32)
            total = total + jnp.sum(values * values)
        inverse = 1.0 / (jnp.sqrt(total) + 1e-07)
        ratio = inverse * inverse
        shift = total * ratio * (1.0 / D)
        gram_rest(low, rest, ratio, shift)
        scale = gram_sweeps(rest, poly, square, total_ref, shift)
        poly[...] = (inverse * total_ref[...]).astype(BF16)
        apply_factor(low, poly, inverse * scale, width)
        for step in range(GRAM_STEPS, NS_STEPS):
            sweep(low, rest, poly, width, width if step + 1 < NS_STEPS else hidden)
        out_ref[...] = low[:, 0:hidden]

    return whole_kernel(
        body,
        low_shape(D, hidden),
        scratch=[pltpu.VMEM((D, width), BF16)]
        + [pltpu.VMEM((D, D), BF16)] * 3
        + [pltpu.VMEM((D, D), F32), pltpu.SemaphoreType.DMA],
        flops=30 * UNIT,
        moved=3 << 20,
        name="orthogonalize_wide",
    )


def wide_shard(hidden):
    def body(info_ref, expand_far, contract_far, out_ref, block, sem):
        @pl.when(info_ref[0] == 0)
        def _():
            copy = pltpu.make_async_copy(expand_far, block.at[:, 0:hidden], sem)
            copy.start()
            copy.wait()
            out_ref[...] = block[:, 0:hidden].astype(BF16)

        @pl.when(info_ref[0] != 0)
        def _():
            copy = pltpu.make_async_copy(contract_far, block.at[0:hidden, :], sem)
            copy.start()
            copy.wait()
            out_ref[...] = block[0:hidden, :].T.astype(BF16)

    return whole_kernel(
        body,
        low_shape(D, hidden),
        scratch=[pltpu.VMEM((D, D), F32), pltpu.SemaphoreType.DMA],
        moved=3 << 20,
        name="wide_shard",
    )


def fence(values, after, space=pl.ANY):
    def body(source_ref, *refs):
        pass

    return pl.pallas_call(
        body,
        out_shape=jax.ShapeDtypeStruct(values.shape, values.dtype),
        in_specs=[pl.BlockSpec(memory_space=pl.ANY)] * (1 + len(after)),
        out_specs=pl.BlockSpec(memory_space=pl.ANY),
        input_output_aliases={0: 0},
        name="fence",
    )(values, *after)


def halves_sum(layout, kept, got, name, after=()):
    half = kept.shape[0] // 2

    def body(info_ref, kept_ref, got_ref, upper_ref, lower_ref):
        for position in range(half):
            for ref, at in ((upper_ref, half + position), (lower_ref, position)):
                ref[position] = (kept_ref[at].astype(F32) + got_ref[at].astype(F32)).astype(BF16)

    part = low_shape(half, *kept.shape[1:])
    return whole_kernel(body, (part, part), moved=4 * kept.size, name=name)(
        kept, got, after=after
    )


def nest_of(grad, momentum):
    return (1.0 + MOMENTUM_DECAY) * grad + MOMENTUM_DECAY * MOMENTUM_DECAY * momentum


def wide_nest(layout, hidden):
    count = layout.planes

    def body(info_ref, got_ref, momentum_ref, out_ref):
        total = sum(got_ref[plane].astype(F32) for plane in range(count))
        nest = nest_of(total, momentum_ref[...]).astype(BF16)
        for plane in range(count):
            out_ref[plane] = nest

    return whole_kernel(
        body, low_shape(count, D // count, hidden), moved=1 << 20, name="wide_nest"
    )


def wide_slots_sum(layout, hidden):
    def body(info_ref, kept_ref, got_ref, out_ref):
        out_ref[...] = (kept_ref[0].astype(F32) + got_ref[0].astype(F32)).astype(BF16)

    shape = low_shape(layout.planes, D // layout.planes, hidden)
    return whole_kernel(body, shape, moved=1 << 20, name="wide_slots_sum")


def attention_slots(layout):
    rows, planes, width = layout.rows, layout.planes, layout.width

    def body(info_ref, cross_ref, cross_got, self_ref, self_got, out_ref):
        for slot in range(planes):
            for start, kept, got in ((0, cross_ref, cross_got), (rows, self_ref, self_got)):
                total = kept[0, slot].astype(F32) + got[0, slot].astype(F32)
                out_ref[slot, start : start + total.shape[0], :] = total.astype(BF16)

    return whole_kernel(
        body,
        low_shape(planes, 2 * rows + NORM_ROWS, width),
        moved=2 << 20,
        name="attention_slots",
    )


def attention_nest(layout):
    rows, planes, width = layout.rows, layout.planes, layout.width

    def body(info_ref, got_ref, momentum_far, mine_ref, other_ref, grad_ref, norm_ref, *refs):
        momentum, sems = refs
        first_core, tensor, copies = info_ref[0] == 0, info_ref[2], Copies(sems)
        cols = slice(None)
        if layout.parts > 1:
            part = lax.rem(tensor, layout.parts) * width
            cols = pl.ds(pl.multiple_of(part, width), width)
        moving = [
            copies.start(
                momentum_far.at[group * GROUP + lax.div(tensor, layout.parts), :, cols],
                momentum.at[index],
            )
            for index, group in enumerate((1, 0))
        ]
        total = sum(got_ref[plane].astype(F32) for plane in range(planes))
        wait_all(moving)
        cross = nest_of(total[0:rows], momentum[0]).astype(BF16)
        own = nest_of(total[rows : 2 * rows], momentum[1]).astype(BF16)
        mine_ref[...] = jnp.where(first_core, own, cross)
        other_ref[...] = jnp.where(first_core, cross, own)
        grad_ref[...] = total[0 : 2 * rows].astype(BF16)
        norm_ref[...] = total[2 * rows : 2 * rows + 8]

    one = low_shape(rows, width)
    return whole_kernel(
        body,
        (one, one, low_shape(2 * rows, width), wide_shape(8, width)),
        scratch=[pltpu.VMEM((2, rows, width), F32), pltpu.SemaphoreType.DMA((2,))],
        moved=2 << 20,
        name="attention_nest",
    )


def attention_pair(layout):
    rows, planes = layout.rows, layout.planes

    def body(info_ref, mine_ref, got_ref, out_ref):
        first_core = info_ref[0] == 0
        mine, got = mine_ref[...], got_ref[...]
        for plane in range(planes):
            out_ref[plane, 0:rows, :] = jnp.where(first_core, mine, got)
            out_ref[plane, rows : 2 * rows, :] = jnp.where(first_core, got, mine)

    return whole_kernel(
        body, low_shape(planes, 2 * rows, layout.width), moved=1 << 20, name="attention_pair"
    )


def wide_momentum(layout, hidden):
    piece_rows = D // layout.planes

    def body(info_ref, expand_ref, contract_ref, out_ref, turned):
        rows = pl.ds(pl.multiple_of(info_ref[1] * piece_rows, piece_rows), piece_rows)
        turned[...] = contract_ref[...].T
        out_ref[...] = jnp.where(info_ref[0] == 0, expand_ref[rows, :], turned[rows, :])

    return whole_kernel(
        body,
        wide_shape(piece_rows, hidden),
        scratch=[pltpu.VMEM((D, hidden), F32)],
        moved=3 << 20,
        name="wide_momentum",
    )


def decayed(master, share, scale):
    return master - MUON_RATE * (MUON_DECAY * master + scale * share)


def finish_wide(layout, hidden, full_hidden):
    scale = 0.2 * math.sqrt(max(D, full_hidden))

    def body(info_ref, mine_ref, other_ref, expand_ref, contract_ref, *refs):
        e_new, e_low, c_new, c_low = refs
        first = info_ref[0] == 0
        mine, other = mine_ref[...], other_ref[...]
        new = decayed(expand_ref[...], jnp.where(first, mine, other).astype(F32), scale)
        e_new[...] = new
        e_low[...] = new.astype(BF16)
        new = decayed(contract_ref[...], jnp.where(first, other, mine).T.astype(F32), scale)
        c_new[...] = new
        c_low[...] = new.astype(BF16)

    return whole_kernel(
        body,
        (wide_shape(D, hidden), low_shape(D, hidden), wide_shape(hidden, D), low_shape(hidden, D)),
        moved=6 << 20,
        name="finish_wide",
    )


def wide_velocity(layout, hidden):
    grad_share = 1.0 / (1.0 + MOMENTUM_DECAY)
    momentum_share = MOMENTUM_DECAY - MOMENTUM_DECAY * MOMENTUM_DECAY * grad_share

    def body(info_ref, mine_ref, other_ref, expand_ref, contract_ref, e_new, c_new, token):
        token[...] = jnp.zeros_like(token)
        first = info_ref[0] == 0
        mine, other = mine_ref[...], other_ref[...]
        nest = jnp.where(first, mine, other).astype(F32)
        e_new[...] = momentum_share * expand_ref[...] + grad_share * nest
        nest = jnp.where(first, other, mine).T.astype(F32)
        c_new[...] = momentum_share * contract_ref[...] + grad_share * nest

    return whole_kernel(
        body,
        (wide_shape(D, hidden), wide_shape(hidden, D), wide_shape(8, 128)),
        moved=6 << 20,
        name="wide_velocity",
    )


def owner_columns(info_ref, layout, position, other=False):
    owner = owner_at(info_ref, layout, position, other)
    if layout.parts == 1:
        return owner, slice(None)
    part = lax.rem(owner, layout.parts) * layout.width
    return lax.div(owner, layout.parts), pl.ds(pl.multiple_of(part, layout.width), layout.width)


def attention_velocity(layout):
    count, rows = layout.tensor, layout.rows

    def body(info_ref, *refs):
        momentum_ref, velocity_ref = refs[count:]
        for position in range(count):
            matrix, cols = owner_columns(info_ref, layout, position)
            for group in range(2):
                index, start = group * GROUP + matrix, (1 - group) * rows
                grad = refs[position][start : start + rows, :].astype(F32)
                velocity_ref[index, :, cols] = (
                    MOMENTUM_DECAY * momentum_ref[index, :, cols] + grad
                )

    return whole_kernel(
        body, wide_shape(2 * GROUP, rows, D), moved=3 << 20, name="attention_velocity"
    )


def finish_attention(layout):
    count = layout.tensor
    scale = 0.2 * math.sqrt(D)

    def body(info_ref, *refs):
        late = refs[:count]
        master_ref, new_ref, low_ref = refs[count:]
        for position in range(count):
            matrix, cols = owner_columns(info_ref, layout, position)
            for group in range(2):
                index = group * GROUP + matrix
                at = info_ref[0] if group == 0 else 1 - info_ref[0]
                new = decayed(
                    master_ref[index, :, cols], late[position][at].astype(F32), scale
                )
                new_ref[index, :, cols] = new
                low_ref[index, :, cols] = new.astype(BF16)

    shape = (2 * GROUP, layout.rows, D)
    return whole_kernel(
        body, (wide_shape(*shape), low_shape(*shape)), moved=4 << 20, name="finish_attention"
    )


def finish_norms(layout):
    def body(info_ref, grad_ref, params_ref, first_ref, second_ref, new, first_new, second_new):
        grad = grad_ref[0:6, 0 : layout.rows]
        first = BETA_FIRST * first_ref[...] + (1.0 - BETA_FIRST) * grad
        second = BETA_SECOND * second_ref[...] + (1.0 - BETA_SECOND) * grad * grad
        corrected = first / (1.0 - BETA_FIRST**STEP)
        denominator = jnp.sqrt(second / (1.0 - BETA_SECOND**STEP)) + ADAM_EPSILON
        new[...] = params_ref[...] - ADAM_RATE * corrected / denominator
        first_new[...] = first
        second_new[...] = second

    return whole_kernel(body, (wide_shape(6, layout.rows),) * 3, moved=1 << 14, name="norms")


def device_program(layout, arguments):
    (
        inputs,
        encoder,
        dec_segments,
        enc_segments,
        cotangent,
        attn_master,
        attn_momentum,
        expand_master,
        expand_momentum,
        contract_master,
        contract_momentum,
        norm_params,
        first_moments,
        second_moments,
    ) = arguments
    tokens, states = inputs.shape[1], encoder.shape[1]
    hidden = expand_master.shape[1]
    full_hidden = hidden * layout.tensor
    dp_at, tensor_at = lax.axis_index("dp"), lax.axis_index("tensor")
    x, enc, cot = inputs[0], encoder[0], cotangent[0]

    if layout.quad:
        shard = wide_shard(hidden)(far=[expand_master, contract_master])
        chunk = weight_chunk(layout, 0, "self_chunk", 1)(
            norm_params, far=[attn_master], after=[shard]
        )
        near = send(shard, layout.inplane(0))
        cross_own = cross_rows(layout)(far=[attn_master], after=[near])
        first, second, tile = self_split(layout)(*send_planes(layout, chunk), after=[cross_own])
        cross_own = exchange_planes(layout, fence(cross_own, [tile]))
        got_first = send(first, layout.plain_inplane(1))
        got_second = send(second, layout.plain_inplane(2))
        tiles = [tile, swap_cores(layout, tile)]
        a_saved, a, gains = first_norm(tokens)(*tiles, far=[x])
        got_first, got_second = fence(got_first, [a]), fence(got_second, [a])
        self_own = [first, second, got_first, got_second]
        self_pieces = self_own + [swap_cores(layout, piece) for piece in self_own]
        near = fence(near, [got_first])
        far = send(fence(shard, [got_first]), layout.inplane(1))
        farthest = send(near, layout.inplane(1))
        before = []
    else:
        low = attn_master.astype(BF16)
        norm_low = lax.all_gather(norm_params.astype(BF16), "dp", axis=1, tiled=True)
        padded = jnp.concatenate([norm_low, jnp.zeros((NORM_ROWS - 6, D), BF16)])
        self_low = lax.all_gather(low[:GROUP], "dp", axis=1, tiled=True)
        cross_low = lax.all_gather(low[GROUP:], "dp", axis=1, tiled=True)
        self_pieces, before = [self_low], []
        tiles = [padded, jnp.zeros_like(padded)]
        shard = wide_shard(hidden)(far=[expand_master, contract_master])
        wide_own = gather_inplane(layout, shard)
        wide_other = [swap_cores(layout, piece) for piece in wide_own]

    dec_row, dec_column = dec_segments.reshape(1, tokens), dec_segments.reshape(tokens, 1)
    enc_column = enc_segments.reshape(states, 1)
    if not layout.quad:
        a_saved, a, gains = first_norm(tokens)(*tiles, far=[x])
    w_self, q, k, v, self_prob, self_mix, mid, c = self_forward(layout, tokens)(
        a, gains, dec_row, dec_column, far=[x, *self_pieces], after=before
    )
    if layout.quad:
        far, farthest = fence(far, [c]), fence(farthest, [c])
        cross_own = fence(cross_own, [far, farthest])
        cross_pieces = [cross_own, swap_cores(layout, cross_own)]
        wide_own = [shard, near, far, farthest]
        wide_other = [swap_cores(layout, piece) for piece in wide_own]
    else:
        cross_pieces = [cross_low]
    w_cross, qc, kc, vc, cross_prob, cross_mix, late, f = cross_forward(layout, tokens, states)(
        c, gains, dec_row, enc_column, far=[enc, mid, *cross_pieces], after=[wide_own[-1]]
    )
    w_in, w_out, post, d_pre, wide_keep, wide_send = feed_forward(layout, tokens, hidden)(
        f, far=[cot, *wide_own, *wide_other]
    )
    output, grad_late, late_low, norm_three = feed_forward_sums(layout, tokens, hidden)(
        w_in, w_out, post, d_pre, late, gains, far=[cot]
    )
    top = layout.bits - 1
    upper, lower = halves_sum(
        layout, wide_keep, swap_cores(layout, wide_send), "wide_sum", after=[late_low]
    )
    encoder_grad, grad_mid, mid_low, norm_two, cross_keep, cross_send = cross_backward(
        layout, tokens, states
    )(
        late_low, cross_mix, grad_late, gains, qc, kc, vc, cross_prob, c, w_cross,
        far=[enc, mid], after=[upper],
    )
    got = send(upper, layout.inplane(top))
    for bit in reversed(range(top)):
        upper, lower = halves_sum(layout, lower, got, "wide_sum", after=[mid_low])
        got = send(upper, layout.inplane(bit))
    cross_upper, cross_lower = halves_sum(
        layout, cross_keep, swap_cores(layout, cross_send), "cross_sum", after=[upper]
    )
    got_cross = send(cross_upper, layout.inplane(top))
    self_out_grad, dq, dk, dv = self_attention_back(layout, tokens)(
        mid_low, w_self, self_mix, q, k, v, self_prob, after=[upper, cross_upper]
    )
    input_grad, self_keep, self_send = self_backward(layout, tokens)(
        self_out_grad, dq, dk, dv, grad_mid, gains, norm_two, norm_three,
        w_self, a_saved, x,
    )
    wide_slots = wide_slots_sum(layout, hidden)(lower, got, after=[self_keep])
    wide_got = exchange_planes(layout, wide_slots)
    self_upper, self_lower = halves_sum(
        layout, self_keep, swap_cores(layout, fence(self_send, [wide_slots])), "self_sum"
    )
    momentum = wide_momentum(layout, hidden)(expand_momentum, contract_momentum)
    got_self = send(self_upper, layout.inplane(top))
    for bit in reversed(range(top)):
        cross_upper, cross_lower = halves_sum(layout, cross_lower, got_cross, "cross_sum")
        got_cross = send(cross_upper, layout.inplane(bit))
    nest_rows = wide_nest(layout, hidden)(wide_got, momentum, after=[self_upper, cross_upper])
    nest = exchange_planes(layout, nest_rows).reshape(D, hidden)
    for bit in reversed(range(top)):
        self_upper, self_lower = halves_sum(layout, self_lower, got_self, "self_sum")
        got_self = send(self_upper, layout.inplane(bit))
    rows_by_slot = attention_slots(layout)(cross_lower, got_cross, self_lower, got_self)
    nest = fence(nest, [rows_by_slot])
    nest_other = swap_cores(layout, nest)
    expand_velocity, contract_velocity, velocity_done = wide_velocity(layout, hidden)(
        nest, nest_other, expand_momentum, contract_momentum
    )
    nest_pieces = gather_inplane(
        layout, nest, lambda piece: fence(piece, [rows_by_slot, velocity_done])
    )
    nest_mine, nest_others, attn_grad, norm_rows = attention_nest(layout)(
        exchange_planes(layout, rows_by_slot), far=[attn_momentum], after=[nest_pieces[layout.tensor // 2 - 1]]
    )

    attn_nest = attention_pair(layout)(nest_mine, swap_cores(layout, nest_others))
    early = gather_inplane_direct(layout, attn_grad)

    def whole_pieces(piece):
        gathered = [piece]
        for bit in range(layout.parts.bit_length() - 1):
            pairs = layout.pairs(lambda d, t: d * layout.tensor + (t ^ (1 << bit)))
            gathered = gathered + [send(one, pairs) for one in gathered]
        return gathered

    wide_ortho = orthogonalize_wide(layout, hidden)(
        *nest_pieces[1:], far=nest_pieces[:1], after=[attn_nest])
    whole = exchange_planes(layout, attn_nest).reshape(D, layout.width)
    mine, others = orthogonalize_attention(layout)(
        *whole_pieces(whole), after=[wide_ortho, *early[1:]]
    )
    late_pieces = gather_inplane_direct(layout, jnp.stack([mine, swap_cores(layout, others)]))
    attn_velocity = attention_velocity(layout)(*early, attn_momentum)
    norm_updated, first_updated, second_updated = finish_norms(layout)(
        norm_rows, norm_params, first_moments, second_moments
    )

    expand_updated, expand_copy, contract_updated, contract_copy = finish_wide(
        layout, hidden, full_hidden
    )(wide_ortho, swap_cores(layout, wide_ortho), expand_master, contract_master)
    attn_updated, attn_copy = finish_attention(layout)(
        *late_pieces, attn_master
    )
    return (
        output[None],
        input_grad[None],
        encoder_grad[None],
        attn_updated,
        attn_velocity,
        attn_copy,
        expand_updated,
        expand_velocity,
        expand_copy,
        contract_updated,
        contract_velocity,
        contract_copy,
        norm_updated,
        first_updated,
        second_updated,
    )


def solution(mesh):
    layout = Layout(mesh.shape["dp"], mesh.shape["tensor"])

    def local(*arguments):
        return device_program(layout, arguments)

    rows = P(AXES, None, None)
    by_dp, by_column, by_row, norm = P(None, "dp", None), P(None, "tensor"), P("tensor", None), P(None, "dp")
    return jax.shard_map(
        local,
        mesh=mesh,
        in_specs=(rows, rows, P(AXES, None), P(AXES, None), rows)
        + (by_dp, by_dp, by_column, by_column, by_row, by_row, norm, norm, norm),
        out_specs=(rows, rows, rows, by_dp, by_dp, by_dp)
        + (by_column, by_column, by_column, by_row, by_row, by_row, norm, norm, norm),
        check_vma=False,
    )
```

```python
import functools
import math

import jax
import jax.numpy as jnp
from jax import lax
from jax.experimental import pallas as pl
from jax.experimental.pallas import tpu as pltpu
from jax.sharding import PartitionSpec as P

D = 512
HEADS = 8
HEAD = D // HEADS
PAIR = 2 * HEAD
NS_STEPS = 5
GRAM_STEPS = 3
STEP = 10

MASKED_SCORE = -1e30
NORM_EPSILON = 1e-05
MOMENTUM_DECAY = 0.95
MUON_RATE = 0.15
MUON_DECAY = 0.01
POLY_FIRST = 3.4445
POLY_SECOND = -4.775
POLY_THIRD = 2.0315
ADAM_RATE = 0.4
BETA_FIRST = 0.9
BETA_SECOND = 0.999
ADAM_EPSILON = 1e-08
GROUP = 4
QUERY_BLOCK = 512

F32 = jnp.float32
BF16 = jnp.bfloat16
AXES = ("dp", "tensor")
MIB = 1 << 20
VMEM_BYTES = 24 * MIB
NORM_ROWS = 16


def mm(left, right):
    return lax.dot_general(left, right, (((1,), (0,)), ((), ())), preferred_element_type=F32)


def mm_nt(left, right):
    return lax.dot_general(left, right, (((1,), (1,)), ((), ())), preferred_element_type=F32)


def mm_tn(left, right):
    return lax.dot_general(left, right, (((0,), (0,)), ((), ())), preferred_element_type=F32)


def normalized(values):
    average = jnp.mean(values, -1, keepdims=True)
    centred = values - average
    inv_std = lax.rsqrt(jnp.mean(centred * centred, -1, keepdims=True) + NORM_EPSILON)
    return centred * inv_std, inv_std


def norm_backward(incoming, values, gain_row):
    normed, inv_std = normalized(values)
    scaled = incoming * gain_row
    inner = (
        scaled
        - jnp.mean(scaled, -1, keepdims=True)
        - normed * jnp.mean(scaled * normed, -1, keepdims=True)
    )
    gain_grad = jnp.sum(incoming * normed, 0, keepdims=True)
    shift_grad = jnp.sum(incoming, 0, keepdims=True)
    return inner * inv_std, gain_grad, shift_grad


def head_mask(half, value):
    lane = lax.broadcasted_iota(jnp.int32, (1, PAIR), 1)
    inside = jnp.logical_and(lane >= half * HEAD, lane < (half + 1) * HEAD)
    return jnp.where(inside, value, 0.0).astype(BF16)


def pair_columns(pair):
    return pl.ds(pl.multiple_of(pair * PAIR, PAIR), PAIR)


def attend(q_ref, k_ref, v_ref, key_seg_ref, query_seg_ref, prob_ref, out_ref, done):
    queries = q_ref.shape[0]
    block = min(QUERY_BLOCK, queries)

    def one_pair(pair, carry):
        cols = pair_columns(pair)
        keys, values = k_ref[:, cols], v_ref[:, cols]
        for start in range(0, queries, block):
            rows = pl.ds(start, block)
            query = q_ref[rows, cols]
            allowed = key_seg_ref[...] == query_seg_ref[:, rows]
            total = None
            for half in range(2):
                scores = mm_nt(keys * head_mask(half, HEAD**-0.5), query)
                scores = jnp.where(allowed, scores, MASKED_SCORE)
                peak = jnp.max(scores, 0, keepdims=True)
                weights = jnp.exp(scores - peak)
                soft = (weights * (1.0 / jnp.sum(weights, 0, keepdims=True))).astype(BF16)
                prob_ref[pair * 2 + half, :, rows] = soft
                part = mm_tn(soft, values * head_mask(half, 1.0))
                total = part if total is None else total + part
            out_ref[rows, cols] = total.astype(BF16)
        done(pair)
        return carry

    lax.fori_loop(0, HEADS // 2, one_pair, 0)


def attend_back(q_ref, k_ref, v_ref, prob_ref, grad_ref, dq_ref, dk_ref, dv_ref, ready):
    queries = q_ref.shape[0]
    block = min(QUERY_BLOCK, queries)
    scaling = HEAD**-0.5

    def one_pair(pair, carry):
        cols = pair_columns(pair)
        keys, values = k_ref[:, cols], v_ref[:, cols]
        key_sum = value_sum = None
        ready(pair)
        for start in range(0, queries, block):
            rows = pl.ds(start, block)
            query, grad = q_ref[rows, cols], grad_ref[rows, cols]
            query_sum = None
            for half in range(2):
                mask = head_mask(half, 1.0)
                soft = prob_ref[pair * 2 + half, :, rows]
                weights = soft.astype(F32)
                grad_soft = mm_nt(values * mask, grad)
                product = weights * grad_soft
                inner = jnp.sum(product, 0, keepdims=True)
                grad_scores = (product - weights * inner).astype(BF16)
                value_part = mm(soft, grad * mask)
                key_part = mm(grad_scores, query * mask)
                query_part = mm_tn(grad_scores, keys * mask)
                value_sum = value_part if value_sum is None else value_sum + value_part
                key_sum = key_part if key_sum is None else key_sum + key_part
                query_sum = query_part if query_sum is None else query_sum + query_part
            dq_ref[rows, cols] = (query_sum * scaling).astype(BF16)
        dk_ref[:, cols] = (key_sum * scaling).astype(BF16)
        dv_ref[:, cols] = value_sum.astype(BF16)
        return carry

    lax.fori_loop(0, HEADS // 2, one_pair, 0)


def pair_copy(source, target, sems, pair):
    heads = pl.ds(pair * 2, 2)
    return pltpu.make_async_copy(source.at[heads], target.at[heads], sems.at[pair])


def reorder(core, position, bits):
    if core == 0:
        return position
    return sum(((position >> bit) & 1) << (bits - 1 - bit) for bit in range(bits))


class Layout:
    def __init__(self, dp_size, tensor_size):
        self.dp, self.tensor = dp_size, tensor_size
        self.bits = tensor_size.bit_length() - 1
        self.planes = dp_size // 2
        self.parts = tensor_size // GROUP
        self.rows = D // dp_size
        self.quad = tensor_size == 4
        self.width = D // self.parts

    def pairs(self, move):
        return [
            (d * self.tensor + t, move(d, t)) for d in range(self.dp) for t in range(self.tensor)
        ]

    def inplane(self, bit):
        return self.pairs(
            lambda d, t: d * self.tensor + (t ^ reorder(d & 1, 1 << bit, self.bits))
        )

    def inplane_position(self, position):
        return self.pairs(
            lambda d, t: d * self.tensor + (t ^ reorder(d & 1, position, self.bits))
        )

    def plain_inplane(self, offset):
        return self.pairs(lambda d, t: d * self.tensor + (t ^ offset))

    def plane(self, slot):
        return self.pairs(lambda d, t: (d ^ (2 * slot)) * self.tensor + t)

    def other_core(self):
        return self.pairs(lambda d, t: (d ^ 1) * self.tensor + t)


def send(values, pairs):
    return lax.ppermute(values, AXES, pairs)


def gather_inplane(layout, piece, forwarded=None):
    pieces = [piece]
    for bit in range(layout.bits):
        if forwarded is not None and bit + 1 == layout.bits:
            pieces = pieces[:1] + [forwarded(one) for one in pieces[1:]]
        pieces = pieces + [send(one, layout.inplane(bit)) for one in pieces]
    return pieces


def gather_inplane_direct(layout, piece):
    return [piece] + [
        send(piece, layout.inplane_position(position)) for position in range(1, layout.tensor)
    ]


def send_planes(layout, piece):
    return [piece] + [send(piece, layout.plane(slot)) for slot in range(1, layout.planes)]


def exchange_planes(layout, pieces):
    groups = [list(range(core, layout.dp, 2)) for core in range(2)]
    return lax.all_to_all(pieces, "dp", 0, 0, axis_index_groups=groups, tiled=True)


def exchange_inplane(pieces):
    return lax.all_to_all(pieces, "tensor", 0, 0, tiled=True)


def swap_cores(layout, values):
    return send(values, layout.other_core())


def whole_kernel(body, out_shape, scratch=(), flops=0, moved=0, name=None, far_outs=0):
    out_specs = jax.tree.map(lambda _: pl.BlockSpec(memory_space=pltpu.VMEM), out_shape)
    shapes = out_shape
    if far_outs:
        out_specs = (pl.BlockSpec(memory_space=pltpu.HBM),) * far_outs + out_specs[far_outs:]
        shapes = tuple(pltpu.HBM(one.shape, one.dtype) for one in out_shape[:far_outs])
        shapes = shapes + out_shape[far_outs:]

    def call(*operands, far=(), loose=(), after=()):
        near = len(operands)
        operands = operands + tuple(far) + tuple(loose)
        read = len(operands)

        def without_after(*refs):
            place = lax.axis_index("dp"), lax.axis_index("tensor")
            info = (place[0] % 2, place[0] // 2, place[1])
            body(info, *refs[:read], *refs[read + len(after) :])

        operands = operands[:near] + tuple(
            pltpu.with_memory_space_constraint(one, pltpu.HBM) for one in far
        ) + tuple(loose)
        return pl.pallas_call(
            without_after,
            out_shape=shapes,
            in_specs=[pl.BlockSpec(memory_space=pltpu.VMEM)] * near
            + [pl.BlockSpec(memory_space=pltpu.HBM)] * len(far)
            + [pl.BlockSpec(memory_space=pl.ANY)] * (len(loose) + len(after)),
            out_specs=out_specs,
            scratch_shapes=list(scratch),
            compiler_params=pltpu.CompilerParams(vmem_limit_bytes=VMEM_BYTES),
            cost_estimate=pl.CostEstimate(flops=flops, bytes_accessed=moved, transcendentals=0),
            name=name,
        )(*operands, *after)

    return call


class Copies:
    def __init__(self, sems):
        self.sems, self.count = sems, 0

    def start(self, source, target):
        copy = pltpu.make_async_copy(source, target, self.sems.at[self.count])
        copy.start()
        self.count += 1
        return copy


def wait_all(copies):
    for copy in copies:
        copy.wait()


def low_shape(*shape):
    return jax.ShapeDtypeStruct(shape, BF16)


def wide_shape(*shape):
    return jax.ShapeDtypeStruct(shape, F32)


UNIT = 2 * D * D * D


def owner_at(info_ref, layout, position, other=False):
    core = info_ref[0]
    first = 1 if other else 0
    offset = jnp.where(
        core == first, reorder(0, position, layout.bits), reorder(1, position, layout.bits)
    )
    return jnp.bitwise_xor(info_ref[2], offset)


def row_start(info_ref, layout, plane, other=False):
    core = 1 - info_ref[0] if other else info_ref[0]
    return pl.multiple_of((plane * 2 + core) * layout.rows, layout.rows)


def quad_matrix(info_ref, position):
    tensor = info_ref[2]
    side = jnp.bitwise_xor(lax.rem(tensor, 2), lax.div(tensor, 2))
    return jnp.bitwise_xor(side, position // 2) * 2 + position % 2


def weight_chunk(layout, group, name, copies_out):
    rows = layout.rows
    tiles = NORM_ROWS if group == 0 else 0

    def body(info_ref, norm_ref, source_ref, out_ref, tile, blocks, sems):
        copies = Copies(sems)
        moving = [
            copies.start(
                source_ref.at[group * GROUP + quad_matrix(info_ref, position)],
                blocks.at[position],
            )
            for position in range(2)
        ]
        if tiles:
            tile[...] = jnp.zeros_like(tile)
            for block in range(layout.dp):

                @pl.when(info_ref[1] * 2 + info_ref[0] == block)
                def _():
                    tile[0:6, block * rows : (block + 1) * rows] = norm_ref[...]

            for plane in range(copies_out):
                out_ref[plane, 2 * rows :, :] = tile[...].astype(BF16)
        wait_all(moving)
        for index in range(2):
            block = blocks[index].astype(BF16)
            for plane in range(copies_out):
                out_ref[plane, index * rows : (index + 1) * rows, :] = block

    return whole_kernel(
        body,
        low_shape(copies_out, 2 * rows + tiles, D),
        scratch=[
            pltpu.VMEM((NORM_ROWS, D), F32),
            pltpu.VMEM((2, rows, D), F32),
            pltpu.SemaphoreType.DMA((2,)),
        ],
        moved=1 << 20,
        name=name,
    )


def self_split(layout):
    rows, planes = layout.rows, layout.planes

    def body(info_ref, *refs):
        slots, outs, tile_ref = refs[:planes], refs[planes : planes + 2], refs[-1]
        tile = None
        for slot, ref in enumerate(slots):
            plane = jnp.bitwise_xor(info_ref[1], slot)
            for index in range(2):
                outs[index][plane] = ref[0, index * rows : (index + 1) * rows, :]
            part = ref[0, 2 * rows :, :].astype(F32)
            tile = part if tile is None else tile + part
        tile_ref[...] = tile.astype(BF16)

    one = low_shape(planes, rows, D)
    return whole_kernel(
        body, (one, one, low_shape(NORM_ROWS, D)), moved=2 << 20, name="self_split"
    )


def cross_rows(layout):
    rows, planes = layout.rows, layout.planes

    def body(info_ref, source_far, out_ref, blocks, sem):
        copy = pltpu.make_async_copy(source_far.at[GROUP : 2 * GROUP], blocks, sem)
        copy.start()
        copy.wait()
        for matrix in range(GROUP):
            block = blocks[matrix].astype(BF16)
            for plane in range(planes):
                out_ref[plane, matrix * rows : (matrix + 1) * rows, :] = block

    return whole_kernel(
        body,
        low_shape(planes, GROUP * rows, D),
        scratch=[pltpu.VMEM((GROUP, rows, D), F32), pltpu.SemaphoreType.DMA],
        moved=2 << 20,
        name="cross_rows",
    )


def fetch_weights(info_ref, layout, refs, weights_ref, copies):
    if not layout.quad:
        return [copies.start(refs[0], weights_ref)]
    moving = []
    for index, ref in enumerate(refs):
        matrix = quad_matrix(info_ref, index % GROUP)
        for plane in range(layout.planes):
            at = pl.ds(row_start(info_ref, layout, plane, index >= GROUP), layout.rows)
            moving.append(copies.start(ref.at[plane], weights_ref.at[matrix, at, :]))
    return moving


def fetch_cross(info_ref, layout, refs, weights_ref, copies):
    if not layout.quad:
        return [[copies.start(refs[0], weights_ref)], [], [], []]
    moving, rows = [], layout.rows
    for matrix in range(GROUP):
        here = slice(matrix * rows, (matrix + 1) * rows)
        moving.append([])
        for index, ref in enumerate(refs):
            for plane in range(layout.planes):
                at = pl.ds(row_start(info_ref, layout, plane, index == 1), rows)
                moving[matrix].append(
                    copies.start(ref.at[plane, here, :], weights_ref.at[matrix, at, :])
                )
    return moving


def weight_pieces(layout):
    return (2 * GROUP, 2 * GROUP * layout.planes) if layout.quad else (1, 1)


def place_grads(info_ref, layout, grads_ref, keep_ref, send_ref):
    for other, ref in ((False, keep_ref), (True, send_ref)):
        for position in range(layout.tensor):
            owner = owner_at(info_ref, layout, position, other)
            for slot in range(layout.planes):
                rows = pl.ds(row_start(info_ref, layout, slot, other), layout.rows)
                if layout.parts == 1:
                    block = grads_ref[owner, rows, :]
                else:
                    part = lax.rem(owner, layout.parts) * layout.width
                    cols = pl.ds(pl.multiple_of(part, layout.width), layout.width)
                    block = grads_ref[lax.div(owner, layout.parts), rows, cols]
                ref[position, slot, 0 : layout.rows, :] = block


def first_norm(tokens):
    def body(info_ref, tile_ref, other_ref, x_far, a_out, a_ref, gains_ref, x_ref, sems):
        copies = Copies(sems)
        x_copy = copies.start(x_far, x_ref)
        gains_ref[...] = tile_ref[...].astype(F32) + other_ref[...].astype(F32)
        x_copy.wait()
        normed, _ = normalized(x_ref[...].astype(F32))
        a_ref[...] = (normed * gains_ref[0:1, :] + gains_ref[1:2, :]).astype(BF16)
        copies.start(a_ref, a_out).wait()

    return whole_kernel(
        body,
        (low_shape(tokens, D), low_shape(tokens, D), wide_shape(NORM_ROWS, D)),
        scratch=[pltpu.VMEM((tokens, D), BF16), pltpu.SemaphoreType.DMA((2,))],
        moved=1 << 20,
        name="first_norm",
        far_outs=1,
    )


def self_forward(layout, tokens):
    count, pieces = weight_pieces(layout)

    def body(info_ref, a_ref, gains_ref, query_seg_ref, key_seg_ref, x_far, *refs):
        w_out, q_out, k_out, v_out, prob_out, mix_out, mid_out, c_ref = refs[count : count + 8]
        x_ref, w_ref, q_ref, k_ref, v_ref, prob_ref, mix_ref, mid_ref = refs[count + 8 : -2]
        sems, pair_sems = refs[-2:]
        copies = Copies(sems)
        arriving = fetch_weights(info_ref, layout, refs[:count], w_ref, copies)
        x_copy = copies.start(x_far, x_ref)
        wait_all(arriving)
        leaving = [copies.start(w_ref, w_out)]
        for index, (ref, out) in enumerate(((q_ref, q_out), (k_ref, k_out), (v_ref, v_out))):
            ref[...] = mm(a_ref[...], w_ref[index]).astype(BF16)
            leaving.append(copies.start(ref, out))
        attend(
            q_ref, k_ref, v_ref, key_seg_ref, query_seg_ref, prob_ref, mix_ref,
            lambda pair: pair_copy(prob_ref, prob_out, pair_sems, pair).start(),
        )
        leaving.append(copies.start(mix_ref, mix_out))
        x_copy.wait()
        mid = x_ref[...].astype(F32) + mm(mix_ref[...], w_ref[3])
        mid_ref[...] = mid
        leaving.append(copies.start(mid_ref, mid_out))
        normed, _ = normalized(mid)
        c_ref[...] = (normed * gains_ref[2:3, :] + gains_ref[3:4, :]).astype(BF16)
        wait_all(leaving)
        for pair in range(HEADS // 2):
            pair_copy(prob_ref, prob_out, pair_sems, pair).wait()

    low, rows = low_shape(tokens, D), pltpu.VMEM((tokens, D), BF16)
    probs = (HEADS, tokens, tokens)
    return whole_kernel(
        body,
        (
            low_shape(GROUP, D, D),
            low,
            low,
            low,
            low_shape(*probs),
            low,
            wide_shape(tokens, D),
            low,
        ),
        scratch=[rows, pltpu.VMEM((GROUP, D, D), BF16), rows, rows, rows]
        + [pltpu.VMEM(probs, BF16), rows, pltpu.VMEM((tokens, D), F32)]
        + [pltpu.SemaphoreType.DMA((pieces + 8,)), pltpu.SemaphoreType.DMA((HEADS // 2,))],
        flops=14 * UNIT,
        moved=12 << 20,
        name="self_forward",
        far_outs=7,
    )


def cross_forward(layout, tokens, states):
    count, pieces = (2, weight_pieces(layout)[1]) if layout.quad else (1, 1)

    def body(info_ref, c_ref, gains_ref, query_seg_ref, key_seg_ref, enc_far, mid_far, *refs):
        w_ref, q_ref, k_ref, v_ref, prob_ref, mix_ref, late_ref, f_ref = refs[count : count + 8]
        enc_ref, mid_ref, sems = refs[count + 8 :]
        copies = Copies(sems)
        arriving = fetch_cross(info_ref, layout, refs[:count], w_ref, copies)
        arriving[1].append(copies.start(enc_far, enc_ref))
        mid_copy = copies.start(mid_far, mid_ref)
        for index, (source, ref) in enumerate(
            ((c_ref, q_ref), (enc_ref, k_ref), (enc_ref, v_ref))
        ):
            wait_all(arriving[index])
            ref[...] = mm(source[...], w_ref[index]).astype(BF16)
        attend(
            q_ref, k_ref, v_ref, key_seg_ref, query_seg_ref, prob_ref, mix_ref, lambda pair: None
        )
        mid_copy.wait()
        wait_all(arriving[3])
        late = mid_ref[...] + mm(mix_ref[...], w_ref[3])
        late_ref[...] = late
        normed, _ = normalized(late)
        f_ref[...] = (normed * gains_ref[4:5, :] + gains_ref[5:6, :]).astype(BF16)

    low = low_shape(tokens, D)
    return whole_kernel(
        body,
        (
            low_shape(GROUP, D, D),
            low,
            low_shape(states, D),
            low_shape(states, D),
            low_shape(HEADS, states, tokens),
            low,
            wide_shape(tokens, D),
            low,
        ),
        scratch=[pltpu.VMEM((states, D), BF16), pltpu.VMEM((tokens, D), F32)]
        + [pltpu.SemaphoreType.DMA((pieces + 2,))],
        flops=14 * UNIT,
        moved=12 << 20,
        name="cross_forward",
    )


def gelu_parts(pre):
    slope = math.sqrt(2.0 / math.pi)
    square = pre * pre
    bent = jnp.tanh(slope * pre * (1.0 + 0.044715 * square))
    half = 0.5 * (1.0 + bent)
    inner = slope * (1.0 + 3 * 0.044715 * square)
    return pre * half, half + 0.5 * pre * (1.0 - bent * bent) * inner


def feed_forward(layout, tokens, hidden):
    count, planes = layout.tensor, layout.planes
    piece_rows, full = D // planes, layout.tensor * hidden

    def body(info_ref, f_ref, cot_far, *refs):
        mine, others = refs[:count], refs[count : 2 * count]
        w_in, w_out, post_ref, d_pre_ref, keep_ref, send_ref = refs[2 * count : -5]
        cot_ref, f_t, cot_t, sems, cot_sem = refs[-5:]
        first_core = info_ref[0] == 0

        def columns(position):
            return slice(position * hidden, (position + 1) * hidden)

        def fetch(source, target, matrix, position):
            return pltpu.make_async_copy(
                source, target.at[:, columns(position)], sems.at[matrix, position]
            )

        cot_copy = pltpu.make_async_copy(cot_far, cot_ref, cot_sem)
        cot_copy.start()
        for position in range(count):
            turned = reorder(1, position, layout.bits)

            @pl.when(first_core)
            def _():
                fetch(mine[position], w_in, 0, position).start()
                fetch(others[turned], w_out, 1, position).start()

            @pl.when(jnp.logical_not(first_core))
            def _():
                fetch(others[position], w_in, 0, position).start()
                fetch(mine[turned], w_out, 1, position).start()

        f_t[...] = f_ref[...].T
        cot_copy.wait()
        cot_t[...] = cot_ref[...].T
        for position in range(count):
            cols = columns(position)
            fetch(mine[0], w_in, 0, position).wait()
            fetch(mine[0], w_out, 1, position).wait()
            pre = mm(f_ref[...], w_in[:, cols])
            grad_post = mm(cot_ref[...], w_out[:, cols])
            post, slope = gelu_parts(pre)
            post_ref[:, cols] = post.astype(BF16)
            d_pre_ref[:, cols] = (slope * grad_post).astype(BF16)
        for position in range(count):
            cols = columns(position)
            turned = reorder(1, position, layout.bits)
            keep_at = jnp.where(first_core, position, turned)
            send_at = jnp.where(first_core, turned, position)
            grad_in = mm(f_t[...], d_pre_ref[:, cols]).astype(BF16)
            grad_out = mm(cot_t[...], post_ref[:, cols]).astype(BF16)
            for slot in range(planes):
                part = slice(slot * piece_rows, (slot + 1) * piece_rows)
                keep_ref[keep_at, slot] = jnp.where(first_core, grad_in[part], grad_out[part])
                send_ref[send_at, slot] = jnp.where(first_core, grad_out[part], grad_in[part])

    pieces = low_shape(count, planes, piece_rows, hidden)
    return whole_kernel(
        body,
        (low_shape(D, full), low_shape(D, full), low_shape(tokens, full), low_shape(tokens, full))
        + (pieces, pieces),
        scratch=[
            pltpu.VMEM((tokens, D), BF16),
            pltpu.VMEM((D, tokens), BF16),
            pltpu.VMEM((D, tokens), BF16),
            pltpu.SemaphoreType.DMA((2, count)),
            pltpu.SemaphoreType.DMA,
        ],
        flops=4 * UNIT * full // D,
        moved=14 << 20,
        name="feed_forward",
    )


def feed_forward_sums(layout, tokens, hidden):
    def body(info_ref, w_in, w_out, post_ref, d_pre_ref, late_ref, gains_ref, cot_far, *refs):
        out_ref, glate_ref, dlate_ref, norm_ref, cot_ref, sem = refs
        cot_copy = pltpu.make_async_copy(cot_far, cot_ref, sem)
        cot_copy.start()
        late = late_ref[...]
        back = mm_nt(d_pre_ref[...], w_in[...])
        back, gain_grad, shift_grad = norm_backward(back, late, gains_ref[4:5, :])
        cot_copy.wait()
        grad_late = cot_ref[...].astype(F32) + back
        glate_ref[...] = grad_late
        dlate_ref[...] = grad_late.astype(BF16)
        norm_ref[0:1, :] = gain_grad
        norm_ref[1:2, :] = shift_grad
        out_ref[...] = (late + mm_nt(post_ref[...], w_out[...])).astype(BF16)

    low = low_shape(tokens, D)
    return whole_kernel(
        body,
        (low, wide_shape(tokens, D), low, wide_shape(2, D)),
        scratch=[pltpu.VMEM((tokens, D), BF16), pltpu.SemaphoreType.DMA],
        flops=2 * UNIT * layout.tensor * hidden // D,
        moved=4 << 20,
        name="feed_forward_sums",
    )


def cross_backward(layout, tokens, states):
    def body(info_ref, dlate_ref, mix_ref, glate_ref, gains_ref, *refs):
        q_ref, k_ref, v_ref, prob_ref, c_ref, w_ref, enc_far, mid_far = refs[:8]
        enc_grad_ref, gmid_ref, dmid_ref, norm_ref, keep_ref, send_ref = refs[8:14]
        enc_ref, mid_ref, dq, dk, dv, grads, d_mix, sems = refs[14:]
        copies = Copies(sems)
        later = [copies.start(enc_far, enc_ref), copies.start(mid_far, mid_ref)]
        d_mix[...] = mm_nt(dlate_ref[...], w_ref[3]).astype(BF16)
        grads[3] = mm_tn(mix_ref[...], dlate_ref[...]).astype(BF16)
        attend_back(
            q_ref, k_ref, v_ref, prob_ref, d_mix, dq, dk, dv, lambda pair: None
        )
        wait_all(later)
        grads[0] = mm_tn(c_ref[...], dq[...]).astype(BF16)
        enc_t = enc_ref[...].T
        grads[1] = mm(enc_t, dk[...]).astype(BF16)
        grads[2] = mm(enc_t, dv[...]).astype(BF16)
        place_grads(info_ref, layout, grads, keep_ref, send_ref)
        enc_grad_ref[...] = (mm_nt(dk[...], w_ref[1]) + mm_nt(dv[...], w_ref[2])).astype(BF16)
        back, gain_grad, shift_grad = norm_backward(
            mm_nt(dq[...], w_ref[0]), mid_ref[...], gains_ref[2:3, :]
        )
        grad_mid = glate_ref[...] + back
        gmid_ref[...] = grad_mid
        dmid_ref[...] = grad_mid.astype(BF16)
        norm_ref[0:1, :] = gain_grad
        norm_ref[1:2, :] = shift_grad

    low, rows = low_shape(tokens, D), pltpu.VMEM((tokens, D), BF16)
    keys = pltpu.VMEM((states, D), BF16)
    pieces = low_shape(layout.tensor, layout.planes, layout.rows, layout.width)
    return whole_kernel(
        body,
        (low_shape(states, D), wide_shape(tokens, D), low, wide_shape(2, D), pieces, pieces),
        scratch=[keys, pltpu.VMEM((tokens, D), F32), rows, keys, keys]
        + [pltpu.VMEM((GROUP, D, D), BF16), rows, pltpu.SemaphoreType.DMA((2,))],
        flops=26 * UNIT,
        moved=14 << 20,
        name="cross_backward",
    )


def self_attention_back(layout, tokens):
    def body(info_ref, dmid_ref, w_ref, mix_ref, q_ref, k_ref, v_ref, prob_ref, *refs):
        out_ref, dq, dk, dv, d_mix = refs
        d_mix[...] = mm_nt(dmid_ref[...], w_ref[3]).astype(BF16)
        attend_back(
            q_ref, k_ref, v_ref, prob_ref, d_mix, dq, dk, dv, lambda pair: None
        )
        out_ref[...] = mm_tn(mix_ref[...], dmid_ref[...]).astype(BF16)

    low = low_shape(tokens, D)
    return whole_kernel(
        body,
        (low_shape(D, D), low, low, low),
        scratch=[pltpu.VMEM((tokens, D), BF16)],
        flops=18 * UNIT,
        moved=10 << 20,
        name="self_attention_back",
    )


def self_backward(layout, tokens):
    def body(info_ref, out_grad_ref, dq, dk, dv, gmid_ref, gains_ref, *refs):
        norm_two_ref, norm_three_ref, w_ref, a_ref, x_ref = refs[:5]
        grad_ref, keep_ref, send_ref, grads, norms, tile = refs[5:]
        grads[3] = out_grad_ref[...]
        a_t = a_ref[...].T
        for index, ref in enumerate((dq, dk, dv)):
            grads[index] = mm(a_t, ref[...]).astype(BF16)
        total = None
        for index, ref in enumerate((dq, dk, dv)):
            part = mm_nt(ref[...], w_ref[index])
            total = part if total is None else total + part
        place_grads(info_ref, layout, grads, keep_ref, send_ref)
        back, gain_grad, shift_grad = norm_backward(
            total, x_ref[...].astype(F32), gains_ref[0:1, :]
        )
        grad_ref[...] = (gmid_ref[...] + back).astype(BF16)
        tile[...] = jnp.zeros_like(tile)
        for index, row in enumerate((gain_grad, shift_grad)):
            norms[index : index + 1, :] = row
        norms[2:4, :] = norm_two_ref[...]
        norms[4:6, :] = norm_three_ref[...]
        for block in range(layout.dp):
            columns = slice(block * layout.rows, (block + 1) * layout.rows)
            tile[block, 0:6, 0 : layout.rows] = norms[0:6, columns].astype(BF16)
        for other, ref in ((False, keep_ref), (True, send_ref)):
            core = 1 - info_ref[0] if other else info_ref[0]
            for slot in range(layout.planes):
                block = tile[slot * 2 + core]
                for position in range(layout.tensor):
                    ref[position, slot, layout.rows :, :] = block

    low = low_shape(tokens, D)
    pieces = low_shape(layout.tensor, layout.planes, layout.rows + NORM_ROWS, layout.width)
    return whole_kernel(
        body,
        (low, pieces, pieces),
        scratch=[
            pltpu.VMEM((GROUP, D, D), BF16),
            pltpu.VMEM((8, D), F32),
            pltpu.VMEM((layout.dp, NORM_ROWS, layout.width), BF16),
        ],
        flops=7 * UNIT,
        moved=6 << 20,
        name="self_backward",
    )


def gram_rest(low_ref, rest_ref, ratio, shift):
    half = D // 2
    diagonal = lax.broadcasted_iota(jnp.int32, (half, half), 0) == lax.broadcasted_iota(
        jnp.int32, (half, half), 1
    )
    shifted = jnp.where(diagonal, shift, 0.0)
    top, bottom = slice(0, half), slice(half, D)
    upper, lower = low_ref[top, :], low_ref[bottom, :]
    rest_ref[top, top] = (ratio * mm_nt(upper, upper) - shifted).astype(BF16)
    corner = (ratio * mm_nt(upper, lower)).astype(BF16)
    rest_ref[top, bottom] = corner
    rest_ref[bottom, top] = corner.T
    rest_ref[bottom, bottom] = (ratio * mm_nt(lower, lower) - shifted).astype(BF16)


def apply_factor(low_ref, poly_ref, scale, kept):
    for start in range(0, kept, D):
        cols = slice(start, min(start + D, kept))
        part = low_ref[:, cols]
        low_ref[:, cols] = (scale * part.astype(F32) + mm(poly_ref[...], part)).astype(BF16)


def sweep(low_ref, rest_ref, poly_ref, width, kept, first=False):
    shift = jnp.zeros((), F32)
    for start in range(0, width, D):
        part = low_ref[:, start : start + D].astype(F32)
        shift = shift + jnp.sum(part * part)
    inverse = 1.0 / (jnp.sqrt(shift) + 1e-07) if first else 1.0
    shift = shift * (inverse * inverse * (1.0 / D))
    gram_rest(low_ref, rest_ref, inverse * inverse, shift)
    slope = POLY_SECOND + 2.0 * POLY_THIRD * shift
    scale = POLY_FIRST + POLY_SECOND * shift + POLY_THIRD * shift * shift
    half = D // 2
    for rows in (slice(0, half), slice(half, D)):
        square = mm(rest_ref[rows, :], rest_ref[...])
        poly = slope * rest_ref[rows, :].astype(F32) + POLY_THIRD * square
        poly_ref[rows, :] = (inverse * poly).astype(BF16)
    apply_factor(low_ref, poly_ref, inverse * scale, kept)


def orthogonalize_attention(layout):
    parts, rows = layout.parts, layout.rows

    def body(info_ref, *refs):
        pieces = refs[:parts]
        mine_ref, other_ref, low, rest, poly = refs[parts:]
        for part, ref in enumerate(pieces):
            low[:, part * layout.width : (part + 1) * layout.width] = ref[...]
        sweep(low, rest, poly, D, D, first=True)

        def one(step, carry):
            sweep(low, rest, poly, D, D)
            return carry

        lax.fori_loop(1, NS_STEPS, one, 0)
        for ref, core in ((mine_ref, info_ref[0]), (other_ref, 1 - info_ref[0])):
            start = pl.multiple_of((2 * info_ref[1] + core) * rows, rows)
            ref[...] = low[pl.ds(start, rows), 0 : layout.width]

    return whole_kernel(
        body,
        (low_shape(rows, layout.width), low_shape(rows, layout.width)),
        scratch=[pltpu.VMEM((D, D), BF16)] * 3,
        flops=15 * UNIT,
        moved=2 << 20,
        name="orthogonalize_attention",
    )


def gram_sweeps(rest_ref, poly_ref, square_ref, sum_ref, shift):
    diagonal = lax.broadcasted_iota(jnp.int32, (D, D), 0) == lax.broadcasted_iota(
        jnp.int32, (D, D), 1
    )
    scale = None
    for step in range(GRAM_STEPS):
        rest = rest_ref[...]
        slope = POLY_SECOND + 2.0 * POLY_THIRD * shift
        here = POLY_FIRST + POLY_SECOND * shift + POLY_THIRD * shift * shift
        poly = slope * rest.astype(F32) + POLY_THIRD * mm(rest, rest)
        poly_ref[...] = poly.astype(BF16)
        low = poly_ref[...]
        if scale is None:
            scale = here
            sum_ref[...] = poly
        else:
            before = sum_ref[...]
            sum_ref[...] = here * before + scale * poly + mm(low, before.astype(BF16))
            scale = scale * here
        if step + 1 < GRAM_STEPS:
            square = 2.0 * here * poly + mm(low, low)
            square_ref[...] = square.astype(BF16)
            twice = here * here
            rest = twice * rest.astype(F32) + shift * square + mm(square_ref[...], rest)
            more = jnp.sum(jnp.where(diagonal, rest, 0.0)) * (1.0 / D)
            rest_ref[...] = jnp.where(diagonal, rest - more, rest).astype(BF16)
            shift = twice * shift + more
    return scale


def orthogonalize_wide(layout, hidden):
    count = layout.tensor
    width = count * hidden

    def body(info_ref, *refs):
        pieces = refs[:count]
        out_ref, low, rest, poly, square, total_ref, sem = refs[count:]
        total = jnp.zeros((), F32)
        own = pltpu.make_async_copy(pieces[-1], low.at[:, 0:hidden], sem)
        own.start()
        for index in reversed(range(count)):
            cols = slice(index * hidden, (index + 1) * hidden)
            if index == 0:
                own.wait()
                part = low[:, cols]
            else:
                part = pieces[index - 1][...]
                low[:, cols] = part
            values = part.astype(F32)
            total = total + jnp.sum(values * values)
        inverse = 1.0 / (jnp.sqrt(total) + 1e-07)
        ratio = inverse * inverse
        shift = total * ratio * (1.0 / D)
        gram_rest(low, rest, ratio, shift)
        scale = gram_sweeps(rest, poly, square, total_ref, shift)
        poly[...] = (inverse * total_ref[...]).astype(BF16)
        apply_factor(low, poly, inverse * scale, width)
        for step in range(GRAM_STEPS, NS_STEPS):
            sweep(low, rest, poly, width, width if step + 1 < NS_STEPS else hidden)
        out_ref[...] = low[:, 0:hidden]

    return whole_kernel(
        body,
        low_shape(D, hidden),
        scratch=[pltpu.VMEM((D, width), BF16)]
        + [pltpu.VMEM((D, D), BF16)] * 3
        + [pltpu.VMEM((D, D), F32), pltpu.SemaphoreType.DMA],
        flops=30 * UNIT,
        moved=3 << 20,
        name="orthogonalize_wide",
    )


def wide_shard(hidden):
    def body(info_ref, expand_far, contract_far, out_ref, block, sem):
        @pl.when(info_ref[0] == 0)
        def _():
            copy = pltpu.make_async_copy(expand_far, block.at[:, 0:hidden], sem)
            copy.start()
            copy.wait()
            out_ref[...] = block[:, 0:hidden].astype(BF16)

        @pl.when(info_ref[0] != 0)
        def _():
            copy = pltpu.make_async_copy(contract_far, block.at[0:hidden, :], sem)
            copy.start()
            copy.wait()
            out_ref[...] = block[0:hidden, :].T.astype(BF16)

    return whole_kernel(
        body,
        low_shape(D, hidden),
        scratch=[pltpu.VMEM((D, D), F32), pltpu.SemaphoreType.DMA],
        moved=3 << 20,
        name="wide_shard",
    )


def fence(values, after, space=pl.ANY):
    def body(source_ref, *refs):
        pass

    return pl.pallas_call(
        body,
        out_shape=jax.ShapeDtypeStruct(values.shape, values.dtype),
        in_specs=[pl.BlockSpec(memory_space=pl.ANY)] * (1 + len(after)),
        out_specs=pl.BlockSpec(memory_space=pl.ANY),
        input_output_aliases={0: 0},
        name="fence",
    )(values, *after)


def halves_sum(layout, kept, got, name, after=()):
    half = kept.shape[0] // 2

    def body(info_ref, kept_ref, got_ref, upper_ref, lower_ref):
        for position in range(half):
            for ref, at in ((upper_ref, half + position), (lower_ref, position)):
                ref[position] = (kept_ref[at].astype(F32) + got_ref[at].astype(F32)).astype(BF16)

    part = low_shape(half, *kept.shape[1:])
    return whole_kernel(body, (part, part), moved=4 * kept.size, name=name)(
        kept, got, after=after
    )


def nest_of(grad, momentum):
    return (1.0 + MOMENTUM_DECAY) * grad + MOMENTUM_DECAY * MOMENTUM_DECAY * momentum


def wide_nest(layout, hidden):
    count = layout.planes

    def body(info_ref, got_ref, momentum_ref, out_ref):
        total = sum(got_ref[plane].astype(F32) for plane in range(count))
        nest = nest_of(total, momentum_ref[...]).astype(BF16)
        for plane in range(count):
            out_ref[plane] = nest

    return whole_kernel(
        body, low_shape(count, D // count, hidden), moved=1 << 20, name="wide_nest"
    )


def wide_slots_sum(layout, hidden):
    def body(info_ref, kept_ref, got_ref, out_ref):
        out_ref[...] = (kept_ref[0].astype(F32) + got_ref[0].astype(F32)).astype(BF16)

    shape = low_shape(layout.planes, D // layout.planes, hidden)
    return whole_kernel(body, shape, moved=1 << 20, name="wide_slots_sum")


def attention_slots(layout):
    rows, planes, width = layout.rows, layout.planes, layout.width

    def body(info_ref, cross_ref, cross_got, self_ref, self_got, out_ref):
        for slot in range(planes):
            for start, kept, got in ((0, cross_ref, cross_got), (rows, self_ref, self_got)):
                total = kept[0, slot].astype(F32) + got[0, slot].astype(F32)
                out_ref[slot, start : start + total.shape[0], :] = total.astype(BF16)

    return whole_kernel(
        body,
        low_shape(planes, 2 * rows + NORM_ROWS, width),
        moved=2 << 20,
        name="attention_slots",
    )


def attention_nest(layout):
    rows, planes, width = layout.rows, layout.planes, layout.width

    def body(info_ref, got_ref, momentum_far, mine_ref, other_ref, grad_ref, norm_ref, *refs):
        momentum, sems = refs
        first_core, tensor, copies = info_ref[0] == 0, info_ref[2], Copies(sems)
        cols = slice(None)
        if layout.parts > 1:
            part = lax.rem(tensor, layout.parts) * width
            cols = pl.ds(pl.multiple_of(part, width), width)
        moving = [
            copies.start(
                momentum_far.at[group * GROUP + lax.div(tensor, layout.parts), :, cols],
                momentum.at[index],
            )
            for index, group in enumerate((1, 0))
        ]
        total = sum(got_ref[plane].astype(F32) for plane in range(planes))
        wait_all(moving)
        cross = nest_of(total[0:rows], momentum[0]).astype(BF16)
        own = nest_of(total[rows : 2 * rows], momentum[1]).astype(BF16)
        mine_ref[...] = jnp.where(first_core, own, cross)
        other_ref[...] = jnp.where(first_core, cross, own)
        grad_ref[...] = total[0 : 2 * rows].astype(BF16)
        norm_ref[...] = total[2 * rows : 2 * rows + 8]

    one = low_shape(rows, width)
    return whole_kernel(
        body,
        (one, one, low_shape(2 * rows, width), wide_shape(8, width)),
        scratch=[pltpu.VMEM((2, rows, width), F32), pltpu.SemaphoreType.DMA((2,))],
        moved=2 << 20,
        name="attention_nest",
    )


def attention_pair(layout):
    rows, planes = layout.rows, layout.planes

    def body(info_ref, mine_ref, got_ref, out_ref):
        first_core = info_ref[0] == 0
        mine, got = mine_ref[...], got_ref[...]
        for plane in range(planes):
            out_ref[plane, 0:rows, :] = jnp.where(first_core, mine, got)
            out_ref[plane, rows : 2 * rows, :] = jnp.where(first_core, got, mine)

    return whole_kernel(
        body, low_shape(planes, 2 * rows, layout.width), moved=1 << 20, name="attention_pair"
    )


def wide_momentum(layout, hidden):
    piece_rows = D // layout.planes

    def body(info_ref, expand_ref, contract_ref, out_ref, turned):
        rows = pl.ds(pl.multiple_of(info_ref[1] * piece_rows, piece_rows), piece_rows)
        turned[...] = contract_ref[...].T
        out_ref[...] = jnp.where(info_ref[0] == 0, expand_ref[rows, :], turned[rows, :])

    return whole_kernel(
        body,
        wide_shape(piece_rows, hidden),
        scratch=[pltpu.VMEM((D, hidden), F32)],
        moved=3 << 20,
        name="wide_momentum",
    )


def decayed(master, share, scale):
    return master - MUON_RATE * (MUON_DECAY * master + scale * share)


def finish_wide(layout, hidden, full_hidden):
    scale = 0.2 * math.sqrt(max(D, full_hidden))

    def body(info_ref, mine_ref, other_ref, expand_ref, contract_ref, *refs):
        e_new, e_low, c_new, c_low = refs
        first = info_ref[0] == 0
        mine, other = mine_ref[...], other_ref[...]
        new = decayed(expand_ref[...], jnp.where(first, mine, other).astype(F32), scale)
        e_new[...] = new
        e_low[...] = new.astype(BF16)
        new = decayed(contract_ref[...], jnp.where(first, other, mine).T.astype(F32), scale)
        c_new[...] = new
        c_low[...] = new.astype(BF16)

    return whole_kernel(
        body,
        (wide_shape(D, hidden), low_shape(D, hidden), wide_shape(hidden, D), low_shape(hidden, D)),
        moved=6 << 20,
        name="finish_wide",
    )


def wide_velocity(layout, hidden):
    grad_share = 1.0 / (1.0 + MOMENTUM_DECAY)
    momentum_share = MOMENTUM_DECAY - MOMENTUM_DECAY * MOMENTUM_DECAY * grad_share

    def body(info_ref, mine_ref, other_ref, expand_ref, contract_ref, e_new, c_new, token):
        token[...] = jnp.zeros_like(token)
        first = info_ref[0] == 0
        mine, other = mine_ref[...], other_ref[...]
        nest = jnp.where(first, mine, other).astype(F32)
        e_new[...] = momentum_share * expand_ref[...] + grad_share * nest
        nest = jnp.where(first, other, mine).T.astype(F32)
        c_new[...] = momentum_share * contract_ref[...] + grad_share * nest

    return whole_kernel(
        body,
        (wide_shape(D, hidden), wide_shape(hidden, D), wide_shape(8, 128)),
        moved=6 << 20,
        name="wide_velocity",
    )


def owner_columns(info_ref, layout, position, other=False):
    owner = owner_at(info_ref, layout, position, other)
    if layout.parts == 1:
        return owner, slice(None)
    part = lax.rem(owner, layout.parts) * layout.width
    return lax.div(owner, layout.parts), pl.ds(pl.multiple_of(part, layout.width), layout.width)


def attention_velocity(layout):
    count, rows = layout.tensor, layout.rows

    def body(info_ref, *refs):
        momentum_ref, velocity_ref = refs[count:]
        for position in range(count):
            matrix, cols = owner_columns(info_ref, layout, position)
            for group in range(2):
                index, start = group * GROUP + matrix, (1 - group) * rows
                grad = refs[position][start : start + rows, :].astype(F32)
                velocity_ref[index, :, cols] = (
                    MOMENTUM_DECAY * momentum_ref[index, :, cols] + grad
                )

    return whole_kernel(
        body, wide_shape(2 * GROUP, rows, D), moved=3 << 20, name="attention_velocity"
    )


def finish_attention(layout):
    count = layout.tensor
    scale = 0.2 * math.sqrt(D)

    def body(info_ref, *refs):
        late = refs[:count]
        master_ref, new_ref, low_ref = refs[count:]
        for position in range(count):
            matrix, cols = owner_columns(info_ref, layout, position)
            for group in range(2):
                index = group * GROUP + matrix
                at = info_ref[0] if group == 0 else 1 - info_ref[0]
                new = decayed(
                    master_ref[index, :, cols], late[position][at].astype(F32), scale
                )
                new_ref[index, :, cols] = new
                low_ref[index, :, cols] = new.astype(BF16)

    shape = (2 * GROUP, layout.rows, D)
    return whole_kernel(
        body, (wide_shape(*shape), low_shape(*shape)), moved=4 << 20, name="finish_attention"
    )


def finish_norms(layout):
    def body(info_ref, grad_ref, params_ref, first_ref, second_ref, new, first_new, second_new):
        grad = grad_ref[0:6, 0 : layout.rows]
        first = BETA_FIRST * first_ref[...] + (1.0 - BETA_FIRST) * grad
        second = BETA_SECOND * second_ref[...] + (1.0 - BETA_SECOND) * grad * grad
        corrected = first / (1.0 - BETA_FIRST**STEP)
        denominator = jnp.sqrt(second / (1.0 - BETA_SECOND**STEP)) + ADAM_EPSILON
        new[...] = params_ref[...] - ADAM_RATE * corrected / denominator
        first_new[...] = first
        second_new[...] = second

    return whole_kernel(body, (wide_shape(6, layout.rows),) * 3, moved=1 << 14, name="norms")


def device_program(layout, arguments):
    (
        inputs,
        encoder,
        dec_segments,
        enc_segments,
        cotangent,
        attn_master,
        attn_momentum,
        expand_master,
        expand_momentum,
        contract_master,
        contract_momentum,
        norm_params,
        first_moments,
        second_moments,
    ) = arguments
    tokens, states = inputs.shape[1], encoder.shape[1]
    hidden = expand_master.shape[1]
    full_hidden = hidden * layout.tensor
    dp_at, tensor_at = lax.axis_index("dp"), lax.axis_index("tensor")
    x, enc, cot = inputs[0], encoder[0], cotangent[0]

    if layout.quad:
        shard = wide_shard(hidden)(far=[expand_master, contract_master])
        chunk = weight_chunk(layout, 0, "self_chunk", 1)(
            norm_params, far=[attn_master], after=[shard]
        )
        near = send(shard, layout.inplane(0))
        cross_own = cross_rows(layout)(far=[attn_master], after=[near])
        first, second, tile = self_split(layout)(*send_planes(layout, chunk), after=[cross_own])
        cross_own = exchange_planes(layout, fence(cross_own, [tile]))
        got_first = send(first, layout.plain_inplane(1))
        got_second = send(second, layout.plain_inplane(2))
        tiles = [tile, swap_cores(layout, tile)]
        a_saved, a, gains = first_norm(tokens)(*tiles, far=[x])
        got_first, got_second = fence(got_first, [a]), fence(got_second, [a])
        self_own = [first, second, got_first, got_second]
        self_pieces = self_own + [swap_cores(layout, piece) for piece in self_own]
        near = fence(near, [got_first])
        far = send(fence(shard, [got_first]), layout.inplane(1))
        farthest = send(near, layout.inplane(1))
        before = []
    else:
        low = attn_master.astype(BF16)
        norm_low = lax.all_gather(norm_params.astype(BF16), "dp", axis=1, tiled=True)
        padded = jnp.concatenate([norm_low, jnp.zeros((NORM_ROWS - 6, D), BF16)])
        self_low = lax.all_gather(low[:GROUP], "dp", axis=1, tiled=True)
        cross_low = lax.all_gather(low[GROUP:], "dp", axis=1, tiled=True)
        self_pieces, before = [self_low], []
        tiles = [padded, jnp.zeros_like(padded)]
        shard = wide_shard(hidden)(far=[expand_master, contract_master])
        wide_own = gather_inplane(layout, shard)
        wide_other = [swap_cores(layout, piece) for piece in wide_own]

    dec_row, dec_column = dec_segments.reshape(1, tokens), dec_segments.reshape(tokens, 1)
    enc_column = enc_segments.reshape(states, 1)
    if not layout.quad:
        a_saved, a, gains = first_norm(tokens)(*tiles, far=[x])
    w_self, q, k, v, self_prob, self_mix, mid, c = self_forward(layout, tokens)(
        a, gains, dec_row, dec_column, far=[x, *self_pieces], after=before
    )
    if layout.quad:
        far, farthest = fence(far, [c]), fence(farthest, [c])
        cross_own = fence(cross_own, [far, farthest])
        cross_pieces = [cross_own, swap_cores(layout, cross_own)]
        wide_own = [shard, near, far, farthest]
        wide_other = [swap_cores(layout, piece) for piece in wide_own]
    else:
        cross_pieces = [cross_low]
    w_cross, qc, kc, vc, cross_prob, cross_mix, late, f = cross_forward(layout, tokens, states)(
        c, gains, dec_row, enc_column, far=[enc, mid, *cross_pieces], after=[wide_own[-1]]
    )
    w_in, w_out, post, d_pre, wide_keep, wide_send = feed_forward(layout, tokens, hidden)(
        f, far=[cot, *wide_own, *wide_other]
    )
    output, grad_late, late_low, norm_three = feed_forward_sums(layout, tokens, hidden)(
        w_in, w_out, post, d_pre, late, gains, far=[cot]
    )
    top = layout.bits - 1
    upper, lower = halves_sum(
        layout, wide_keep, swap_cores(layout, wide_send), "wide_sum", after=[late_low]
    )
    encoder_grad, grad_mid, mid_low, norm_two, cross_keep, cross_send = cross_backward(
        layout, tokens, states
    )(
        late_low, cross_mix, grad_late, gains, qc, kc, vc, cross_prob, c, w_cross,
        far=[enc, mid], after=[upper],
    )
    got = send(upper, layout.inplane(top))
    for bit in reversed(range(top)):
        upper, lower = halves_sum(layout, lower, got, "wide_sum", after=[mid_low])
        got = send(upper, layout.inplane(bit))
    self_out_grad, dq, dk, dv = self_attention_back(layout, tokens)(
        mid_low, w_self, self_mix, q, k, v, self_prob, after=[upper]
    )
    input_grad, self_keep, self_send = self_backward(layout, tokens)(
        self_out_grad, dq, dk, dv, grad_mid, gains, norm_two, norm_three,
        w_self, a_saved, x,
    )
    wide_slots = wide_slots_sum(layout, hidden)(lower, got, after=[self_keep])
    wide_got = exchange_planes(layout, wide_slots)
    self_upper, self_lower = halves_sum(
        layout, self_keep, swap_cores(layout, fence(self_send, [wide_slots])), "self_sum"
    )
    cross_upper, cross_lower = halves_sum(
        layout, cross_keep, swap_cores(layout, cross_send), "cross_sum", after=[wide_slots]
    )
    got_cross = send(cross_upper, layout.inplane(top))
    momentum = wide_momentum(layout, hidden)(expand_momentum, contract_momentum)
    got_self = send(self_upper, layout.inplane(top))
    for bit in reversed(range(top)):
        cross_upper, cross_lower = halves_sum(layout, cross_lower, got_cross, "cross_sum")
        got_cross = send(cross_upper, layout.inplane(bit))
    nest_rows = wide_nest(layout, hidden)(wide_got, momentum, after=[self_upper, cross_upper])
    nest = exchange_planes(layout, nest_rows).reshape(D, hidden)
    for bit in reversed(range(top)):
        self_upper, self_lower = halves_sum(layout, self_lower, got_self, "self_sum")
        got_self = send(self_upper, layout.inplane(bit))
    rows_by_slot = attention_slots(layout)(cross_lower, got_cross, self_lower, got_self)
    nest = fence(nest, [rows_by_slot])
    nest_other = swap_cores(layout, nest)
    expand_velocity, contract_velocity, velocity_done = wide_velocity(layout, hidden)(
        nest, nest_other, expand_momentum, contract_momentum
    )
    nest_pieces = gather_inplane(
        layout, nest, lambda piece: fence(piece, [rows_by_slot, velocity_done])
    )
    nest_mine, nest_others, attn_grad, norm_rows = attention_nest(layout)(
        exchange_planes(layout, rows_by_slot), far=[attn_momentum], after=[nest_pieces[layout.tensor // 2 - 1]]
    )

    attn_nest = attention_pair(layout)(nest_mine, swap_cores(layout, nest_others))
    early = gather_inplane_direct(layout, attn_grad)

    def whole_pieces(piece):
        gathered = [piece]
        for bit in range(layout.parts.bit_length() - 1):
            pairs = layout.pairs(lambda d, t: d * layout.tensor + (t ^ (1 << bit)))
            gathered = gathered + [send(one, pairs) for one in gathered]
        return gathered

    wide_ortho = orthogonalize_wide(layout, hidden)(
        *nest_pieces[1:], far=nest_pieces[:1], after=[attn_nest])
    whole = exchange_planes(layout, attn_nest).reshape(D, layout.width)
    mine, others = orthogonalize_attention(layout)(
        *whole_pieces(whole), after=[wide_ortho, *early[1:]]
    )
    late_pieces = gather_inplane_direct(layout, jnp.stack([mine, swap_cores(layout, others)]))
    attn_velocity = attention_velocity(layout)(*early, attn_momentum)
    norm_updated, first_updated, second_updated = finish_norms(layout)(
        norm_rows, norm_params, first_moments, second_moments
    )

    expand_updated, expand_copy, contract_updated, contract_copy = finish_wide(
        layout, hidden, full_hidden
    )(wide_ortho, swap_cores(layout, wide_ortho), expand_master, contract_master)
    attn_updated, attn_copy = finish_attention(layout)(
        *late_pieces, attn_master
    )
    return (
        output[None],
        input_grad[None],
        encoder_grad[None],
        attn_updated,
        attn_velocity,
        attn_copy,
        expand_updated,
        expand_velocity,
        expand_copy,
        contract_updated,
        contract_velocity,
        contract_copy,
        norm_updated,
        first_updated,
        second_updated,
    )


def solution(mesh):
    layout = Layout(mesh.shape["dp"], mesh.shape["tensor"])

    def local(*arguments):
        return device_program(layout, arguments)

    rows = P(AXES, None, None)
    by_dp, by_column, by_row, norm = P(None, "dp", None), P(None, "tensor"), P("tensor", None), P(None, "dp")
    return jax.shard_map(
        local,
        mesh=mesh,
        in_specs=(rows, rows, P(AXES, None), P(AXES, None), rows)
        + (by_dp, by_dp, by_column, by_column, by_row, by_row, norm, norm, norm),
        out_specs=(rows, rows, rows, by_dp, by_dp, by_dp)
        + (by_column, by_column, by_column, by_row, by_row, by_row, norm, norm, norm),
        check_vma=False,
    )
```

```python
import functools
import math

import jax
import jax.numpy as jnp
from jax import lax
from jax.experimental import pallas as pl
from jax.experimental.pallas import tpu as pltpu
from jax.sharding import PartitionSpec as P

D = 512
HEADS = 8
HEAD = D // HEADS
PAIR = 2 * HEAD
NS_STEPS = 5
GRAM_STEPS = 3
STEP = 10

MASKED_SCORE = -1e30
NORM_EPSILON = 1e-05
MOMENTUM_DECAY = 0.95
MUON_RATE = 0.15
MUON_DECAY = 0.01
POLY_FIRST = 3.4445
POLY_SECOND = -4.775
POLY_THIRD = 2.0315
ADAM_RATE = 0.4
BETA_FIRST = 0.9
BETA_SECOND = 0.999
ADAM_EPSILON = 1e-08
GROUP = 4
QUERY_BLOCK = 512

F32 = jnp.float32
BF16 = jnp.bfloat16
AXES = ("dp", "tensor")
MIB = 1 << 20
VMEM_BYTES = 24 * MIB
NORM_ROWS = 16


def mm(left, right):
    return lax.dot_general(left, right, (((1,), (0,)), ((), ())), preferred_element_type=F32)


def mm_nt(left, right):
    return lax.dot_general(left, right, (((1,), (1,)), ((), ())), preferred_element_type=F32)


def mm_tn(left, right):
    return lax.dot_general(left, right, (((0,), (0,)), ((), ())), preferred_element_type=F32)


def normalized(values):
    average = jnp.mean(values, -1, keepdims=True)
    centred = values - average
    inv_std = lax.rsqrt(jnp.mean(centred * centred, -1, keepdims=True) + NORM_EPSILON)
    return centred * inv_std, inv_std


def norm_backward(incoming, values, gain_row):
    normed, inv_std = normalized(values)
    scaled = incoming * gain_row
    inner = (
        scaled
        - jnp.mean(scaled, -1, keepdims=True)
        - normed * jnp.mean(scaled * normed, -1, keepdims=True)
    )
    gain_grad = jnp.sum(incoming * normed, 0, keepdims=True)
    shift_grad = jnp.sum(incoming, 0, keepdims=True)
    return inner * inv_std, gain_grad, shift_grad


def head_mask(half, value):
    lane = lax.broadcasted_iota(jnp.int32, (1, PAIR), 1)
    inside = jnp.logical_and(lane >= half * HEAD, lane < (half + 1) * HEAD)
    return jnp.where(inside, value, 0.0).astype(BF16)


def pair_columns(pair):
    return pl.ds(pl.multiple_of(pair * PAIR, PAIR), PAIR)


def attend(q_ref, k_ref, v_ref, key_seg_ref, query_seg_ref, prob_ref, out_ref, done):
    queries = q_ref.shape[0]
    block = min(QUERY_BLOCK, queries)

    def one_pair(pair, carry):
        cols = pair_columns(pair)
        keys, values = k_ref[:, cols], v_ref[:, cols]
        for start in range(0, queries, block):
            rows = pl.ds(start, block)
            query = q_ref[rows, cols]
            allowed = key_seg_ref[...] == query_seg_ref[:, rows]
            total = None
            for half in range(2):
                scores = mm_nt(keys * head_mask(half, HEAD**-0.5), query)
                scores = jnp.where(allowed, scores, MASKED_SCORE)
                peak = jnp.max(scores, 0, keepdims=True)
                weights = jnp.exp(scores - peak)
                soft = (weights * (1.0 / jnp.sum(weights, 0, keepdims=True))).astype(BF16)
                prob_ref[pair * 2 + half, :, rows] = soft
                part = mm_tn(soft, values * head_mask(half, 1.0))
                total = part if total is None else total + part
            out_ref[rows, cols] = total.astype(BF16)
        done(pair)
        return carry

    lax.fori_loop(0, HEADS // 2, one_pair, 0)


def attend_back(q_ref, k_ref, v_ref, prob_ref, grad_ref, dq_ref, dk_ref, dv_ref, ready):
    queries = q_ref.shape[0]
    block = min(QUERY_BLOCK, queries)
    scaling = HEAD**-0.5

    def one_pair(pair, carry):
        cols = pair_columns(pair)
        keys, values = k_ref[:, cols], v_ref[:, cols]
        key_sum = value_sum = None
        ready(pair)
        for start in range(0, queries, block):
            rows = pl.ds(start, block)
            query, grad = q_ref[rows, cols], grad_ref[rows, cols]
            query_sum = None
            for half in range(2):
                mask = head_mask(half, 1.0)
                soft = prob_ref[pair * 2 + half, :, rows]
                weights = soft.astype(F32)
                grad_soft = mm_nt(values * mask, grad)
                product = weights * grad_soft
                inner = jnp.sum(product, 0, keepdims=True)
                grad_scores = (product - weights * inner).astype(BF16)
                value_part = mm(soft, grad * mask)
                key_part = mm(grad_scores, query * mask)
                query_part = mm_tn(grad_scores, keys * mask)
                value_sum = value_part if value_sum is None else value_sum + value_part
                key_sum = key_part if key_sum is None else key_sum + key_part
                query_sum = query_part if query_sum is None else query_sum + query_part
            dq_ref[rows, cols] = (query_sum * scaling).astype(BF16)
        dk_ref[:, cols] = (key_sum * scaling).astype(BF16)
        dv_ref[:, cols] = value_sum.astype(BF16)
        return carry

    lax.fori_loop(0, HEADS // 2, one_pair, 0)


def pair_copy(source, target, sems, pair):
    heads = pl.ds(pair * 2, 2)
    return pltpu.make_async_copy(source.at[heads], target.at[heads], sems.at[pair])


def reorder(core, position, bits):
    if core == 0:
        return position
    return sum(((position >> bit) & 1) << (bits - 1 - bit) for bit in range(bits))


class Layout:
    def __init__(self, dp_size, tensor_size):
        self.dp, self.tensor = dp_size, tensor_size
        self.bits = tensor_size.bit_length() - 1
        self.planes = dp_size // 2
        self.parts = tensor_size // GROUP
        self.rows = D // dp_size
        self.quad = tensor_size == 4
        self.width = D // self.parts

    def pairs(self, move):
        return [
            (d * self.tensor + t, move(d, t)) for d in range(self.dp) for t in range(self.tensor)
        ]

    def inplane(self, bit):
        return self.pairs(
            lambda d, t: d * self.tensor + (t ^ reorder(d & 1, 1 << bit, self.bits))
        )

    def inplane_position(self, position):
        return self.pairs(
            lambda d, t: d * self.tensor + (t ^ reorder(d & 1, position, self.bits))
        )

    def plain_inplane(self, offset):
        return self.pairs(lambda d, t: d * self.tensor + (t ^ offset))

    def plane(self, slot):
        return self.pairs(lambda d, t: (d ^ (2 * slot)) * self.tensor + t)

    def other_core(self):
        return self.pairs(lambda d, t: (d ^ 1) * self.tensor + t)


def send(values, pairs):
    return lax.ppermute(values, AXES, pairs)


def gather_inplane(layout, piece, forwarded=None):
    pieces = [piece]
    for bit in range(layout.bits):
        if forwarded is not None and bit + 1 == layout.bits:
            pieces = pieces[:1] + [forwarded(one) for one in pieces[1:]]
        pieces = pieces + [send(one, layout.inplane(bit)) for one in pieces]
    return pieces


def gather_inplane_direct(layout, piece):
    return [piece] + [
        send(piece, layout.inplane_position(position)) for position in range(1, layout.tensor)
    ]


def send_planes(layout, piece):
    return [piece] + [send(piece, layout.plane(slot)) for slot in range(1, layout.planes)]


def exchange_planes(layout, pieces):
    groups = [list(range(core, layout.dp, 2)) for core in range(2)]
    return lax.all_to_all(pieces, "dp", 0, 0, axis_index_groups=groups, tiled=True)


def exchange_inplane(pieces):
    return lax.all_to_all(pieces, "tensor", 0, 0, tiled=True)


def swap_cores(layout, values):
    return send(values, layout.other_core())


def whole_kernel(body, out_shape, scratch=(), flops=0, moved=0, name=None, far_outs=0):
    out_specs = jax.tree.map(lambda _: pl.BlockSpec(memory_space=pltpu.VMEM), out_shape)
    shapes = out_shape
    if far_outs:
        out_specs = (pl.BlockSpec(memory_space=pltpu.HBM),) * far_outs + out_specs[far_outs:]
        shapes = tuple(pltpu.HBM(one.shape, one.dtype) for one in out_shape[:far_outs])
        shapes = shapes + out_shape[far_outs:]

    def call(*operands, far=(), loose=(), after=()):
        near = len(operands)
        operands = operands + tuple(far) + tuple(loose)
        read = len(operands)

        def without_after(*refs):
            place = lax.axis_index("dp"), lax.axis_index("tensor")
            info = (place[0] % 2, place[0] // 2, place[1])
            body(info, *refs[:read], *refs[read + len(after) :])

        operands = operands[:near] + tuple(
            pltpu.with_memory_space_constraint(one, pltpu.HBM) for one in far
        ) + tuple(loose)
        return pl.pallas_call(
            without_after,
            out_shape=shapes,
            in_specs=[pl.BlockSpec(memory_space=pltpu.VMEM)] * near
            + [pl.BlockSpec(memory_space=pltpu.HBM)] * len(far)
            + [pl.BlockSpec(memory_space=pl.ANY)] * (len(loose) + len(after)),
            out_specs=out_specs,
            scratch_shapes=list(scratch),
            compiler_params=pltpu.CompilerParams(vmem_limit_bytes=VMEM_BYTES),
            cost_estimate=pl.CostEstimate(flops=flops, bytes_accessed=moved, transcendentals=0),
            name=name,
        )(*operands, *after)

    return call


class Copies:
    def __init__(self, sems):
        self.sems, self.count = sems, 0

    def start(self, source, target):
        copy = pltpu.make_async_copy(source, target, self.sems.at[self.count])
        copy.start()
        self.count += 1
        return copy


def wait_all(copies):
    for copy in copies:
        copy.wait()


def low_shape(*shape):
    return jax.ShapeDtypeStruct(shape, BF16)


def wide_shape(*shape):
    return jax.ShapeDtypeStruct(shape, F32)


UNIT = 2 * D * D * D


def owner_at(info_ref, layout, position, other=False):
    core = info_ref[0]
    first = 1 if other else 0
    offset = jnp.where(
        core == first, reorder(0, position, layout.bits), reorder(1, position, layout.bits)
    )
    return jnp.bitwise_xor(info_ref[2], offset)


def row_start(info_ref, layout, plane, other=False):
    core = 1 - info_ref[0] if other else info_ref[0]
    return pl.multiple_of((plane * 2 + core) * layout.rows, layout.rows)


def quad_matrix(info_ref, position):
    tensor = info_ref[2]
    side = jnp.bitwise_xor(lax.rem(tensor, 2), lax.div(tensor, 2))
    return jnp.bitwise_xor(side, position // 2) * 2 + position % 2


def weight_chunk(layout, group, name, copies_out):
    rows = layout.rows
    tiles = NORM_ROWS if group == 0 else 0

    def body(info_ref, norm_ref, source_ref, out_ref, tile, blocks, sems):
        copies = Copies(sems)
        moving = [
            copies.start(
                source_ref.at[group * GROUP + quad_matrix(info_ref, position)],
                blocks.at[position],
            )
            for position in range(2)
        ]
        if tiles:
            tile[...] = jnp.zeros_like(tile)
            for block in range(layout.dp):

                @pl.when(info_ref[1] * 2 + info_ref[0] == block)
                def _():
                    tile[0:6, block * rows : (block + 1) * rows] = norm_ref[...]

            for plane in range(copies_out):
                out_ref[plane, 2 * rows :, :] = tile[...].astype(BF16)
        wait_all(moving)
        for index in range(2):
            block = blocks[index].astype(BF16)
            for plane in range(copies_out):
                out_ref[plane, index * rows : (index + 1) * rows, :] = block

    return whole_kernel(
        body,
        low_shape(copies_out, 2 * rows + tiles, D),
        scratch=[
            pltpu.VMEM((NORM_ROWS, D), F32),
            pltpu.VMEM((2, rows, D), F32),
            pltpu.SemaphoreType.DMA((2,)),
        ],
        moved=1 << 20,
        name=name,
    )


def self_split(layout):
    rows, planes = layout.rows, layout.planes

    def body(info_ref, *refs):
        slots, outs, tile_ref = refs[:planes], refs[planes : planes + 2], refs[-1]
        tile = None
        for slot, ref in enumerate(slots):
            plane = jnp.bitwise_xor(info_ref[1], slot)
            for index in range(2):
                outs[index][plane] = ref[0, index * rows : (index + 1) * rows, :]
            part = ref[0, 2 * rows :, :].astype(F32)
            tile = part if tile is None else tile + part
        tile_ref[...] = tile.astype(BF16)

    one = low_shape(planes, rows, D)
    return whole_kernel(
        body, (one, one, low_shape(NORM_ROWS, D)), moved=2 << 20, name="self_split"
    )


def cross_rows(layout):
    rows, planes = layout.rows, layout.planes

    def body(info_ref, source_far, out_ref, blocks, sem):
        copy = pltpu.make_async_copy(source_far.at[GROUP : 2 * GROUP], blocks, sem)
        copy.start()
        copy.wait()
        for matrix in range(GROUP):
            block = blocks[matrix].astype(BF16)
            for plane in range(planes):
                out_ref[plane, matrix * rows : (matrix + 1) * rows, :] = block

    return whole_kernel(
        body,
        low_shape(planes, GROUP * rows, D),
        scratch=[pltpu.VMEM((GROUP, rows, D), F32), pltpu.SemaphoreType.DMA],
        moved=2 << 20,
        name="cross_rows",
    )


def fetch_weights(info_ref, layout, refs, weights_ref, copies):
    if not layout.quad:
        return [copies.start(refs[0], weights_ref)]
    moving = []
    for index, ref in enumerate(refs):
        matrix = quad_matrix(info_ref, index % GROUP)
        for plane in range(layout.planes):
            at = pl.ds(row_start(info_ref, layout, plane, index >= GROUP), layout.rows)
            moving.append(copies.start(ref.at[plane], weights_ref.at[matrix, at, :]))
    return moving


def fetch_cross(info_ref, layout, refs, weights_ref, copies):
    if not layout.quad:
        return [[copies.start(refs[0], weights_ref)], [], [], []]
    moving, rows = [], layout.rows
    for matrix in range(GROUP):
        here = slice(matrix * rows, (matrix + 1) * rows)
        moving.append([])
        for index, ref in enumerate(refs):
            for plane in range(layout.planes):
                at = pl.ds(row_start(info_ref, layout, plane, index == 1), rows)
                moving[matrix].append(
                    copies.start(ref.at[plane, here, :], weights_ref.at[matrix, at, :])
                )
    return moving


def weight_pieces(layout):
    return (2 * GROUP, 2 * GROUP * layout.planes) if layout.quad else (1, 1)


def place_grads(info_ref, layout, grads_ref, keep_ref, send_ref):
    for other, ref in ((False, keep_ref), (True, send_ref)):
        for position in range(layout.tensor):
            owner = owner_at(info_ref, layout, position, other)
            for slot in range(layout.planes):
                rows = pl.ds(row_start(info_ref, layout, slot, other), layout.rows)
                if layout.parts == 1:
                    block = grads_ref[owner, rows, :]
                else:
                    part = lax.rem(owner, layout.parts) * layout.width
                    cols = pl.ds(pl.multiple_of(part, layout.width), layout.width)
                    block = grads_ref[lax.div(owner, layout.parts), rows, cols]
                ref[position, slot, 0 : layout.rows, :] = block


def first_norm(tokens):
    def body(info_ref, tile_ref, other_ref, x_far, a_out, a_ref, gains_ref, x_ref, sems):
        copies = Copies(sems)
        x_copy = copies.start(x_far, x_ref)
        gains_ref[...] = tile_ref[...].astype(F32) + other_ref[...].astype(F32)
        x_copy.wait()
        normed, _ = normalized(x_ref[...].astype(F32))
        a_ref[...] = (normed * gains_ref[0:1, :] + gains_ref[1:2, :]).astype(BF16)
        copies.start(a_ref, a_out).wait()

    return whole_kernel(
        body,
        (low_shape(tokens, D), low_shape(tokens, D), wide_shape(NORM_ROWS, D)),
        scratch=[pltpu.VMEM((tokens, D), BF16), pltpu.SemaphoreType.DMA((2,))],
        moved=1 << 20,
        name="first_norm",
        far_outs=1,
    )


def self_forward(layout, tokens):
    count, pieces = weight_pieces(layout)

    def body(info_ref, a_ref, gains_ref, query_seg_ref, key_seg_ref, x_far, *refs):
        w_out, q_out, k_out, v_out, prob_out, mix_out, mid_out, c_ref = refs[count : count + 8]
        x_ref, w_ref, q_ref, k_ref, v_ref, prob_ref, mix_ref, mid_ref = refs[count + 8 : -2]
        sems, pair_sems = refs[-2:]
        copies = Copies(sems)
        arriving = fetch_weights(info_ref, layout, refs[:count], w_ref, copies)
        x_copy = copies.start(x_far, x_ref)
        wait_all(arriving)
        leaving = [copies.start(w_ref, w_out)]
        for index, (ref, out) in enumerate(((q_ref, q_out), (k_ref, k_out), (v_ref, v_out))):
            ref[...] = mm(a_ref[...], w_ref[index]).astype(BF16)
            leaving.append(copies.start(ref, out))
        attend(
            q_ref, k_ref, v_ref, key_seg_ref, query_seg_ref, prob_ref, mix_ref,
            lambda pair: pair_copy(prob_ref, prob_out, pair_sems, pair).start(),
        )
        leaving.append(copies.start(mix_ref, mix_out))
        x_copy.wait()
        mid = x_ref[...].astype(F32) + mm(mix_ref[...], w_ref[3])
        mid_ref[...] = mid
        leaving.append(copies.start(mid_ref, mid_out))
        normed, _ = normalized(mid)
        c_ref[...] = (normed * gains_ref[2:3, :] + gains_ref[3:4, :]).astype(BF16)
        wait_all(leaving)
        for pair in range(HEADS // 2):
            pair_copy(prob_ref, prob_out, pair_sems, pair).wait()

    low, rows = low_shape(tokens, D), pltpu.VMEM((tokens, D), BF16)
    probs = (HEADS, tokens, tokens)
    return whole_kernel(
        body,
        (
            low_shape(GROUP, D, D),
            low,
            low,
            low,
            low_shape(*probs),
            low,
            wide_shape(tokens, D),
            low,
        ),
        scratch=[rows, pltpu.VMEM((GROUP, D, D), BF16), rows, rows, rows]
        + [pltpu.VMEM(probs, BF16), rows, pltpu.VMEM((tokens, D), F32)]
        + [pltpu.SemaphoreType.DMA((pieces + 8,)), pltpu.SemaphoreType.DMA((HEADS // 2,))],
        flops=14 * UNIT,
        moved=12 << 20,
        name="self_forward",
        far_outs=7,
    )


def cross_forward(layout, tokens, states):
    count, pieces = (2, weight_pieces(layout)[1]) if layout.quad else (1, 1)

    def body(info_ref, c_ref, gains_ref, query_seg_ref, key_seg_ref, enc_far, mid_far, *refs):
        w_ref, q_ref, k_ref, v_ref, prob_ref, mix_ref, late_ref, f_ref = refs[count : count + 8]
        enc_ref, mid_ref, sems = refs[count + 8 :]
        copies = Copies(sems)
        arriving = fetch_cross(info_ref, layout, refs[:count], w_ref, copies)
        arriving[1].append(copies.start(enc_far, enc_ref))
        mid_copy = copies.start(mid_far, mid_ref)
        for index, (source, ref) in enumerate(
            ((c_ref, q_ref), (enc_ref, k_ref), (enc_ref, v_ref))
        ):
            wait_all(arriving[index])
            ref[...] = mm(source[...], w_ref[index]).astype(BF16)
        attend(
            q_ref, k_ref, v_ref, key_seg_ref, query_seg_ref, prob_ref, mix_ref, lambda pair: None
        )
        mid_copy.wait()
        wait_all(arriving[3])
        late = mid_ref[...] + mm(mix_ref[...], w_ref[3])
        late_ref[...] = late
        normed, _ = normalized(late)
        f_ref[...] = (normed * gains_ref[4:5, :] + gains_ref[5:6, :]).astype(BF16)

    low = low_shape(tokens, D)
    return whole_kernel(
        body,
        (
            low_shape(GROUP, D, D),
            low,
            low_shape(states, D),
            low_shape(states, D),
            low_shape(HEADS, states, tokens),
            low,
            wide_shape(tokens, D),
            low,
        ),
        scratch=[pltpu.VMEM((states, D), BF16), pltpu.VMEM((tokens, D), F32)]
        + [pltpu.SemaphoreType.DMA((pieces + 2,))],
        flops=14 * UNIT,
        moved=12 << 20,
        name="cross_forward",
    )


def gelu_parts(pre):
    slope = math.sqrt(2.0 / math.pi)
    square = pre * pre
    bent = jnp.tanh(slope * pre * (1.0 + 0.044715 * square))
    half = 0.5 * (1.0 + bent)
    inner = slope * (1.0 + 3 * 0.044715 * square)
    return pre * half, half + 0.5 * pre * (1.0 - bent * bent) * inner


def feed_forward(layout, tokens, hidden):
    count, planes = layout.tensor, layout.planes
    piece_rows, full = D // planes, layout.tensor * hidden

    def body(info_ref, f_ref, cot_far, *refs):
        mine, others = refs[:count], refs[count : 2 * count]
        w_in, w_out, post_ref, d_pre_ref, keep_ref, send_ref = refs[2 * count : -5]
        cot_ref, f_t, cot_t, sems, cot_sem = refs[-5:]
        first_core = info_ref[0] == 0

        def columns(position):
            return slice(position * hidden, (position + 1) * hidden)

        def fetch(source, target, matrix, position):
            return pltpu.make_async_copy(
                source, target.at[:, columns(position)], sems.at[matrix, position]
            )

        cot_copy = pltpu.make_async_copy(cot_far, cot_ref, cot_sem)
        cot_copy.start()
        for position in range(count):
            turned = reorder(1, position, layout.bits)

            @pl.when(first_core)
            def _():
                fetch(mine[position], w_in, 0, position).start()
                fetch(others[turned], w_out, 1, position).start()

            @pl.when(jnp.logical_not(first_core))
            def _():
                fetch(others[position], w_in, 0, position).start()
                fetch(mine[turned], w_out, 1, position).start()

        f_t[...] = f_ref[...].T
        cot_copy.wait()
        cot_t[...] = cot_ref[...].T
        for position in range(count):
            cols = columns(position)
            fetch(mine[0], w_in, 0, position).wait()
            fetch(mine[0], w_out, 1, position).wait()
            pre = mm(f_ref[...], w_in[:, cols])
            grad_post = mm(cot_ref[...], w_out[:, cols])
            post, slope = gelu_parts(pre)
            post_ref[:, cols] = post.astype(BF16)
            d_pre_ref[:, cols] = (slope * grad_post).astype(BF16)
        for position in range(count):
            cols = columns(position)
            turned = reorder(1, position, layout.bits)
            keep_at = jnp.where(first_core, position, turned)
            send_at = jnp.where(first_core, turned, position)
            grad_in = mm(f_t[...], d_pre_ref[:, cols]).astype(BF16)
            grad_out = mm(cot_t[...], post_ref[:, cols]).astype(BF16)
            for slot in range(planes):
                part = slice(slot * piece_rows, (slot + 1) * piece_rows)
                keep_ref[keep_at, slot] = jnp.where(first_core, grad_in[part], grad_out[part])
                send_ref[send_at, slot] = jnp.where(first_core, grad_out[part], grad_in[part])

    pieces = low_shape(count, planes, piece_rows, hidden)
    return whole_kernel(
        body,
        (low_shape(D, full), low_shape(D, full), low_shape(tokens, full), low_shape(tokens, full))
        + (pieces, pieces),
        scratch=[
            pltpu.VMEM((tokens, D), BF16),
            pltpu.VMEM((D, tokens), BF16),
            pltpu.VMEM((D, tokens), BF16),
            pltpu.SemaphoreType.DMA((2, count)),
            pltpu.SemaphoreType.DMA,
        ],
        flops=4 * UNIT * full // D,
        moved=14 << 20,
        name="feed_forward",
    )


def feed_forward_sums(layout, tokens, hidden):
    def body(info_ref, w_in, w_out, post_ref, d_pre_ref, late_ref, gains_ref, cot_far, *refs):
        out_ref, glate_ref, dlate_ref, norm_ref, cot_ref, sem = refs
        cot_copy = pltpu.make_async_copy(cot_far, cot_ref, sem)
        cot_copy.start()
        late = late_ref[...]
        back = mm_nt(d_pre_ref[...], w_in[...])
        back, gain_grad, shift_grad = norm_backward(back, late, gains_ref[4:5, :])
        cot_copy.wait()
        grad_late = cot_ref[...].astype(F32) + back
        glate_ref[...] = grad_late
        dlate_ref[...] = grad_late.astype(BF16)
        norm_ref[0:1, :] = gain_grad
        norm_ref[1:2, :] = shift_grad
        out_ref[...] = (late + mm_nt(post_ref[...], w_out[...])).astype(BF16)

    low = low_shape(tokens, D)
    return whole_kernel(
        body,
        (low, wide_shape(tokens, D), low, wide_shape(2, D)),
        scratch=[pltpu.VMEM((tokens, D), BF16), pltpu.SemaphoreType.DMA],
        flops=2 * UNIT * layout.tensor * hidden // D,
        moved=4 << 20,
        name="feed_forward_sums",
    )


def cross_backward(layout, tokens, states):
    def body(info_ref, dlate_ref, mix_ref, glate_ref, gains_ref, *refs):
        q_ref, k_ref, v_ref, prob_ref, c_ref, w_ref, enc_far, mid_far = refs[:8]
        enc_grad_ref, gmid_ref, dmid_ref, norm_ref, keep_ref, send_ref = refs[8:14]
        enc_ref, mid_ref, dq, dk, dv, grads, d_mix, sems = refs[14:]
        copies = Copies(sems)
        later = [copies.start(enc_far, enc_ref), copies.start(mid_far, mid_ref)]
        d_mix[...] = mm_nt(dlate_ref[...], w_ref[3]).astype(BF16)
        grads[3] = mm_tn(mix_ref[...], dlate_ref[...]).astype(BF16)
        attend_back(
            q_ref, k_ref, v_ref, prob_ref, d_mix, dq, dk, dv, lambda pair: None
        )
        wait_all(later)
        grads[0] = mm_tn(c_ref[...], dq[...]).astype(BF16)
        enc_t = enc_ref[...].T
        grads[1] = mm(enc_t, dk[...]).astype(BF16)
        grads[2] = mm(enc_t, dv[...]).astype(BF16)
        place_grads(info_ref, layout, grads, keep_ref, send_ref)
        enc_grad_ref[...] = (mm_nt(dk[...], w_ref[1]) + mm_nt(dv[...], w_ref[2])).astype(BF16)
        back, gain_grad, shift_grad = norm_backward(
            mm_nt(dq[...], w_ref[0]), mid_ref[...], gains_ref[2:3, :]
        )
        grad_mid = glate_ref[...] + back
        gmid_ref[...] = grad_mid
        dmid_ref[...] = grad_mid.astype(BF16)
        norm_ref[0:1, :] = gain_grad
        norm_ref[1:2, :] = shift_grad

    low, rows = low_shape(tokens, D), pltpu.VMEM((tokens, D), BF16)
    keys = pltpu.VMEM((states, D), BF16)
    pieces = low_shape(layout.tensor, layout.planes, layout.rows, layout.width)
    return whole_kernel(
        body,
        (low_shape(states, D), wide_shape(tokens, D), low, wide_shape(2, D), pieces, pieces),
        scratch=[keys, pltpu.VMEM((tokens, D), F32), rows, keys, keys]
        + [pltpu.VMEM((GROUP, D, D), BF16), rows, pltpu.SemaphoreType.DMA((2,))],
        flops=26 * UNIT,
        moved=14 << 20,
        name="cross_backward",
    )


def self_attention_back(layout, tokens):
    def body(info_ref, dmid_ref, w_ref, mix_ref, q_ref, k_ref, v_ref, prob_ref, *refs):
        out_ref, dq, dk, dv, d_mix = refs
        d_mix[...] = mm_nt(dmid_ref[...], w_ref[3]).astype(BF16)
        attend_back(
            q_ref, k_ref, v_ref, prob_ref, d_mix, dq, dk, dv, lambda pair: None
        )
        out_ref[...] = mm_tn(mix_ref[...], dmid_ref[...]).astype(BF16)

    low = low_shape(tokens, D)
    return whole_kernel(
        body,
        (low_shape(D, D), low, low, low),
        scratch=[pltpu.VMEM((tokens, D), BF16)],
        flops=18 * UNIT,
        moved=10 << 20,
        name="self_attention_back",
    )


def self_backward(layout, tokens):
    def body(info_ref, out_grad_ref, dq, dk, dv, gmid_ref, gains_ref, *refs):
        norm_two_ref, norm_three_ref, w_ref, a_ref, x_ref = refs[:5]
        grad_ref, keep_ref, send_ref, grads, norms, tile = refs[5:]
        grads[3] = out_grad_ref[...]
        a_t = a_ref[...].T
        for index, ref in enumerate((dq, dk, dv)):
            grads[index] = mm(a_t, ref[...]).astype(BF16)
        total = None
        for index, ref in enumerate((dq, dk, dv)):
            part = mm_nt(ref[...], w_ref[index])
            total = part if total is None else total + part
        place_grads(info_ref, layout, grads, keep_ref, send_ref)
        back, gain_grad, shift_grad = norm_backward(
            total, x_ref[...].astype(F32), gains_ref[0:1, :]
        )
        grad_ref[...] = (gmid_ref[...] + back).astype(BF16)
        tile[...] = jnp.zeros_like(tile)
        for index, row in enumerate((gain_grad, shift_grad)):
            norms[index : index + 1, :] = row
        norms[2:4, :] = norm_two_ref[...]
        norms[4:6, :] = norm_three_ref[...]
        for block in range(layout.dp):
            columns = slice(block * layout.rows, (block + 1) * layout.rows)
            tile[block, 0:6, 0 : layout.rows] = norms[0:6, columns].astype(BF16)
        for other, ref in ((False, keep_ref), (True, send_ref)):
            core = 1 - info_ref[0] if other else info_ref[0]
            for slot in range(layout.planes):
                block = tile[slot * 2 + core]
                for position in range(layout.tensor):
                    ref[position, slot, layout.rows :, :] = block

    low = low_shape(tokens, D)
    pieces = low_shape(layout.tensor, layout.planes, layout.rows + NORM_ROWS, layout.width)
    return whole_kernel(
        body,
        (low, pieces, pieces),
        scratch=[
            pltpu.VMEM((GROUP, D, D), BF16),
            pltpu.VMEM((8, D), F32),
            pltpu.VMEM((layout.dp, NORM_ROWS, layout.width), BF16),
        ],
        flops=7 * UNIT,
        moved=6 << 20,
        name="self_backward",
    )


def gram_rest(low_ref, rest_ref, ratio, shift):
    half = D // 2
    diagonal = lax.broadcasted_iota(jnp.int32, (half, half), 0) == lax.broadcasted_iota(
        jnp.int32, (half, half), 1
    )
    shifted = jnp.where(diagonal, shift, 0.0)
    top, bottom = slice(0, half), slice(half, D)
    upper, lower = low_ref[top, :], low_ref[bottom, :]
    rest_ref[top, top] = (ratio * mm_nt(upper, upper) - shifted).astype(BF16)
    corner = (ratio * mm_nt(upper, lower)).astype(BF16)
    rest_ref[top, bottom] = corner
    rest_ref[bottom, top] = corner.T
    rest_ref[bottom, bottom] = (ratio * mm_nt(lower, lower) - shifted).astype(BF16)


def apply_factor(low_ref, poly_ref, scale, kept):
    for start in range(0, kept, D):
        cols = slice(start, min(start + D, kept))
        part = low_ref[:, cols]
        low_ref[:, cols] = (scale * part.astype(F32) + mm(poly_ref[...], part)).astype(BF16)


def sweep(low_ref, rest_ref, poly_ref, width, kept, first=False):
    shift = jnp.zeros((), F32)
    for start in range(0, width, D):
        part = low_ref[:, start : start + D].astype(F32)
        shift = shift + jnp.sum(part * part)
    inverse = 1.0 / (jnp.sqrt(shift) + 1e-07) if first else 1.0
    shift = shift * (inverse * inverse * (1.0 / D))
    gram_rest(low_ref, rest_ref, inverse * inverse, shift)
    slope = POLY_SECOND + 2.0 * POLY_THIRD * shift
    scale = POLY_FIRST + POLY_SECOND * shift + POLY_THIRD * shift * shift
    half = D // 2
    for rows in (slice(0, half), slice(half, D)):
        square = mm(rest_ref[rows, :], rest_ref[...])
        poly = slope * rest_ref[rows, :].astype(F32) + POLY_THIRD * square
        poly_ref[rows, :] = (inverse * poly).astype(BF16)
    apply_factor(low_ref, poly_ref, inverse * scale, kept)


def orthogonalize_attention(layout):
    parts, rows = layout.parts, layout.rows

    def body(info_ref, *refs):
        pieces = refs[:parts]
        mine_ref, other_ref, low, rest, poly = refs[parts:]
        for part, ref in enumerate(pieces):
            low[:, part * layout.width : (part + 1) * layout.width] = ref[...]
        sweep(low, rest, poly, D, D, first=True)

        def one(step, carry):
            sweep(low, rest, poly, D, D)
            return carry

        lax.fori_loop(1, NS_STEPS, one, 0)
        for ref, core in ((mine_ref, info_ref[0]), (other_ref, 1 - info_ref[0])):
            start = pl.multiple_of((2 * info_ref[1] + core) * rows, rows)
            ref[...] = low[pl.ds(start, rows), 0 : layout.width]

    return whole_kernel(
        body,
        (low_shape(rows, layout.width), low_shape(rows, layout.width)),
        scratch=[pltpu.VMEM((D, D), BF16)] * 3,
        flops=15 * UNIT,
        moved=2 << 20,
        name="orthogonalize_attention",
    )


def gram_sweeps(rest_ref, poly_ref, square_ref, sum_ref, shift):
    diagonal = lax.broadcasted_iota(jnp.int32, (D, D), 0) == lax.broadcasted_iota(
        jnp.int32, (D, D), 1
    )
    scale = None
    for step in range(GRAM_STEPS):
        rest = rest_ref[...]
        slope = POLY_SECOND + 2.0 * POLY_THIRD * shift
        here = POLY_FIRST + POLY_SECOND * shift + POLY_THIRD * shift * shift
        poly = slope * rest.astype(F32) + POLY_THIRD * mm(rest, rest)
        poly_ref[...] = poly.astype(BF16)
        low = poly_ref[...]
        if scale is None:
            scale = here
            sum_ref[...] = poly
        else:
            before = sum_ref[...]
            sum_ref[...] = here * before + scale * poly + mm(low, before.astype(BF16))
            scale = scale * here
        if step + 1 < GRAM_STEPS:
            square = 2.0 * here * poly + mm(low, low)
            square_ref[...] = square.astype(BF16)
            twice = here * here
            rest = twice * rest.astype(F32) + shift * square + mm(square_ref[...], rest)
            more = jnp.sum(jnp.where(diagonal, rest, 0.0)) * (1.0 / D)
            rest_ref[...] = jnp.where(diagonal, rest - more, rest).astype(BF16)
            shift = twice * shift + more
    return scale


def orthogonalize_wide(layout, hidden):
    count = layout.tensor
    width = count * hidden

    def body(info_ref, *refs):
        pieces = refs[:count]
        out_ref, low, rest, poly, square, total_ref, sem = refs[count:]
        total = jnp.zeros((), F32)
        copies = [
            pltpu.make_async_copy(
                pieces[count - 2 + index],
                low.at[:, index * hidden : (index + 1) * hidden],
                sem.at[index],
            )
            for index in range(2)
        ]
        for copy in copies:
            copy.start()
        for index in reversed(range(count)):
            cols = slice(index * hidden, (index + 1) * hidden)
            if index < 2:
                copies[index].wait()
                part = low[:, cols]
            else:
                part = pieces[index - 2][...]
                low[:, cols] = part
            values = part.astype(F32)
            total = total + jnp.sum(values * values)
        inverse = 1.0 / (jnp.sqrt(total) + 1e-07)
        ratio = inverse * inverse
        shift = total * ratio * (1.0 / D)
        gram_rest(low, rest, ratio, shift)
        scale = gram_sweeps(rest, poly, square, total_ref, shift)
        poly[...] = (inverse * total_ref[...]).astype(BF16)
        apply_factor(low, poly, inverse * scale, width)
        for step in range(GRAM_STEPS, NS_STEPS):
            sweep(low, rest, poly, width, width if step + 1 < NS_STEPS else hidden)
        out_ref[...] = low[:, 0:hidden]

    return whole_kernel(
        body,
        low_shape(D, hidden),
        scratch=[pltpu.VMEM((D, width), BF16)]
        + [pltpu.VMEM((D, D), BF16)] * 3
        + [pltpu.VMEM((D, D), F32), pltpu.SemaphoreType.DMA((2,))],
        flops=30 * UNIT,
        moved=3 << 20,
        name="orthogonalize_wide",
    )


def wide_shard(hidden):
    def body(info_ref, expand_far, contract_far, out_ref, block, sem):
        @pl.when(info_ref[0] == 0)
        def _():
            copy = pltpu.make_async_copy(expand_far, block.at[:, 0:hidden], sem)
            copy.start()
            copy.wait()
            out_ref[...] = block[:, 0:hidden].astype(BF16)

        @pl.when(info_ref[0] != 0)
        def _():
            copy = pltpu.make_async_copy(contract_far, block.at[0:hidden, :], sem)
            copy.start()
            copy.wait()
            out_ref[...] = block[0:hidden, :].T.astype(BF16)

    return whole_kernel(
        body,
        low_shape(D, hidden),
        scratch=[pltpu.VMEM((D, D), F32), pltpu.SemaphoreType.DMA],
        moved=3 << 20,
        name="wide_shard",
    )


def fence(values, after, space=pl.ANY):
    def body(source_ref, *refs):
        pass

    return pl.pallas_call(
        body,
        out_shape=jax.ShapeDtypeStruct(values.shape, values.dtype),
        in_specs=[pl.BlockSpec(memory_space=pl.ANY)] * (1 + len(after)),
        out_specs=pl.BlockSpec(memory_space=pl.ANY),
        input_output_aliases={0: 0},
        name="fence",
    )(values, *after)


def halves_sum(layout, kept, got, name, after=()):
    half = kept.shape[0] // 2

    def body(info_ref, kept_ref, got_ref, upper_ref, lower_ref):
        for position in range(half):
            for ref, at in ((upper_ref, half + position), (lower_ref, position)):
                ref[position] = (kept_ref[at].astype(F32) + got_ref[at].astype(F32)).astype(BF16)

    part = low_shape(half, *kept.shape[1:])
    return whole_kernel(body, (part, part), moved=4 * kept.size, name=name)(
        kept, got, after=after
    )


def nest_of(grad, momentum):
    return (1.0 + MOMENTUM_DECAY) * grad + MOMENTUM_DECAY * MOMENTUM_DECAY * momentum


def wide_nest(layout, hidden):
    count = layout.planes

    def body(info_ref, got_ref, momentum_ref, out_ref):
        total = sum(got_ref[plane].astype(F32) for plane in range(count))
        nest = nest_of(total, momentum_ref[...]).astype(BF16)
        for plane in range(count):
            out_ref[plane] = nest

    return whole_kernel(
        body, low_shape(count, D // count, hidden), moved=1 << 20, name="wide_nest"
    )


def wide_slots_sum(layout, hidden):
    def body(info_ref, kept_ref, got_ref, out_ref):
        out_ref[...] = (kept_ref[0].astype(F32) + got_ref[0].astype(F32)).astype(BF16)

    shape = low_shape(layout.planes, D // layout.planes, hidden)
    return whole_kernel(body, shape, moved=1 << 20, name="wide_slots_sum")


def attention_slots(layout):
    rows, planes, width = layout.rows, layout.planes, layout.width

    def body(info_ref, cross_ref, cross_got, self_ref, self_got, out_ref):
        for slot in range(planes):
            for start, kept, got in ((0, cross_ref, cross_got), (rows, self_ref, self_got)):
                total = kept[0, slot].astype(F32) + got[0, slot].astype(F32)
                out_ref[slot, start : start + total.shape[0], :] = total.astype(BF16)

    return whole_kernel(
        body,
        low_shape(planes, 2 * rows + NORM_ROWS, width),
        moved=2 << 20,
        name="attention_slots",
    )


def attention_nest(layout):
    rows, planes, width = layout.rows, layout.planes, layout.width

    def body(info_ref, got_ref, momentum_far, unread, *refs):
        mine_ref, other_ref, grad_ref, norm_ref, momentum, sems = refs
        first_core, tensor, copies = info_ref[0] == 0, info_ref[2], Copies(sems)
        cols = slice(None)
        if layout.parts > 1:
            part = lax.rem(tensor, layout.parts) * width
            cols = pl.ds(pl.multiple_of(part, width), width)
        moving = [
            copies.start(
                momentum_far.at[group * GROUP + lax.div(tensor, layout.parts), :, cols],
                momentum.at[index],
            )
            for index, group in enumerate((1, 0))
        ]
        total = sum(got_ref[plane].astype(F32) for plane in range(planes))
        wait_all(moving)
        cross = nest_of(total[0:rows], momentum[0]).astype(BF16)
        own = nest_of(total[rows : 2 * rows], momentum[1]).astype(BF16)
        mine_ref[...] = jnp.where(first_core, own, cross)
        other_ref[...] = jnp.where(first_core, cross, own)
        grad_ref[...] = total[0 : 2 * rows].astype(BF16)
        norm_ref[...] = total[2 * rows : 2 * rows + 8]

    one = low_shape(rows, width)
    return whole_kernel(
        body,
        (one, one, low_shape(2 * rows, width), wide_shape(8, width)),
        scratch=[pltpu.VMEM((2, rows, width), F32), pltpu.SemaphoreType.DMA((2,))],
        moved=2 << 20,
        name="attention_nest",
    )


def attention_pair(layout):
    rows, planes = layout.rows, layout.planes

    def body(info_ref, mine_ref, got_ref, out_ref):
        first_core = info_ref[0] == 0
        mine, got = mine_ref[...], got_ref[...]
        for plane in range(planes):
            out_ref[plane, 0:rows, :] = jnp.where(first_core, mine, got)
            out_ref[plane, rows : 2 * rows, :] = jnp.where(first_core, got, mine)

    return whole_kernel(
        body, low_shape(planes, 2 * rows, layout.width), moved=1 << 20, name="attention_pair"
    )


def wide_momentum(layout, hidden):
    piece_rows = D // layout.planes

    def body(info_ref, expand_ref, contract_ref, out_ref, turned):
        rows = pl.ds(pl.multiple_of(info_ref[1] * piece_rows, piece_rows), piece_rows)
        turned[...] = contract_ref[...].T
        out_ref[...] = jnp.where(info_ref[0] == 0, expand_ref[rows, :], turned[rows, :])

    return whole_kernel(
        body,
        wide_shape(piece_rows, hidden),
        scratch=[pltpu.VMEM((D, hidden), F32)],
        moved=3 << 20,
        name="wide_momentum",
    )


def decayed(master, share, scale):
    return master - MUON_RATE * (MUON_DECAY * master + scale * share)


def finish_wide(layout, hidden, full_hidden):
    scale = 0.2 * math.sqrt(max(D, full_hidden))

    def body(info_ref, mine_ref, other_ref, expand_ref, contract_ref, *refs):
        e_new, e_low, c_new, c_low = refs
        first = info_ref[0] == 0
        mine, other = mine_ref[...], other_ref[...]
        new = decayed(expand_ref[...], jnp.where(first, mine, other).astype(F32), scale)
        e_new[...] = new
        e_low[...] = new.astype(BF16)
        new = decayed(contract_ref[...], jnp.where(first, other, mine).T.astype(F32), scale)
        c_new[...] = new
        c_low[...] = new.astype(BF16)

    return whole_kernel(
        body,
        (wide_shape(D, hidden), low_shape(D, hidden), wide_shape(hidden, D), low_shape(hidden, D)),
        moved=6 << 20,
        name="finish_wide",
    )


def wide_velocity(layout, hidden):
    grad_share = 1.0 / (1.0 + MOMENTUM_DECAY)
    momentum_share = MOMENTUM_DECAY - MOMENTUM_DECAY * MOMENTUM_DECAY * grad_share

    def body(info_ref, mine_ref, other_ref, expand_ref, contract_ref, e_new, c_new, token):
        token[...] = jnp.zeros_like(token)
        first = info_ref[0] == 0
        mine, other = mine_ref[...], other_ref[...]
        nest = jnp.where(first, mine, other).astype(F32)
        e_new[...] = momentum_share * expand_ref[...] + grad_share * nest
        nest = jnp.where(first, other, mine).T.astype(F32)
        c_new[...] = momentum_share * contract_ref[...] + grad_share * nest

    return whole_kernel(
        body,
        (wide_shape(D, hidden), wide_shape(hidden, D), wide_shape(8, 128)),
        moved=6 << 20,
        name="wide_velocity",
    )


def owner_columns(info_ref, layout, position, other=False):
    owner = owner_at(info_ref, layout, position, other)
    if layout.parts == 1:
        return owner, slice(None)
    part = lax.rem(owner, layout.parts) * layout.width
    return lax.div(owner, layout.parts), pl.ds(pl.multiple_of(part, layout.width), layout.width)


def attention_velocity(layout):
    count, rows = layout.tensor, layout.rows

    def body(info_ref, *refs):
        momentum_ref, velocity_ref = refs[count:]
        for position in range(count):
            matrix, cols = owner_columns(info_ref, layout, position)
            for group in range(2):
                index, start = group * GROUP + matrix, (1 - group) * rows
                grad = refs[position][start : start + rows, :].astype(F32)
                velocity_ref[index, :, cols] = (
                    MOMENTUM_DECAY * momentum_ref[index, :, cols] + grad
                )

    return whole_kernel(
        body, wide_shape(2 * GROUP, rows, D), moved=3 << 20, name="attention_velocity"
    )


def finish_attention(layout):
    count = layout.tensor
    scale = 0.2 * math.sqrt(D)

    def body(info_ref, *refs):
        late = refs[:count]
        master_ref, new_ref, low_ref = refs[count:]
        for position in range(count):
            matrix, cols = owner_columns(info_ref, layout, position)
            for group in range(2):
                index = group * GROUP + matrix
                at = info_ref[0] if group == 0 else 1 - info_ref[0]
                new = decayed(
                    master_ref[index, :, cols], late[position][at].astype(F32), scale
                )
                new_ref[index, :, cols] = new
                low_ref[index, :, cols] = new.astype(BF16)

    shape = (2 * GROUP, layout.rows, D)
    return whole_kernel(
        body, (wide_shape(*shape), low_shape(*shape)), moved=4 << 20, name="finish_attention"
    )


def finish_norms(layout):
    def body(info_ref, grad_ref, params_ref, first_ref, second_ref, new, first_new, second_new):
        grad = grad_ref[0:6, 0 : layout.rows]
        first = BETA_FIRST * first_ref[...] + (1.0 - BETA_FIRST) * grad
        second = BETA_SECOND * second_ref[...] + (1.0 - BETA_SECOND) * grad * grad
        corrected = first / (1.0 - BETA_FIRST**STEP)
        denominator = jnp.sqrt(second / (1.0 - BETA_SECOND**STEP)) + ADAM_EPSILON
        new[...] = params_ref[...] - ADAM_RATE * corrected / denominator
        first_new[...] = first
        second_new[...] = second

    return whole_kernel(body, (wide_shape(6, layout.rows),) * 3, moved=1 << 14, name="norms")


def device_program(layout, arguments):
    (
        inputs,
        encoder,
        dec_segments,
        enc_segments,
        cotangent,
        attn_master,
        attn_momentum,
        expand_master,
        expand_momentum,
        contract_master,
        contract_momentum,
        norm_params,
        first_moments,
        second_moments,
    ) = arguments
    tokens, states = inputs.shape[1], encoder.shape[1]
    hidden = expand_master.shape[1]
    full_hidden = hidden * layout.tensor
    dp_at, tensor_at = lax.axis_index("dp"), lax.axis_index("tensor")
    x, enc, cot = inputs[0], encoder[0], cotangent[0]

    if layout.quad:
        shard = wide_shard(hidden)(far=[expand_master, contract_master])
        chunk = weight_chunk(layout, 0, "self_chunk", 1)(
            norm_params, far=[attn_master], after=[shard]
        )
        near = send(shard, layout.inplane(0))
        cross_own = cross_rows(layout)(far=[attn_master], after=[near])
        first, second, tile = self_split(layout)(*send_planes(layout, chunk), after=[cross_own])
        cross_own = exchange_planes(layout, fence(cross_own, [tile]))
        got_first = send(first, layout.plain_inplane(1))
        got_second = send(second, layout.plain_inplane(2))
        tiles = [tile, swap_cores(layout, tile)]
        a_saved, a, gains = first_norm(tokens)(*tiles, far=[x])
        got_first, got_second = fence(got_first, [a]), fence(got_second, [a])
        self_own = [first, second, got_first, got_second]
        self_pieces = self_own + [swap_cores(layout, piece) for piece in self_own]
        near = fence(near, [got_first])
        far = send(fence(shard, [got_first]), layout.inplane(1))
        farthest = send(near, layout.inplane(1))
        before = []
    else:
        low = attn_master.astype(BF16)
        norm_low = lax.all_gather(norm_params.astype(BF16), "dp", axis=1, tiled=True)
        padded = jnp.concatenate([norm_low, jnp.zeros((NORM_ROWS - 6, D), BF16)])
        self_low = lax.all_gather(low[:GROUP], "dp", axis=1, tiled=True)
        cross_low = lax.all_gather(low[GROUP:], "dp", axis=1, tiled=True)
        self_pieces, before = [self_low], []
        tiles = [padded, jnp.zeros_like(padded)]
        shard = wide_shard(hidden)(far=[expand_master, contract_master])
        wide_own = gather_inplane(layout, shard)
        wide_other = [swap_cores(layout, piece) for piece in wide_own]

    dec_row, dec_column = dec_segments.reshape(1, tokens), dec_segments.reshape(tokens, 1)
    enc_column = enc_segments.reshape(states, 1)
    if not layout.quad:
        a_saved, a, gains = first_norm(tokens)(*tiles, far=[x])
    w_self, q, k, v, self_prob, self_mix, mid, c = self_forward(layout, tokens)(
        a, gains, dec_row, dec_column, far=[x, *self_pieces], after=before
    )
    if layout.quad:
        far, farthest = fence(far, [c]), fence(farthest, [c])
        cross_own = fence(cross_own, [far, farthest])
        cross_pieces = [cross_own, swap_cores(layout, cross_own)]
        wide_own = [shard, near, far, farthest]
        wide_other = [swap_cores(layout, piece) for piece in wide_own]
    else:
        cross_pieces = [cross_low]
    w_cross, qc, kc, vc, cross_prob, cross_mix, late, f = cross_forward(layout, tokens, states)(
        c, gains, dec_row, enc_column, far=[enc, mid, *cross_pieces], after=[wide_own[-1]]
    )
    w_in, w_out, post, d_pre, wide_keep, wide_send = feed_forward(layout, tokens, hidden)(
        f, far=[cot, *wide_own, *wide_other]
    )
    output, grad_late, late_low, norm_three = feed_forward_sums(layout, tokens, hidden)(
        w_in, w_out, post, d_pre, late, gains, far=[cot]
    )
    top = layout.bits - 1
    upper, lower = halves_sum(
        layout, wide_keep, swap_cores(layout, wide_send), "wide_sum", after=[late_low]
    )
    encoder_grad, grad_mid, mid_low, norm_two, cross_keep, cross_send = cross_backward(
        layout, tokens, states
    )(
        late_low, cross_mix, grad_late, gains, qc, kc, vc, cross_prob, c, w_cross,
        far=[enc, mid], after=[upper],
    )
    got = send(upper, layout.inplane(top))
    for bit in reversed(range(top)):
        upper, lower = halves_sum(layout, lower, got, "wide_sum", after=[mid_low])
        got = send(upper, layout.inplane(bit))
    self_out_grad, dq, dk, dv = self_attention_back(layout, tokens)(
        mid_low, w_self, self_mix, q, k, v, self_prob, after=[upper]
    )
    input_grad, self_keep, self_send = self_backward(layout, tokens)(
        self_out_grad, dq, dk, dv, grad_mid, gains, norm_two, norm_three,
        w_self, a_saved, x,
        after=[got],
    )
    wide_slots = wide_slots_sum(layout, hidden)(lower, got, after=[self_keep])
    wide_got = exchange_planes(layout, wide_slots)
    self_upper, self_lower = halves_sum(
        layout, self_keep, swap_cores(layout, self_send), "self_sum"
    )
    cross_upper, cross_lower = halves_sum(
        layout, cross_keep, swap_cores(layout, cross_send), "cross_sum", after=[wide_slots]
    )
    got_cross = send(cross_upper, layout.inplane(top))
    momentum = wide_momentum(layout, hidden)(expand_momentum, contract_momentum)
    got_self = send(self_upper, layout.inplane(top))
    for bit in reversed(range(top)):
        cross_upper, cross_lower = halves_sum(layout, cross_lower, got_cross, "cross_sum")
        got_cross = send(cross_upper, layout.inplane(bit))
    nest_rows = wide_nest(layout, hidden)(wide_got, momentum, after=[self_upper, cross_upper])
    nest = exchange_planes(layout, nest_rows).reshape(D, hidden)
    for bit in reversed(range(top)):
        self_upper, self_lower = halves_sum(layout, self_lower, got_self, "self_sum")
        got_self = send(self_upper, layout.inplane(bit))
    rows_by_slot = attention_slots(layout)(cross_lower, got_cross, self_lower, got_self)
    nest = fence(nest, [rows_by_slot])
    nest_other = swap_cores(layout, nest)
    expand_velocity, contract_velocity, velocity_done = wide_velocity(layout, hidden)(
        nest, nest_other, expand_momentum, contract_momentum
    )
    nest_pieces = gather_inplane(
        layout, nest, lambda piece: fence(piece, [rows_by_slot, velocity_done])
    )
    nest_mine, nest_others, attn_grad, norm_rows = attention_nest(layout)(
        exchange_planes(layout, rows_by_slot), far=[attn_momentum, nest_pieces[layout.tensor // 2 - 1]]
    )

    attn_nest = attention_pair(layout)(nest_mine, swap_cores(layout, nest_others))
    early = gather_inplane_direct(layout, attn_grad)

    def whole_pieces(piece):
        gathered = [piece]
        for bit in range(layout.parts.bit_length() - 1):
            pairs = layout.pairs(lambda d, t: d * layout.tensor + (t ^ (1 << bit)))
            gathered = gathered + [send(one, pairs) for one in gathered]
        return gathered

    wide_ortho = orthogonalize_wide(layout, hidden)(
        *nest_pieces[2:], far=nest_pieces[:2], after=[attn_nest])
    whole = exchange_planes(layout, attn_nest).reshape(D, layout.width)
    mine, others = orthogonalize_attention(layout)(
        *whole_pieces(whole), after=[wide_ortho, *early[1:]]
    )
    late_pieces = gather_inplane_direct(layout, jnp.stack([mine, swap_cores(layout, others)]))
    attn_velocity = attention_velocity(layout)(*early, attn_momentum)
    norm_updated, first_updated, second_updated = finish_norms(layout)(
        norm_rows, norm_params, first_moments, second_moments
    )

    expand_updated, expand_copy, contract_updated, contract_copy = finish_wide(
        layout, hidden, full_hidden
    )(wide_ortho, swap_cores(layout, wide_ortho), expand_master, contract_master)
    attn_updated, attn_copy = finish_attention(layout)(
        *late_pieces, attn_master
    )
    return (
        output[None],
        input_grad[None],
        encoder_grad[None],
        attn_updated,
        attn_velocity,
        attn_copy,
        expand_updated,
        expand_velocity,
        expand_copy,
        contract_updated,
        contract_velocity,
        contract_copy,
        norm_updated,
        first_updated,
        second_updated,
    )


def solution(mesh):
    layout = Layout(mesh.shape["dp"], mesh.shape["tensor"])

    def local(*arguments):
        return device_program(layout, arguments)

    rows = P(AXES, None, None)
    by_dp, by_column, by_row, norm = P(None, "dp", None), P(None, "tensor"), P("tensor", None), P(None, "dp")
    return jax.shard_map(
        local,
        mesh=mesh,
        in_specs=(rows, rows, P(AXES, None), P(AXES, None), rows)
        + (by_dp, by_dp, by_column, by_column, by_row, by_row, norm, norm, norm),
        out_specs=(rows, rows, rows, by_dp, by_dp, by_dp)
        + (by_column, by_column, by_column, by_row, by_row, by_row, norm, norm, norm),
        check_vma=False,
    )
```
